32 devices in a mesh: wide: 8 (over y, x, core), narrow: 4 (over z).
Axes of the slice: x: 2, y: 2, z: 4, core: 2. Of those that a mesh axis runs over, the one named last changes fastest.
Arguments:
- inputs: bfloat16 [2, 32, 512, 768], P(None, ('wide', 'narrow')), may hold values from -6 to 6
- encoder_out: bfloat16 [2, 32, 512, 768], P(None, ('wide', 'narrow')), may hold values from -6 to 6
- segments: int32 [2, 32, 512], P(None, ('wide', 'narrow')), may hold values from 0 to 3, as said below
- enc_segments: int32 [2, 32, 512], P(None, ('wide', 'narrow')), may hold values from 0 to 3, as said below
- buckets: int32 [512], replicated, may hold values from 0 to 31, as said below
- gains: bfloat16 [3, 768], P(None, ('wide', 'narrow')), may hold values from 0.5 to 1.5
- rel_bias: float32 [32, 12], replicated, may hold values from -4 to 4
- self_q: bfloat16 [768, 768], P(('wide', 'narrow')), may hold values from -0.0546875 to 0.0546875
- self_kv: bfloat16 [2, 768, 768], P(None, ('wide', 'narrow')), may hold values from -0.21875 to 0.21875
- self_out: bfloat16 [768, 768], P(None, ('wide', 'narrow')), may hold values from -1.25 to 1.25
- cross_q: bfloat16 [768, 768], P(('wide', 'narrow')), may hold values from -0.0546875 to 0.0546875
- cross_kv: bfloat16 [2, 768, 768], P(None, ('wide', 'narrow')), may hold values from -0.21875 to 0.21875
- cross_out: bfloat16 [768, 768], P(None, ('wide', 'narrow')), may hold values from -1.25 to 1.25
- ffn_in: bfloat16 [768, 3072], P(('wide', 'narrow')), may hold values from -0.21875 to 0.21875
- ffn_out: bfloat16 [3072, 768], P(None, ('wide', 'narrow')), may hold values from -0.15625 to 0.15625
- out_grad: bfloat16 [2, 32, 512, 768], P(None, ('wide', 'narrow')), may hold values from -6 to 6
Outputs:
- layer_out: bfloat16 [2, 32, 512, 768], P(None, ('wide', 'narrow'))
- input_grad: float32 [2, 32, 512, 768], P(None, ('wide', 'narrow'))
- encoder_grad: float32 [2, 32, 512, 768], P(None, ('wide', 'narrow'))
- gains_grad: float32 [3, 768], P(None, ('wide', 'narrow'))
- rel_bias_grad: float32 [32, 12], replicated
- self_q_grad: float32 [768, 768], P(('wide', 'narrow'))
- self_kv_grad: float32 [2, 768, 768], P(None, ('wide', 'narrow'))
- self_out_grad: float32 [768, 768], P(None, ('wide', 'narrow'))
- cross_q_grad: float32 [768, 768], P(('wide', 'narrow'))
- cross_kv_grad: float32 [2, 768, 768], P(None, ('wide', 'narrow'))
- cross_out_grad: float32 [768, 768], P(None, ('wide', 'narrow'))
- ffn_in_grad: float32 [768, 3072], P(('wide', 'narrow'))
- ffn_out_grad: float32 [3072, 768], P(None, ('wide', 'narrow'))
The draws below stay inside these ranges and needn't reach their ends.
Inputs may be any that keep to these rules, and one draw needn't show every extreme that they name: `segments`: along each row the ids never fall; the first position has 0 and the last 3; a document may be empty. `enc_segments`: along each row the ids never fall, and every id 0 to 3 appears in every row. buckets[0] is 0, the buckets never fall as the distance grows, and the last is 31.
All inputs are finite; a program needn't handle non-finite values.
Results may differ from the reference program's by a relative error of at most 0.023.
The reference program's roundings to bfloat16 on the way count: a program that leaves them out, or rounds other values in their place, can miss the bound.
Values may be sent and summed in bfloat16 or wider, within the bound.
No kernel may reach another device: no remote copies, remote signals or barrier semaphores. Data moves between devices by JAX's collectives and lax.ppermute only.
A program may use at most 320 MiB of HBM per device.

```python
import jax
import jax.numpy as jnp
from jax import lax

D = 768
H = 12
DH = 64
FF = 3072
NB = 32
LEN = 512
ENC = 512
NSEG = 4
MICRO = 2
HD = 768
BATCH = 32


def draw_segments(key, part):
    cuts = jax.random.randint(key, (MICRO, BATCH, NSEG - 1), 1, LEN)
    positions = jnp.arange(LEN)
    above = (positions[None, None, :, None] >= cuts[:, :, None, :]).astype(jnp.int32)
    return jnp.sum(above, axis=-1).astype(jnp.int32)


def draw_enc_segments(key, part):
    span = ENC // NSEG
    jitter = jax.random.randint(key, (MICRO, BATCH, NSEG - 1), 0, span)
    cuts = jnp.arange(1, NSEG)[None, None, :] * span + jitter
    positions = jnp.arange(ENC)
    above = (positions[None, None, :, None] >= cuts[:, :, None, :]).astype(jnp.int32)
    return jnp.sum(above, axis=-1).astype(jnp.int32)


def draw_buckets(key, part):
    positions = jnp.arange(LEN)
    increments = jax.random.randint(key, (LEN,), 0, 2)
    increments = jnp.where(positions == 0, 0, increments)
    bucket_rows = jnp.minimum(jnp.cumsum(increments), NB - 1)
    return jnp.where(positions == LEN - 1, NB - 1, bucket_rows).astype(jnp.int32)


def block_levels(own_key, shape, cuts, smallest, largest):
    loudness, own = 1.0, jax.random.fold_in(own_key, 6)
    for axis_at, blocks in cuts:
        draws = jnp.exp(jax.random.uniform(jax.random.fold_in(own, axis_at), (blocks,), jnp.float32, smallest / len(cuts), largest / len(cuts)))
        loudness = loudness * jnp.repeat(draws, shape[axis_at] // blocks).reshape([-1 if axis == axis_at else 1 for axis in range(len(shape))])
    return loudness


def bell_draw(rng, extent, deviation, limit, split=(), kind=jnp.bfloat16):
    factor_of = block_levels(rng, extent, split, -0.22, 0.18) if split else 1.0
    array = jax.random.normal(rng, extent, jnp.float32) * deviation * factor_of
    return jnp.minimum(jnp.maximum(array, -limit), limit).astype(kind)


def setup_inputs(seed: int = 0) -> dict:
    seeds = jax.random.split(jax.random.key(seed), 17)
    return {
        "inputs": bell_draw(seeds[0], (MICRO, BATCH, LEN, D), 1.0, 6.0, ((1, 32),)),
        "encoder_out": bell_draw(seeds[1], (MICRO, BATCH, ENC, D), 1.0, 6.0, ((1, 32),)),
        "segments": draw_segments(jax.random.fold_in(seeds[16], 71), 0),
        "enc_segments": draw_enc_segments(jax.random.fold_in(seeds[16], 71), 0),
        "buckets": draw_buckets(jax.random.fold_in(seeds[16], 71), 0),
        "gains": jnp.clip(1.0 + 0.1 * jax.random.normal(seeds[5], (3, D), jnp.float32), 0.5, 1.5).astype(jnp.bfloat16),
        "rel_bias": bell_draw(seeds[6], (NB, H), 1.0, 4.0, (), jnp.float32),
        "self_q": bell_draw(seeds[7], (D, HD), (16 * D) ** -0.5, 0.0546875, ((0, 32),)),
        "self_kv": bell_draw(seeds[8], (2, D, HD), D ** -0.5, 0.21875, ((1, 32),)),
        "self_out": bell_draw(seeds[9], (HD, D), (D // 32) ** -0.5, 1.25, ((1, 32),)),
        "cross_q": bell_draw(seeds[10], (D, HD), (16 * D) ** -0.5, 0.0546875, ((0, 32),)),
        "cross_kv": bell_draw(seeds[11], (2, D, HD), D ** -0.5, 0.21875, ((1, 32),)),
        "cross_out": bell_draw(seeds[12], (HD, D), (D // 32) ** -0.5, 1.25, ((1, 32),)),
        "ffn_in": bell_draw(seeds[13], (D, FF), D ** -0.5, 0.21875, ((0, 32),)),
        "ffn_out": bell_draw(seeds[14], (FF, D), (FF // 2) ** -0.5, 0.15625, ((1, 32),)),
        "out_grad": bell_draw(seeds[15], (MICRO, BATCH, LEN, D), 1.0, 6.0, ((1, 32),)),
    }


EPSILON = 1e-06
NEGATIVE = -1e+30
HIGHEST = lax.Precision.HIGHEST
ROOT_HALF = 0.7071067811865476

@jax.custom_vjp
def low(v):
    return lax.optimization_barrier(v.astype(jnp.bfloat16)).astype(jnp.float32)

@jax.custom_vjp
def low_back(v):
    return v

def low_keep(v):
    return (low(v), None)

def low_pass(kept, grad):
    return (grad,)

def back_keep(v):
    return (v, None)

def back_low(kept, grad):
    return (low(grad),)
low.defvjp(low_keep, low_pass)
low_back.defvjp(back_keep, back_low)

def matmul(left_rows, right_rows):
    return jnp.dot(left_rows, right_rows, precision=HIGHEST, preferred_element_type=jnp.float32)

def gelu_exact(values):
    return values * 0.5 * (1.0 + lax.erf(values * ROOT_HALF))

def rms_norm(value_rows, gain_row):
    inverse = lax.rsqrt(lax.optimization_barrier(jnp.mean(value_rows * value_rows, axis=-1, keepdims=True)) + EPSILON)
    return value_rows * inverse * gain_row

def expand_bias(bias_params, buckets):
    length = buckets.shape[0]
    per_distance = bias_params[buckets]
    positions = jnp.arange(length)
    distance = jnp.clip(positions[:, None] - positions[None, :], 0, length - 1).astype(jnp.int32)
    return jnp.transpose(per_distance[distance], (2, 0, 1))

def attend(queries, key_rows, value_rows, bias_term, allowed):
    count_q = queries.shape[0]
    heads_q = queries.reshape(count_q, H, DH)
    heads_k = key_rows.reshape(key_rows.shape[0], H, DH)
    heads_v = value_rows.reshape(value_rows.shape[0], H, DH)
    scores = jnp.einsum('qhd,khd->hqk', heads_q, heads_k, precision=HIGHEST) + bias_term
    scores = low_back(scores)
    scores = jnp.where(allowed[None], scores, NEGATIVE)
    shifted = scores - lax.optimization_barrier(jnp.max(scores, axis=-1, keepdims=True))
    exponent = jnp.exp(shifted)
    probs = low(exponent / lax.optimization_barrier(jnp.sum(exponent, axis=-1, keepdims=True)))
    mixture = jnp.einsum('hqk,khd->qhd', probs, heads_v, precision=HIGHEST)
    return low(low_back(mixture.reshape(count_q, H * DH)))

def layer_row(row_items, params, buckets):
    state_in, encoded, seg_row, enc_seg_row = row_items
    gain_rows, bias_params, w_query, w_keyval, w_output, c_query, c_keyval, c_output, w_inner, w_outer = params
    positions = jnp.arange(LEN)
    causal = (positions[:, None] >= positions[None, :]) & (seg_row[:, None] == seg_row[None, :])
    cross_mask = seg_row[:, None] == enc_seg_row[None, :]
    bias_term = expand_bias(bias_params, buckets)
    normed_one = low(rms_norm(state_in, gain_rows[0]))
    queries = low(low_back(matmul(normed_one, w_query)))
    key_rows = low(low_back(matmul(normed_one, w_keyval[0])))
    value_rows = low(low_back(matmul(normed_one, w_keyval[1])))
    attended = attend(queries, key_rows, value_rows, bias_term, causal)
    state_two = state_in + low_back(matmul(attended, w_output))
    normed_two = low(rms_norm(state_two, gain_rows[1]))
    cross_queries = low(low_back(matmul(normed_two, c_query)))
    cross_keys = low(low_back(matmul(encoded, c_keyval[0])))
    cross_values = low(low_back(matmul(encoded, c_keyval[1])))
    cross_mixed = attend(cross_queries, cross_keys, cross_values, 0.0, cross_mask)
    state_three = state_two + low_back(matmul(cross_mixed, c_output))
    normed_three = low(rms_norm(state_three, gain_rows[2]))
    inner_act = low(gelu_exact(low_back(matmul(normed_three, w_inner))))
    return state_three + low_back(matmul(inner_act, w_outer))

def reference(inputs, encoder_out, segments, enc_segments, buckets, gains, rel_bias, self_q, self_kv, self_out, cross_q, cross_kv, cross_out, ffn_in, ffn_out, out_grad):
    rows = MICRO * BATCH
    states = inputs.astype(jnp.float32).reshape(rows, LEN, D)
    encoded = encoder_out.astype(jnp.float32).reshape(rows, ENC, D)
    seg_rows = segments.reshape(rows, LEN).astype(jnp.int32)
    enc_seg_rows = enc_segments.reshape(rows, ENC).astype(jnp.int32)
    params = tuple((weight.astype(jnp.float32) for weight in (gains, rel_bias, self_q, self_kv, self_out, cross_q, cross_kv, cross_out, ffn_in, ffn_out)))

    def forward(states, encoded, params):

        def one_row(row_items):
            return layer_row(row_items, params, buckets)
        return lax.map(jax.checkpoint(one_row), (states, encoded, seg_rows, enc_seg_rows))
    outputs, pullback = jax.vjp(forward, states, encoded, params)
    grad_states, grad_encoded, grad_params = pullback(out_grad.astype(jnp.float32).reshape(rows, LEN, D))
    return (outputs.astype(jnp.bfloat16).reshape(MICRO, BATCH, LEN, D), grad_states.reshape(MICRO, BATCH, LEN, D), grad_encoded.reshape(MICRO, BATCH, ENC, D), grad_params[0], grad_params[1], grad_params[2], grad_params[3], grad_params[4], grad_params[5], grad_params[6], grad_params[7], grad_params[8], grad_params[9])
```

```python
import functools
import jax
import jax.numpy as jnp
from jax import lax
from jax.sharding import PartitionSpec as P
from jax.experimental import pallas as pl
from jax.experimental.pallas import tpu as pltpu

DH = 64
NEGATIVE = -1e30
BF = jnp.bfloat16
F32 = jnp.float32
NN = (((1,), (0,)), ((), ()))
NT = (((1,), (1,)), ((), ()))
TN = (((0,), (0,)), ((), ()))
MB = 1 << 20


def dot(a, b, dims=NN):
    return lax.dot_general(a, b, dims, preferred_element_type=F32)


def segment_columns(query_seg, key_seg):
    ids = jnp.arange(128)
    other = (query_seg[..., None] != ids) & (ids < 4)
    query_cols = jnp.where(other, NEGATIVE, 0.0).astype(BF)
    key_cols = (key_seg[..., None] == ids).astype(BF)
    return query_cols, key_cols


def attn_fwd_kernel(causal, q_ref, k_ref, v_ref, qs_ref, ks_ref, *rest):
    if causal:
        t_ref, o_ref, p_ref, bias = rest
    else:
        o_ref, p_ref = rest
    length = q_ref.shape[0]
    if causal:
        @pl.when(pl.program_id(1) == 0)
        def _():
            for h in range(2):
                for d in range(length // 128):
                    row = jnp.concatenate([t_ref[h, :, pl.ds(128 * (d + 1), 128)], t_ref[h, :, pl.ds(128 * d, 128)]], axis=1)
                    tile = pltpu.roll(jnp.broadcast_to(row, (128, 256)), 0, 1, stride=1, stride_axis=0)
                    bias[h, d] = tile[:, :128]
    lane = lax.broadcasted_iota(jnp.int32, (1, 128), 1)
    q = q_ref[...]
    keys = jnp.concatenate([k_ref[...], ks_ref[...]], axis=1)
    v_t = v_ref[...].T
    parts = []
    for h in range(2):
        mine = (lane // DH) == h
        qa = jnp.concatenate([jnp.where(mine, q, 0).astype(BF), qs_ref[...]], axis=1)
        cols = []
        for c in range(length // 256):
            n = 256 * (c + 1) if causal else length
            s = dot(keys[:n], qa[256 * c: 256 * (c + 1)], NT)
            if causal:
                rows = []
                for kb in range(n // 128):
                    tiles = []
                    for qb in (2 * c, 2 * c + 1):
                        st = s[128 * kb:128 * (kb + 1), 128 * (qb - 2 * c):128 * (qb - 2 * c + 1)]
                        if qb >= kb:
                            tiles.append(st + bias[h, qb - kb])
                        else:
                            tiles.append(jnp.full((128, 128), NEGATIVE, F32))
                    rows.append(jnp.concatenate(tiles, axis=1))
                s = jnp.concatenate(rows, axis=0)
            top = jnp.max(s, axis=0, keepdims=True)
            e = jnp.exp(s - top)
            p = (e * (1.0 / jnp.sum(e, axis=0, keepdims=True))).astype(BF)
            p_ref[h, pl.ds(0, n), pl.ds(256 * c, 256)] = p
            if n < length:
                p_ref[h, pl.ds(n, length - n), pl.ds(256 * c, 256)] = jnp.zeros((length - n, 256), BF)
            cols.append(dot(v_t[DH * h: DH * (h + 1), :n], p))
        parts.append(jnp.concatenate(cols, axis=1))
    o_ref[...] = jnp.concatenate(parts, axis=0).T.astype(BF)


def attn_fwd(q_arr, q_col, k_arr, k_col, v_arr, v_col, q_seg, k_seg, table=None):
    rows, length = q_seg.shape[:2]
    pairs = 6
    causal = table is not None
    block = lambda col: pl.BlockSpec((length, 128), lambda h, b: (b, col + h))
    seg = pl.BlockSpec((None, length, 128), lambda h, b: (b, 0, 0))
    in_specs = [block(q_col), block(k_col), block(v_col), seg, seg]
    args = [q_arr, k_arr, v_arr, q_seg, k_seg]
    scratch = []
    if causal:
        in_specs.append(pl.BlockSpec((2, 1, table.shape[2]), lambda h, b: (h, 0, 0)))
        args.append(table)
        scratch = [pltpu.VMEM((2, length // 128, 128, 128), F32)]
    return pl.pallas_call(
        functools.partial(attn_fwd_kernel, causal),
        grid=(pairs, rows),
        in_specs=in_specs,
        out_specs=[pl.BlockSpec((length, 128), lambda h, b: (b, h)), pl.BlockSpec((None, 2, length, length), lambda h, b: (b, h, 0, 0))],
        out_shape=[jax.ShapeDtypeStruct((rows * length, pairs * 128), BF), jax.ShapeDtypeStruct((rows, 2 * pairs, length, length), BF)],
        scratch_shapes=scratch,
        compiler_params=pltpu.CompilerParams(vmem_limit_bytes=32 * MB),
        name="attn_fwd_self" if causal else "attn_fwd_cross",
    )(*args)


def attn_bwd_kernel(causal, q_ref, k_ref, v_ref, g_ref, o_ref, p_ref, *rest):
    if causal:
        dq_ref, dk_ref, dv_ref, diag_ref, acc = rest
    else:
        dq_ref, dk_ref, dv_ref = rest
    length = q_ref.shape[0]
    lane = lax.broadcasted_iota(jnp.int32, (1, 128), 1)
    q = q_ref[...]
    g = g_ref[...]
    values = jnp.concatenate([v_ref[...], jnp.broadcast_to((lane < 2).astype(BF), (length, 128))], axis=1)
    k_t = k_ref[...].T
    prod = g.astype(F32) * o_ref[...].astype(F32)
    if causal:
        @pl.when(pl.program_id(1) == 0)
        def _():
            acc[...] = jnp.zeros_like(acc)
    dq_parts = []
    dk = [None] * (length // 256)
    dv = [None] * (length // 256)
    add = lambda old, new: new if old is None else old + new
    for h in range(2):
        mine = (lane // DH) == h
        delta = -jnp.sum(jnp.where(mine, prod, 0.0), axis=1, keepdims=True)
        high = delta.astype(BF)
        lowp = (delta - high.astype(F32)).astype(BF)
        extra = jnp.where(lane == 0, high, jnp.where(lane == 1, lowp, jnp.zeros_like(lowp)))
        gm = jnp.where(mine, g, 0).astype(BF)
        qm = jnp.where(mine, q, 0).astype(BF)
        ga = jnp.concatenate([gm, extra], axis=1)
        cols = []
        for c in range(length // 256):
            n = 256 * (c + 1) if causal else length
            qsl = slice(256 * c, 256 * (c + 1))
            p = p_ref[h, pl.ds(0, n), pl.ds(256 * c, 256)]
            dp = dot(values[:n], ga[qsl], NT)
            ds = (p.astype(F32) * dp).astype(BF)
            if causal:
                for kb in range(n // 128):
                    for qb in (2 * c, 2 * c + 1):
                        if qb >= kb:
                            acc[h, qb - kb] += ds[128 * kb:128 * (kb + 1), 128 * (qb - 2 * c):128 * (qb - 2 * c + 1)].astype(F32)
            cols.append(dot(k_t[DH * h: DH * (h + 1), :n], ds))
            dkn = dot(ds, qm[qsl])
            dvn = dot(p, gm[qsl])
            for kc in range(n // 256):
                ksl = slice(256 * kc, 256 * (kc + 1))
                dk[kc] = add(dk[kc], dkn[ksl])
                dv[kc] = add(dv[kc], dvn[ksl])
        dq_parts.append(jnp.concatenate(cols, axis=1))
    dq_ref[...] = jnp.concatenate(dq_parts, axis=0).T.astype(BF)
    dk_ref[...] = jnp.concatenate(dk, axis=0).astype(BF)
    dv_ref[...] = jnp.concatenate(dv, axis=0).astype(BF)
    if causal:
        @pl.when(pl.program_id(1) == pl.num_programs(1) - 1)
        def _():
            flip = (lax.broadcasted_iota(jnp.int32, (128, 128), 0) + lax.broadcasted_iota(jnp.int32, (128, 128), 1) == 127).astype(F32)
            for h in range(2):
                for d in range(length // 128):
                    upside = jnp.dot(flip, acc[h, d], precision=lax.Precision.HIGHEST, preferred_element_type=F32)
                    wide = jnp.concatenate([upside, jnp.zeros((128, 128), F32)], axis=1)
                    turned = pltpu.roll(wide, 0, 1, stride=1, stride_axis=0)
                    diag_ref[h, pl.ds(d, 1), :] = jnp.sum(turned, axis=0, keepdims=True)


def attn_bwd(q_arr, q_col, k_arr, k_col, v_arr, v_col, grad, out, probs, causal):
    rows, heads, length = probs.shape[:3]
    pairs = heads // 2
    block = lambda col: pl.BlockSpec((length, 128), lambda h, b: (b, col + h))
    flat = jax.ShapeDtypeStruct((rows * length, pairs * 128), BF)
    out_specs = [block(0)] * 3
    out_shape = [flat] * 3
    scratch = []
    if causal:
        out_specs.append(pl.BlockSpec((2, length // 128, 256), lambda h, b: (h, 0, 0)))
        out_shape.append(jax.ShapeDtypeStruct((heads, length // 128, 256), F32))
        scratch = [pltpu.VMEM((2, length // 128, 128, 128), F32)]
    return pl.pallas_call(
        functools.partial(attn_bwd_kernel, causal),
        grid=(pairs, rows),
        in_specs=[block(q_col), block(k_col), block(v_col), block(0), block(0), pl.BlockSpec((None, 2, length, length), lambda h, b: (b, h, 0, 0))],
        out_specs=out_specs,
        out_shape=out_shape,
        scratch_shapes=scratch,
        compiler_params=pltpu.CompilerParams(vmem_limit_bytes=40 * MB),
        name="attn_bwd_self" if causal else "attn_bwd_cross",
    )(q_arr, k_arr, v_arr, grad, out, probs)


def score_table(rel_bias, buckets):
    hot = buckets[:, None] == jnp.arange(rel_bias.shape[0])[None, :]
    at = jnp.sum(jnp.where(hot[:, :, None], rel_bias[None], 0.0), axis=1)
    return jnp.concatenate([jnp.full((rel_bias.shape[1], 128), NEGATIVE, F32), at.T], axis=1)[:, None]


def bucket_sums(diag, buckets, count):
    heads, blocks, _ = diag.shape
    own = diag[:, :, 127:255]
    before = jnp.pad(diag[:, 1:, :127], ((0, 0), (0, 1), (1, 0)))
    at = (own + before).reshape(heads, blocks * 128)
    hot = buckets[:, None] == jnp.arange(count)[None, :]
    return jnp.sum(jnp.where(hot[:, :, None], at.T[:, None, :], 0.0), axis=0)


EPSILON = 1e-06
ROOT_HALF = 0.7071067811865476
INV_ROOT_TWO_PI = 0.3989422804014327
WIDE, NARROW = "wide", "narrow"


def rms_forward(value_rows, gain_row):
    inverse = lax.rsqrt(jnp.mean(value_rows * value_rows, axis=-1, keepdims=True) + EPSILON)
    unit_rows = value_rows * inverse
    return (unit_rows * gain_row, unit_rows, inverse)


def rms_backward(grad_norm, unit_rows, inverse, gain_row):
    grad_gain = jnp.sum(grad_norm * unit_rows, axis=0)
    grad_unit = grad_norm * gain_row
    grad_value = inverse * (
        grad_unit - unit_rows * jnp.mean(grad_unit * unit_rows, axis=-1, keepdims=True)
    )
    return (grad_value, grad_gain)


def flipped(size, bit):
    return [(i, i ^ bit) for i in range(size)]


def bits_of(size):
    return [1 << i for i in range(size.bit_length() - 1)]


def wide_order(size, turn):
    low, rest = bits_of(size)[:1], bits_of(size)[1:]
    turn = turn % len(rest)
    return rest[turn:] + rest[:turn] + low


def gather_rows(block, sizes, turn):
    wide, narrow = sizes
    at = lax.axis_index(NARROW)
    for bit in bits_of(narrow):
        other = lax.ppermute(block, NARROW, flipped(narrow, bit))
        upper = (at & bit) != 0
        block = jnp.concatenate([jnp.where(upper, other, block), jnp.where(upper, block, other)], axis=0)
    pieces, offsets = [block], [0]
    for bit in wide_order(wide, turn):
        pieces = pieces + [lax.ppermute(piece, WIDE, flipped(wide, bit)) for piece in pieces]
        offsets = offsets + [offset ^ bit for offset in offsets]
    me = lax.axis_index(WIDE)
    rows = block.shape[0]
    whole = jnp.zeros((wide * rows, block.shape[1]), block.dtype)
    for piece, offset in zip(pieces, offsets):
        whole = lax.dynamic_update_slice(whole, piece, ((me ^ offset) * rows, 0))
    return whole


def scatter_rows(total, sizes, turn):
    wide, narrow = sizes
    columns = total.shape[1]
    me, at = lax.axis_index(WIDE), lax.axis_index(NARROW)

    def halve(value, axis_name, size, place, bit, parts):
        value = value.reshape(parts, 2, -1, columns)
        mine = (place // bit) % 2
        keep = lax.dynamic_slice_in_dim(value, mine, 1, 1)
        send = lax.dynamic_slice_in_dim(value, 1 - mine, 1, 1)
        received = lax.ppermute(send, axis_name, flipped(size, bit))
        return keep.astype(F32) + received.astype(F32)

    order = wide_order(wide, turn)[::-1]
    value = total
    left = list(bits_of(wide))
    for bit in order:
        parts = 1 << sum(b > bit for b in left)
        value = halve(value, WIDE, wide, me, bit, parts).astype(BF)
        left.remove(bit)
    for bit in bits_of(narrow)[::-1]:
        value = halve(value, NARROW, narrow, at, bit, 1)
        if bit != 1:
            value = value.astype(BF)
    return value.reshape(-1, columns).astype(F32)


def body(sizes, inputs, encoder_out, segments, enc_segments, buckets, gains, rel_bias, self_q, self_kv, self_out, cross_q, cross_kv, cross_out, ffn_in, ffn_out, out_grad):
    micro, per, length, width = inputs.shape
    rows = micro * per
    hidden = ffn_in.shape[1] // 2
    flat = lambda v: v.reshape(rows * length, width)
    state_in, enc_rows, grad_out = flat(inputs), flat(encoder_out), flat(out_grad)
    seg, enc_seg = segments.reshape(rows, length), enc_segments.reshape(rows, length)
    self_seg = segment_columns(seg, seg)
    cross_seg = segment_columns(seg, enc_seg)
    table = score_table(rel_bias, buckets)

    gain_cols = jnp.pad(gains.T, ((0, 0), (0, 125)))
    slab_self = gather_rows(jnp.concatenate([self_q, self_kv[0], self_kv[1], self_out.T, gain_cols], axis=1), sizes, 0)
    slab_cross = gather_rows(jnp.concatenate([cross_q, cross_kv[0], cross_kv[1], cross_out.T], axis=1), sizes, 1)
    outer_t = ffn_out.T
    slab_ffn = [
        gather_rows(jnp.concatenate([ffn_in[:, hidden * i: hidden * (i + 1)], outer_t[:, hidden * i: hidden * (i + 1)]], axis=1), sizes, i)
        for i in range(2)
    ]
    w_qkv, w_out = slab_self[:, : 3 * width], slab_self[:, 3 * width: 4 * width]
    gain_rows = slab_self[:, 4 * width: 4 * width + 3].T.astype(F32)
    c_query, c_keyval, c_out = slab_cross[:, :width], slab_cross[:, width: 3 * width], slab_cross[:, 3 * width:]

    state_in = state_in.astype(F32)
    normed_one, unit_one, inverse_one = rms_forward(state_in, gain_rows[0])
    normed_one = normed_one.astype(BF)
    qkv = dot(normed_one, w_qkv).astype(BF)
    attended, self_p = attn_fwd(qkv, 0, qkv, 6, qkv, 12, *self_seg, table)
    state_two = state_in + dot(attended, w_out, NT)
    normed_two, unit_two, inverse_two = rms_forward(state_two, gain_rows[1])
    normed_two = normed_two.astype(BF)
    cross_queries = dot(normed_two, c_query).astype(BF)
    cross_keyval = dot(enc_rows, c_keyval).astype(BF)
    mixed, cross_p = attn_fwd(cross_queries, 0, cross_keyval, 0, cross_keyval, 6, *cross_seg)
    state_three = state_two + dot(mixed, c_out, NT)
    normed_three, unit_three, inverse_three = rms_forward(state_three, gain_rows[2])
    normed_three = normed_three.astype(BF)
    layer = state_three
    grad_normed = 0.0
    ffn_grads = []
    for i in range(2):
        w_in, w_back = slab_ffn[i][:, :hidden], slab_ffn[i][:, hidden:]
        pre = dot(normed_three, w_in)
        phi = 0.5 * (1.0 + lax.erf(pre * ROOT_HALF))
        act = (pre * phi).astype(BF)
        layer = layer + dot(act, w_back, NT)
        slope = phi + pre * jnp.exp(-0.5 * pre * pre) * INV_ROOT_TWO_PI
        grad_pre = (dot(grad_out, w_back) * slope).astype(BF)
        grad_normed = grad_normed + dot(grad_pre, w_in, NT)
        pair = jnp.concatenate([dot(normed_three, grad_pre, TN), dot(grad_out, act, TN)], axis=1).astype(BF)
        ffn_grads.append(scatter_rows(pair, sizes, i))
    grad_three, gain_three = rms_backward(grad_normed, unit_three, inverse_three, gain_rows[2])
    grad_three = grad_out.astype(F32) + grad_three
    three_low = grad_three.astype(BF)
    grad_mixed = dot(three_low, c_out).astype(BF)
    grad_cq, grad_ck, grad_cv = attn_bwd(cross_queries, 0, cross_keyval, 0, cross_keyval, 6, grad_mixed, mixed, cross_p, False)
    grad_ckv = jnp.concatenate([grad_ck, grad_cv], axis=1)
    cross_grads = jnp.concatenate([dot(normed_two, grad_cq, TN), dot(enc_rows, grad_ckv, TN), dot(three_low, mixed, TN)], axis=1).astype(BF)
    cross_sum = scatter_rows(cross_grads, sizes, 0)
    grad_encoded = dot(grad_ckv, c_keyval, NT)
    grad_two, gain_two = rms_backward(dot(grad_cq, c_query, NT), unit_two, inverse_two, gain_rows[1])
    grad_two = grad_three + grad_two
    two_low = grad_two.astype(BF)
    grad_att = dot(two_low, w_out).astype(BF)
    grad_q, grad_k, grad_v, diag = attn_bwd(qkv, 0, qkv, 6, qkv, 12, grad_att, attended, self_p, True)
    grad_qkv = jnp.concatenate([grad_q, grad_k, grad_v], axis=1)
    grad_first, gain_one = rms_backward(dot(grad_qkv, w_qkv, NT), unit_one, inverse_one, gain_rows[0])
    grad_input = grad_two + grad_first
    gain_grads = jnp.pad(jnp.stack([gain_one, gain_two, gain_three], axis=1), ((0, 0), (0, 125)))
    self_grads = jnp.concatenate([dot(normed_one, grad_qkv, TN), dot(two_low, attended, TN), gain_grads], axis=1).astype(BF)
    self_sum = scatter_rows(self_grads, sizes, 1)
    bias_sum = lax.psum(bucket_sums(diag, buckets, rel_bias.shape[0]), (WIDE, NARROW))
    part = lambda v, i: v[:, width * i: width * (i + 1)]
    shaped = lambda v: v.reshape(micro, per, length, width)
    return (
        shaped(layer.astype(BF)),
        shaped(grad_input),
        shaped(grad_encoded),
        self_sum[:, 4 * width: 4 * width + 3].T,
        bias_sum,
        part(self_sum, 0),
        jnp.stack([part(self_sum, 1), part(self_sum, 2)]),
        part(self_sum, 3).T,
        part(cross_sum, 0),
        jnp.stack([part(cross_sum, 1), part(cross_sum, 2)]),
        part(cross_sum, 3).T,
        jnp.concatenate([g[:, :hidden] for g in ffn_grads], axis=1),
        jnp.concatenate([g[:, hidden:] for g in ffn_grads], axis=1).T,
    )


def solution(mesh):
    axes = (WIDE, NARROW)
    batch4, batch3 = P(None, axes, None, None), P(None, axes, None)
    first, second, middle = P(axes, None), P(None, axes), P(None, axes, None)
    sizes = (mesh.shape[WIDE], mesh.shape[NARROW])
    weights = (first, middle, second, first, middle, second, first, second)
    return jax.shard_map(
        functools.partial(body, sizes),
        mesh=mesh,
        in_specs=(batch4, batch4, batch3, batch3, P(), second, P()) + weights + (batch4,),
        out_specs=(batch4, batch4, batch4, second, P()) + weights,
        check_vma=False,
    )
```

```python
import functools
import jax
import jax.numpy as jnp
from jax import lax
from jax.sharding import PartitionSpec as P
from jax.experimental import pallas as pl
from jax.experimental.pallas import tpu as pltpu

DH = 64
NEGATIVE = -1e30
BF = jnp.bfloat16
F32 = jnp.float32
NN = (((1,), (0,)), ((), ()))
NT = (((1,), (1,)), ((), ()))
TN = (((0,), (0,)), ((), ()))
MB = 1 << 20


def dot(a, b, dims=NN):
    return lax.dot_general(a, b, dims, preferred_element_type=F32)


def segment_columns(query_seg, key_seg):
    ids = jnp.arange(128)
    other = (query_seg[..., None] != ids) & (ids < 4)
    query_cols = jnp.where(other, NEGATIVE, 0.0).astype(BF)
    key_cols = (key_seg[..., None] == ids).astype(BF)
    return query_cols, key_cols


def attn_fwd_kernel(causal, q_ref, k_ref, v_ref, qs_ref, ks_ref, *rest):
    if causal:
        t_ref, o_ref, p_ref, bias = rest
    else:
        o_ref, p_ref = rest
    length = q_ref.shape[0]
    if causal:
        @pl.when(pl.program_id(1) == 0)
        def _():
            for h in range(2):
                for d in range(length // 128):
                    row = jnp.concatenate([t_ref[h, :, pl.ds(128 * (d + 1), 128)], t_ref[h, :, pl.ds(128 * d, 128)]], axis=1)
                    tile = pltpu.roll(jnp.broadcast_to(row, (128, 256)), 0, 1, stride=1, stride_axis=0)
                    bias[h, d] = tile[:, :128]
    lane = lax.broadcasted_iota(jnp.int32, (1, 128), 1)
    q = q_ref[...]
    keys = jnp.concatenate([k_ref[...], ks_ref[...]], axis=1)
    v_t = v_ref[...].T
    parts = []
    for h in range(2):
        mine = (lane // DH) == h
        qa = jnp.concatenate([jnp.where(mine, q, 0).astype(BF), qs_ref[...]], axis=1)
        cols = []
        for c in range(length // 256):
            n = 256 * (c + 1) if causal else length
            s = dot(keys[:n], qa[256 * c: 256 * (c + 1)], NT)
            if causal:
                rows = []
                for kb in range(n // 128):
                    tiles = []
                    for qb in (2 * c, 2 * c + 1):
                        st = s[128 * kb:128 * (kb + 1), 128 * (qb - 2 * c):128 * (qb - 2 * c + 1)]
                        if qb >= kb:
                            tiles.append(st + bias[h, qb - kb])
                        else:
                            tiles.append(jnp.full((128, 128), NEGATIVE, F32))
                    rows.append(jnp.concatenate(tiles, axis=1))
                s = jnp.concatenate(rows, axis=0)
            top = jnp.max(s, axis=0, keepdims=True)
            e = jnp.exp(s - top)
            p = (e * (1.0 / jnp.sum(e, axis=0, keepdims=True))).astype(BF)
            p_ref[h, pl.ds(0, n), pl.ds(256 * c, 256)] = p
            if n < length:
                p_ref[h, pl.ds(n, length - n), pl.ds(256 * c, 256)] = jnp.zeros((length - n, 256), BF)
            cols.append(dot(v_t[DH * h: DH * (h + 1), :n], p))
        parts.append(jnp.concatenate(cols, axis=1))
    o_ref[...] = jnp.concatenate(parts, axis=0).T.astype(BF)


def attn_fwd(span, q_arr, q_col, k_arr, k_col, v_arr, v_col, q_seg, k_seg, table=None):
    rows, length = q_seg.shape[:2]
    begin, pairs = span
    causal = table is not None
    block = lambda col: pl.BlockSpec((length, 128), lambda h, b: (b, begin + col + h))
    seg = pl.BlockSpec((None, length, 128), lambda h, b: (b, 0, 0))
    in_specs = [block(q_col), block(k_col), block(v_col), seg, seg]
    args = [q_arr, k_arr, v_arr, q_seg, k_seg]
    scratch = []
    if causal:
        in_specs.append(pl.BlockSpec((2, 1, table.shape[2]), lambda h, b: (begin + h, 0, 0)))
        args.append(table)
        scratch = [pltpu.VMEM((2, length // 128, 128, 128), F32)]
    return pl.pallas_call(
        functools.partial(attn_fwd_kernel, causal),
        grid=(pairs, rows),
        in_specs=in_specs,
        out_specs=[pl.BlockSpec((length, 128), lambda h, b: (b, h)), pl.BlockSpec((None, 2, length, length), lambda h, b: (b, h, 0, 0))],
        out_shape=[jax.ShapeDtypeStruct((rows * length, pairs * 128), BF), jax.ShapeDtypeStruct((rows, 2 * pairs, length, length), BF)],
        scratch_shapes=scratch,
        compiler_params=pltpu.CompilerParams(vmem_limit_bytes=32 * MB),
        cost_estimate=pl.CostEstimate(flops=16 * rows * pairs * length * length * 256, bytes_accessed=4 * rows * pairs * length * length, transcendentals=0),
        name="attn_fwd_self" if causal else "attn_fwd_cross",
    )(*args)


def attn_bwd_kernel(causal, q_ref, k_ref, v_ref, g_ref, o_ref, p_ref, *rest):
    if causal:
        dq_ref, dk_ref, dv_ref, diag_ref, acc = rest
    else:
        dq_ref, dk_ref, dv_ref = rest
    length = q_ref.shape[0]
    lane = lax.broadcasted_iota(jnp.int32, (1, 128), 1)
    q = q_ref[...]
    g = g_ref[...]
    values = jnp.concatenate([v_ref[...], jnp.broadcast_to((lane < 2).astype(BF), (length, 128))], axis=1)
    k_t = k_ref[...].T
    prod = g.astype(F32) * o_ref[...].astype(F32)
    if causal:
        @pl.when(pl.program_id(1) == 0)
        def _():
            acc[...] = jnp.zeros_like(acc)
    dq_parts = []
    dk = [None] * (length // 256)
    dv = [None] * (length // 256)
    add = lambda old, new: new if old is None else old + new
    for h in range(2):
        mine = (lane // DH) == h
        delta = -jnp.sum(jnp.where(mine, prod, 0.0), axis=1, keepdims=True)
        high = delta.astype(BF)
        lowp = (delta - high.astype(F32)).astype(BF)
        extra = jnp.where(lane == 0, high, jnp.where(lane == 1, lowp, jnp.zeros_like(lowp)))
        gm = jnp.where(mine, g, 0).astype(BF)
        qm = jnp.where(mine, q, 0).astype(BF)
        ga = jnp.concatenate([gm, extra], axis=1)
        cols = []
        for c in range(length // 256):
            n = 256 * (c + 1) if causal else length
            qsl = slice(256 * c, 256 * (c + 1))
            p = p_ref[h, pl.ds(0, n), pl.ds(256 * c, 256)]
            dp = dot(values[:n], ga[qsl], NT)
            ds = (p.astype(F32) * dp).astype(BF)
            if causal:
                for kb in range(n // 128):
                    for qb in (2 * c, 2 * c + 1):
                        if qb >= kb:
                            acc[h, qb - kb] += ds[128 * kb:128 * (kb + 1), 128 * (qb - 2 * c):128 * (qb - 2 * c + 1)].astype(F32)
            cols.append(dot(k_t[DH * h: DH * (h + 1), :n], ds))
            dkn = dot(ds, qm[qsl])
            dvn = dot(p, gm[qsl])
            for kc in range(n // 256):
                ksl = slice(256 * kc, 256 * (kc + 1))
                dk[kc] = add(dk[kc], dkn[ksl])
                dv[kc] = add(dv[kc], dvn[ksl])
        dq_parts.append(jnp.concatenate(cols, axis=1))
    dq_ref[...] = jnp.concatenate(dq_parts, axis=0).T.astype(BF)
    dk_ref[...] = jnp.concatenate(dk, axis=0).astype(BF)
    dv_ref[...] = jnp.concatenate(dv, axis=0).astype(BF)
    if causal:
        @pl.when(pl.program_id(1) == pl.num_programs(1) - 1)
        def _():
            flip = (lax.broadcasted_iota(jnp.int32, (128, 128), 0) + lax.broadcasted_iota(jnp.int32, (128, 128), 1) == 127).astype(F32)
            for h in range(2):
                for d in range(length // 128):
                    upside = jnp.dot(flip, acc[h, d], precision=lax.Precision.HIGHEST, preferred_element_type=F32)
                    wide = jnp.concatenate([upside, jnp.zeros((128, 128), F32)], axis=1)
                    turned = pltpu.roll(wide, 0, 1, stride=1, stride_axis=0)
                    diag_ref[h, pl.ds(d, 1), :] = jnp.sum(turned, axis=0, keepdims=True)


def attn_bwd(span, q_arr, q_col, k_arr, k_col, v_arr, v_col, grad, out, probs, causal):
    rows, heads, length = probs.shape[:3]
    begin, pairs = span
    block = lambda col: pl.BlockSpec((length, 128), lambda h, b: (b, begin + col + h))
    own = pl.BlockSpec((length, 128), lambda h, b: (b, h))
    flat = jax.ShapeDtypeStruct((rows * length, pairs * 128), BF)
    out_specs = [own] * 3
    out_shape = [flat] * 3
    scratch = []
    if causal:
        out_specs.append(pl.BlockSpec((2, length // 128, 256), lambda h, b: (h, 0, 0)))
        out_shape.append(jax.ShapeDtypeStruct((heads, length // 128, 256), F32))
        scratch = [pltpu.VMEM((2, length // 128, 128, 128), F32)]
    return pl.pallas_call(
        functools.partial(attn_bwd_kernel, causal),
        grid=(pairs, rows),
        in_specs=[block(q_col), block(k_col), block(v_col), block(0), own, pl.BlockSpec((None, 2, length, length), lambda h, b: (b, h, 0, 0))],
        out_specs=out_specs,
        out_shape=out_shape,
        scratch_shapes=scratch,
        compiler_params=pltpu.CompilerParams(vmem_limit_bytes=40 * MB),
        cost_estimate=pl.CostEstimate(flops=16 * rows * pairs * length * length * 256, bytes_accessed=4 * rows * pairs * length * length, transcendentals=0),
        name="attn_bwd_self" if causal else "attn_bwd_cross",
    )(q_arr, k_arr, v_arr, grad, out, probs)


def score_table(rel_bias, buckets):
    hot = buckets[:, None] == jnp.arange(rel_bias.shape[0])[None, :]
    at = jnp.sum(jnp.where(hot[:, :, None], rel_bias[None], 0.0), axis=1)
    return jnp.concatenate([jnp.full((rel_bias.shape[1], 128), NEGATIVE, F32), at.T], axis=1)[:, None]


def bucket_sums(diag, buckets, count):
    heads, blocks, _ = diag.shape
    own = diag[:, :, 127:255]
    before = jnp.pad(diag[:, 1:, :127], ((0, 0), (0, 1), (1, 0)))
    at = (own + before).reshape(heads, blocks * 128)
    hot = buckets[:, None] == jnp.arange(count)[None, :]
    return jnp.sum(jnp.where(hot[:, :, None], at.T[:, None, :], 0.0), axis=0)


EPSILON = 1e-06
ROOT_HALF = 0.7071067811865476
INV_ROOT_TWO_PI = 0.3989422804014327
WIDE, NARROW = "wide", "narrow"
VMEM_LIMIT = 56 * MB


def flipped(size, bit):
    return [(i, i ^ bit) for i in range(size)]


def bits_of(size):
    return [1 << i for i in range(size.bit_length() - 1)]


def merge(blocks, at):
    count = len(blocks)
    slots = []
    for j in range(count):
        slot = blocks[j]
        for k in range(count):
            if k != 0:
                slot = jnp.where((at ^ k) == 0, blocks[j ^ k], slot)
        slots.append(slot)
    return jnp.concatenate(slots, axis=0)


def low_bits(wide, rows):
    low = []
    for bit in bits_of(wide):
        if (rows * bit) % 16 == 0:
            break
        low.append(bit)
    return low


def cross_bits(wide, rows, turn):
    bits = [b for b in bits_of(wide) if b not in low_bits(wide, rows)]
    first, rest = bits[:1], bits[1:]
    turn = turn % max(len(rest), 1)
    return rest[turn:] + rest[:turn] + first


class Gather:
    def __init__(self, sizes, blocks):
        self.wide, self.narrow = sizes
        self.groups = [[b] for b in blocks]
        self.flight = None
        rows = blocks[0].shape[0] * self.narrow
        self.low = low_bits(self.wide, rows)
        self.orders = [cross_bits(self.wide, rows, i) for i in range(len(blocks))]
        self.plan = ["narrow"] + [("low", b) for b in self.low] + list(range(len(self.orders[0])))

    def go(self):
        step = self.plan[0]
        if step == "narrow":
            self.flight = [[lax.ppermute(g[0], NARROW, flipped(self.narrow, k)) for k in range(1, self.narrow)] for g in self.groups]
        elif isinstance(step, tuple):
            self.flight = [[lax.ppermute(g[0], WIDE, flipped(self.wide, step[1]))] for g in self.groups]
        else:
            self.flight = [[lax.ppermute(p, WIDE, flipped(self.wide, self.orders[i][step])) for p in g] for i, g in enumerate(self.groups)]

    def land(self):
        step = self.plan.pop(0)
        if step == "narrow":
            at = lax.axis_index(NARROW)
            self.groups = [[merge(g + f, at)] for g, f in zip(self.groups, self.flight)]
        elif isinstance(step, tuple):
            at = (lax.axis_index(WIDE) // step[1]) % 2
            self.groups = [[merge(g + f, at)] for g, f in zip(self.groups, self.flight)]
        else:
            self.groups = [g + f for g, f in zip(self.groups, self.flight)]
        self.flight = None

    def state(self, landing):
        return (self.groups, self.flight if landing else None)

    def put(self, state, landing):
        self.groups = state[0]
        if landing:
            self.flight = state[1]

    def whole(self):
        skip = 1 << len(self.low)
        offsets = []
        for order in self.orders:
            found = [0]
            for bit in order:
                found = found + [f ^ (bit // skip) for f in found]
            offsets.append(found)
        place = (lax.axis_index(WIDE) // skip).astype(jnp.int32).reshape(1)
        return assemble(self.groups, offsets, place)


def assemble_kernel(offsets, columns, me_ref, *refs):
    pieces, out = refs[:-1], refs[-1]
    for g in range(len(columns)):
        for i, offset in enumerate(offsets[g]):
            piece = pieces[g * len(offsets[g]) + i]
            rows, width = piece.shape
            start = pl.multiple_of((me_ref[0] ^ offset) * rows, 16)
            out[pl.ds(start, rows), columns[g]: columns[g] + width] = piece[...]


def assemble(groups, offsets, place):
    widths = [g[0].shape[1] for g in groups]
    columns = [sum(widths[:i]) for i in range(len(groups))]
    flat = [p for g in groups for p in g]
    rows = groups[0][0].shape[0] * len(groups[0])
    return pl.pallas_call(
        functools.partial(assemble_kernel, offsets, columns),
        in_specs=[pl.BlockSpec(memory_space=pltpu.SMEM)] + [pl.BlockSpec(memory_space=pltpu.VMEM)] * len(flat),
        out_specs=pl.BlockSpec(memory_space=pltpu.VMEM),
        out_shape=jax.ShapeDtypeStruct((rows, sum(widths)), BF),
        compiler_params=pltpu.CompilerParams(vmem_limit_bytes=24 * MB),
        cost_estimate=pl.CostEstimate(flops=0, bytes_accessed=4 * rows * sum(widths), transcendentals=0),
        name="assemble",
    )(place, *flat)


class Scatter:
    def __init__(self, sizes, keep, send, first, turn):
        self.wide, self.narrow = sizes
        self.keep, self.sends = keep, [send]
        self.columns, self.lead = keep.shape[-1], keep.shape[0]
        self.left = [b for b in bits_of(self.wide) if b != first]
        high, low = [b for b in self.left if b > first], [b for b in self.left if b < first]
        turn = turn % max(len(high), 1)
        self.plan = [first] + high[turn:] + high[:turn] + low[::-1] + ["narrow"]
        self.flight = None

    def go(self):
        step = self.plan[0]
        if step == "narrow":
            self.flight = [lax.ppermute(s, NARROW, flipped(self.narrow, k + 1)) for k, s in enumerate(self.sends)]
        else:
            self.flight = [lax.ppermute(self.sends[0], WIDE, flipped(self.wide, step))]

    def land(self):
        self.plan.pop(0)
        value = self.keep.astype(F32)
        for received in self.flight:
            value = value + received.astype(F32)
        self.flight = None
        if not self.plan:
            self.keep, self.sends = value.reshape(self.lead, -1, self.columns), []
            return
        value = value.astype(BF)
        step = self.plan[0]
        if step == "narrow":
            value = value.reshape(self.lead, self.narrow, -1, self.columns)
            at = lax.axis_index(NARROW)
            pick = lambda k: lax.dynamic_slice_in_dim(value, at ^ k, 1, 1)[:, 0]
            self.keep, self.sends = pick(0), [pick(k) for k in range(1, self.narrow)]
        else:
            parts = self.lead << sum(b > step for b in self.left)
            self.left.remove(step)
            value = value.reshape(parts, 2, -1, self.columns)
            mine = (lax.axis_index(WIDE) // step) % 2
            pick = lambda k: lax.dynamic_slice_in_dim(value, k, 1, 1)[:, 0]
            self.keep, self.sends = pick(mine), [pick(1 - mine)]

    def state(self, landing):
        return (self.keep, self.sends, self.flight if landing else None)

    def put(self, state, landing):
        self.keep, self.sends = state[0], state[1]
        if landing:
            self.flight = state[2]


class Total:
    def __init__(self, sizes, value):
        self.value = value
        self.flight = None
        self.plan = [(name, size, bit) for name, size in zip((WIDE, NARROW), sizes) for bit in bits_of(size)]

    def go(self):
        name, size, bit = self.plan[0]
        self.flight = lax.ppermute(self.value, name, flipped(size, bit))

    def land(self):
        self.plan.pop(0)
        self.value, self.flight = self.value + self.flight, None

    def state(self, landing):
        return (self.value, self.flight if landing else None)

    def put(self, state, landing):
        self.value = state[0]
        if landing:
            self.flight = state[1]


class Rounds:
    def __init__(self):
        self.live = {}
        self.moving = []

    def __getitem__(self, name):
        return self.live[name]

    def run(self, work=None, go=(), land=()):
        for mover in go:
            mover.go()
            if mover not in self.moving:
                self.moving.append(mover)
        if work is not None:
            self.live.update(work())
        landing = [m for m in self.moving if m in land]
        known = [m for m in self.moving if m.flight is None or m in landing]
        live, states = lax.optimization_barrier((self.live, [m.state(m in landing) for m in known]))
        self.live = live
        for mover, state in zip(known, states):
            mover.put(state, mover in landing)
        for mover in landing:
            mover.land()

    def step(self, work=None, movers=()):
        movers = [m for m in movers if m.plan]
        self.run(work, movers, movers)


def store_halves(me, first_rows, result, keep_ref, send_ref, at):
    low = result.astype(BF)
    for part in range(result.shape[0] // (2 * first_rows)):
        even = low[2 * part * first_rows: (2 * part + 1) * first_rows]
        odd = low[(2 * part + 1) * first_rows: (2 * part + 2) * first_rows]
        index = at(part)
        keep_ref[index] = jnp.where(me == 0, even, odd)
        send_ref[index] = jnp.where(me == 0, odd, even)


def unit_of(value):
    inverse = lax.rsqrt(jnp.mean(value * value, axis=-1, keepdims=True) + EPSILON)
    return value * inverse, inverse


def norm_back(grad_norm, value, gain):
    unit, inverse = unit_of(value)
    grad_gain = jnp.sum(grad_norm * unit, axis=0, keepdims=True)
    grad_unit = grad_norm * gain
    return inverse * (grad_unit - unit * jnp.mean(grad_unit * unit, axis=-1, keepdims=True)), grad_gain


def call(kernel, name, grid, ins, outs, flops, scratch=(), limit=VMEM_LIMIT):
    spec = lambda block, index: pl.BlockSpec(block, index) if index is not None else pl.BlockSpec(memory_space=block)
    size = lambda shape, kind: jnp.dtype(kind).itemsize * functools.reduce(lambda a, b: a * b, shape, 1)
    moved = sum(size(a.shape, a.dtype) for a, _, _ in ins) + sum(size(o[0], o[1]) for o in outs)
    return pl.pallas_call(
        kernel,
        grid=grid,
        in_specs=[spec(b, i) for _, b, i in ins],
        out_specs=[spec(b, i) for _, _, b, i in outs],
        out_shape=[jax.ShapeDtypeStruct(s, d) for s, d, _, _ in outs],
        scratch_shapes=list(scratch),
        compiler_params=pltpu.CompilerParams(vmem_limit_bytes=limit),
        cost_estimate=pl.CostEstimate(flops=flops, bytes_accessed=moved, transcendentals=0),
        name=name,
    )(*[a for a, _, _ in ins])


ROWS = 256
row_map = lambda i: (i, 0)
col_map = lambda i: (0, i)
whole = lambda i: (0, 0)
at_col = lambda c: (lambda i: (0, c))


def proj_self_kernel(x_ref, gain_ref, w_ref, nt_ref, qkv_ref):
    unit, _ = unit_of(x_ref[...].astype(F32))
    n = (unit * gain_ref[0:1, :]).astype(BF)
    nt_ref[...] = n.T
    qkv_ref[...] = dot(n, w_ref[...]).astype(BF)


def spans_dot(refs, w, dims):
    total, at = None, 0
    for ref in refs:
        columns = ref.shape[1]
        term = dot(ref[...], w[:, at: at + columns], dims)
        total = term if total is None else total + term
        at += columns
    return total


def mid_kernel(x_ref, e_ref, gain_ref, wo_ref, wc_ref, *refs):
    o_refs, (x2_ref, nt_ref, qc_ref, kv_ref, et_ref) = refs[:-5], refs[-5:]
    width = x_ref.shape[1]
    e = e_ref[...]
    et_ref[...] = e.T
    kv_ref[...] = dot(e, wc_ref[:, width: 3 * width]).astype(BF)
    x2 = x_ref[...].astype(F32) + spans_dot(o_refs, wo_ref, NT)
    x2_ref[...] = x2
    unit, _ = unit_of(x2)
    n = (unit * gain_ref[1:2, :]).astype(BF)
    nt_ref[...] = n.T
    qc_ref[...] = dot(n, wc_ref[:, :width]).astype(BF)


def third_kernel(x2_ref, g_ref, gain_ref, wo_ref, *refs):
    o_refs, (x3_ref, n_ref, nt_ref, gt_ref) = refs[:-4], refs[-4:]
    x3 = x2_ref[...] + spans_dot(o_refs, wo_ref, NT)
    x3_ref[...] = x3
    unit, _ = unit_of(x3)
    n = (unit * gain_ref[2:3, :]).astype(BF)
    n_ref[...] = n
    nt_ref[...] = n.T
    gt_ref[...] = g_ref[...].T


def ffn_kernel(first_rows, me_ref, n_ref, nt_ref, g_ref, gt_ref, win_ref, wout_ref, y_ref, dn_ref, keep_in_ref, send_in_ref, keep_out_ref, send_out_ref):
    step = pl.program_id(0)
    w_in, w_out = win_ref[...], wout_ref[...]
    tokens = n_ref.shape[0]

    @pl.when(step == 0)
    def _():
        y_ref[...] = jnp.zeros_like(y_ref)
        dn_ref[...] = jnp.zeros_like(dn_ref)

    acts, grads = [], []
    for r in range(tokens // ROWS):
        rows = pl.ds(ROWS * r, ROWS)
        a = dot(n_ref[rows, :], w_in)
        back = dot(g_ref[rows, :], w_out)
        phi = 0.5 * (1.0 + lax.erf(a * ROOT_HALF))
        act = (a * phi).astype(BF)
        slope = phi + a * jnp.exp(-0.5 * a * a) * INV_ROOT_TWO_PI
        da = (back * slope).astype(BF)
        y_ref[rows, :] += dot(act, w_out, NT)
        dn_ref[rows, :] += dot(da, w_in, NT)
        acts.append(act)
        grads.append(da)
    act = jnp.concatenate(acts, axis=0)
    da = jnp.concatenate(grads, axis=0)
    me = me_ref[0]
    store_halves(me, first_rows, dot(nt_ref[...], da), keep_in_ref, send_in_ref, lambda p: (0, p))
    store_halves(me, first_rows, dot(gt_ref[...], act), keep_out_ref, send_out_ref, lambda p: (0, p))


def top_kernel(ya_ref, yb_ref, da_ref, db_ref, x3_ref, g_ref, gain_ref, wo_ref, out_ref, dx_ref, lowt_ref, doc_ref, gg_ref):
    x3 = x3_ref[...]
    out_ref[...] = (x3 + (ya_ref[...] + yb_ref[...])).astype(BF)
    grad, grad_gain = norm_back(da_ref[...] + db_ref[...], x3, gain_ref[2:3, :])
    dx = g_ref[...].astype(F32) + grad
    dx_ref[...] = dx
    low = dx.astype(BF)
    lowt_ref[...] = low.T
    doc_ref[...] = dot(low, wo_ref[...]).astype(BF)

    @pl.when(pl.program_id(0) == 0)
    def _():
        gg_ref[...] = jnp.zeros_like(gg_ref)

    gg_ref[0:1, :] += grad_gain


def second_kernel(x2_ref, dx3_ref, gain_ref, wq_ref, wo_ref, *refs):
    dq_refs, (dx_ref, lowt_ref, do_ref, gg_ref) = refs[:-4], refs[-4:]
    grad, grad_gain = norm_back(spans_dot(dq_refs, wq_ref, NT), x2_ref[...], gain_ref[1:2, :])
    dx = dx3_ref[...] + grad
    dx_ref[...] = dx
    low = dx.astype(BF)
    lowt_ref[...] = low.T
    do_ref[...] = dot(low, wo_ref[...]).astype(BF)

    @pl.when(pl.program_id(0) == 0)
    def _():
        gg_ref[...] = jnp.zeros_like(gg_ref)

    gg_ref[0:1, :] += grad_gain


def last_kernel(x_ref, dx2_ref, gain_ref, wq_ref, wk_ref, wv_ref, ck_ref, cv_ref, *refs):
    d_refs, (dx_ref, de_ref, gg_ref) = refs[:-3], refs[-3:]
    n = len(d_refs) // 5
    dq, dk, dv, dkc, dvc = (d_refs[n * i: n * (i + 1)] for i in range(5))
    dn = spans_dot(dq, wq_ref, NT) + spans_dot(dk, wk_ref, NT) + spans_dot(dv, wv_ref, NT)
    grad, grad_gain = norm_back(dn, x_ref[...].astype(F32), gain_ref[0:1, :])
    dx_ref[...] = dx2_ref[...] + grad
    de_ref[...] = spans_dot(dkc, ck_ref, NT) + spans_dot(dvc, cv_ref, NT)

    @pl.when(pl.program_id(0) == 0)
    def _():
        gg_ref[...] = jnp.zeros_like(gg_ref)

    gg_ref[0:1, :] += grad_gain


def grads_kernel(first_rows, lefts, count, me_ref, *refs):
    n_left = max(lefts) + 1
    left_refs, right_refs = refs[:n_left], refs[n_left: n_left + count]
    keep_ref, send_ref, left_buf, right_buf, sems = refs[n_left + count:]
    width = right_buf.shape[2]
    tile = 384 if width % 256 else 256
    widths = [width] * count

    def copies(p):
        found = [pltpu.make_async_copy(right_refs[p], right_buf.at[p % 2], sems.at[p % 2])]
        if p == 0 or lefts[p] != lefts[p - 1]:
            found.append(pltpu.make_async_copy(left_refs[lefts[p]], left_buf.at[lefts[p] % 2], sems.at[2 + lefts[p] % 2]))
        return found

    for copy in copies(0):
        copy.start()
    for p in range(count):
        if p + 1 < count:
            for copy in copies(p + 1):
                copy.start()
        for copy in copies(p):
            copy.wait()

        base = sum(widths[:p])

        def column(j, carry, p=p, base=base):
            col = pl.multiple_of(j * tile, tile)
            result = dot(left_buf[lefts[p] % 2], right_buf[p % 2, :, pl.ds(col, tile)])
            out = pl.multiple_of(base + j * tile, 128)
            store_halves(me_ref[0], first_rows, result, keep_ref, send_ref, lambda part: (0, part, slice(None), pl.ds(out, tile)))
            return carry

        lax.fori_loop(0, widths[p] // tile, column, 0)


def weight_grads(name, lefts_arrays, lefts, rights, half, first_rows):
    width = lefts_arrays[0].shape[0]
    tokens = rights[0].shape[0]
    columns = rights[0].shape[1]
    count = len(rights)
    shape = (1, width // (2 * first_rows), first_rows, count * columns)
    flops = 2 * width * tokens * columns * count
    return pl.pallas_call(
        functools.partial(grads_kernel, first_rows, lefts, count),
        in_specs=[pl.BlockSpec(memory_space=pltpu.SMEM)] + [pl.BlockSpec(memory_space=pl.ANY)] * (len(lefts_arrays) + count),
        out_specs=[pl.BlockSpec(memory_space=pltpu.VMEM)] * 2,
        out_shape=[jax.ShapeDtypeStruct(shape, BF)] * 2,
        scratch_shapes=[pltpu.VMEM((2, width, tokens), BF), pltpu.VMEM((2, tokens, columns), BF), pltpu.SemaphoreType.DMA((4,))],
        compiler_params=pltpu.CompilerParams(vmem_limit_bytes=VMEM_LIMIT),
        cost_estimate=pl.CostEstimate(flops=flops, bytes_accessed=2 * tokens * columns * count * 2, transcendentals=0),
        name=name,
    )(half, *lefts_arrays, *rights)


SPANS = ((0, 3), (3, 3))


def body(sizes, inputs, encoder_out, segments, enc_segments, buckets, gains, rel_bias, self_q, self_kv, self_out, cross_q, cross_kv, cross_out, ffn_in, ffn_out, out_grad):
    wide, narrow = sizes
    micro, per, length, width = inputs.shape
    rows = micro * per
    tokens = rows * length
    hidden = ffn_in.shape[1] // 2
    flat = lambda v: v.reshape(tokens, width)
    x, enc, grad_out = flat(inputs), flat(encoder_out), flat(out_grad)
    seg, enc_seg = segments.reshape(rows, length), enc_segments.reshape(rows, length)
    me = lax.axis_index(WIDE)

    outer_t = ffn_out.T
    gain_cols = jnp.pad(gains.T, ((0, 0), (0, 125)))
    g_self, g_cross, g_ffn0, g_ffn1 = [Gather(sizes, shard) for shard in (
        [jnp.concatenate([self_q, self_kv[0]], axis=1), jnp.concatenate([self_kv[1], self_out.T, gain_cols], axis=1)],
        [jnp.concatenate([cross_q, cross_kv[0]], axis=1), jnp.concatenate([cross_kv[1], cross_out.T], axis=1)],
        [ffn_in[:, :hidden], outer_t[:, :hidden]],
        [ffn_in[:, hidden:], outer_t[:, hidden:]],
    )]
    block_rows = self_q.shape[0] * narrow
    first = 1 << len(low_bits(wide, block_rows))
    first_rows = block_rows * first
    half = ((me // first) % 2).astype(jnp.int32).reshape(1)
    parts = width // (2 * first_rows)

    steps = (tokens // ROWS,)
    wide_f32 = lambda: ((tokens, width), F32, (ROWS, width), row_map)
    wide_low = lambda n=1: ((tokens, n * width), BF, (ROWS, n * width), row_map)
    turned = lambda: ((width, tokens), BF, (width, ROWS), col_map)
    gain_out = lambda: ((8, width), F32, (8, width), whole)
    rows_in = lambda v: (v, (ROWS, v.shape[1]), row_map)
    entire = lambda v: (v, v.shape, whole)
    piece = lambda slab, c: (slab, (width, width), at_col(c))
    unit = 2 * tokens * width * width

    r = Rounds()
    movers = [g_self, g_cross, g_ffn0, g_ffn1]
    r.moving = list(movers)
    r.live = {"x": x, "enc": enc, "g": grad_out}

    def prepare():
        return {"self_seg": segment_columns(seg, seg), "cross_seg": segment_columns(seg, enc_seg), "table": score_table(rel_bias, buckets)}

    def take_self():
        slab = g_self.whole()
        return {"slab_self": slab, "gain": slab[:, 4 * width: 4 * width + 3].T.astype(F32)}

    def proj():
        n1t, qkv = call(proj_self_kernel, "proj_self", steps, [rows_in(r["x"]), entire(r["gain"]), (r["slab_self"], (width, 3 * width), whole)], [turned(), wide_low(3)], 3 * unit)
        return {"n1t": n1t, "qkv": qkv}

    def fwd_self(i):
        o, p = attn_fwd(SPANS[i], r["qkv"], 0, r["qkv"], 6, r["qkv"], 12, *r["self_seg"], r["table"])
        return {f"o{i}": o, f"p{i}": p}

    def both(name):
        return [r[f"{name}{i}"] for i in range(len(SPANS))]

    def mid():
        out = call(mid_kernel, "mid", steps,
                   [rows_in(r["x"]), rows_in(r["enc"]), entire(r["gain"]), piece(r["slab_self"], 3), (r["slab_cross"], (width, 3 * width), whole)] + [rows_in(o) for o in both("o")],
                   [wide_f32(), turned(), wide_low(), wide_low(2), turned()], 4 * unit)
        return dict(zip(("x2", "n2t", "qc", "kvc", "et"), out))

    def fwd_cross(i):
        o, p = attn_fwd(SPANS[i], r["qc"], 0, r["kvc"], 0, r["kvc"], 6, *r["cross_seg"])
        return {f"oc{i}": o, f"pc{i}": p}

    def third():
        out = call(third_kernel, "third", steps,
                   [rows_in(r["x2"]), rows_in(r["g"]), entire(r["gain"]), piece(r["slab_cross"], 3)] + [rows_in(o) for o in both("oc")],
                   [wide_f32(), wide_low(), turned(), turned()], unit)
        return dict(zip(("x3", "n3", "n3t", "gt"), out))

    tile = 512
    tiles = hidden // tile
    halves = ((1, parts, first_rows, hidden), BF, (1, parts, first_rows, tile), lambda j: (0, 0, 0, j))
    acc_out = ((tokens, width), F32, (tokens, width), whole)

    def ffn(i):
        slab = r[f"slab_ffn{i}"]
        y, dn, *split = call(
            functools.partial(ffn_kernel, first_rows), "ffn", (tiles,),
            [(half, pltpu.SMEM, None), entire(r["n3"]), entire(r["n3t"]), entire(r["g"]), entire(r["gt"]),
             (slab, (width, tile), lambda j: (0, j)), (slab, (width, tile), lambda j: (0, tiles + j))],
            [acc_out, acc_out] + [halves] * 4, 12 * tokens * width * hidden)
        return {f"y{i}": y, f"dn{i}": dn, f"split{i}": split}

    def top():
        out = call(top_kernel, "top", steps,
                   [rows_in(r["y0"]), rows_in(r["y1"]), rows_in(r["dn0"]), rows_in(r["dn1"]), rows_in(r["x3"]), rows_in(r["g"]), entire(r["gain"]), piece(r["slab_cross"], 3)],
                   [wide_low(), wide_f32(), turned(), wide_low(), gain_out()], unit)
        return dict(zip(("layer", "dx3", "three_t", "doc", "gain3"), out))

    def bwd_cross(i):
        out = attn_bwd(SPANS[i], r["qc"], 0, r["kvc"], 0, r["kvc"], 6, r["doc"], r[f"oc{i}"], r[f"pc{i}"], False)
        return dict(zip((f"dqc{i}", f"dkc{i}", f"dvc{i}"), out))

    def second():
        out = call(second_kernel, "second", steps,
                   [rows_in(r["x2"]), rows_in(r["dx3"]), entire(r["gain"]), piece(r["slab_cross"], 0), piece(r["slab_self"], 3)] + [rows_in(d) for d in both("dqc")],
                   [wide_f32(), turned(), wide_low(), gain_out()], 2 * unit)
        return dict(zip(("dx2", "two_t", "do", "gain2"), out))

    def grads_cross():
        rights = both("dqc") + both("dkc") + both("dvc")
        n = len(SPANS)
        return {"cut_cross": weight_grads("grads_cross", [r["n2t"], r["et"]], (0,) * n + (1,) * (2 * n), rights, half, first_rows)}

    def grads_out():
        n = len(SPANS)
        return {"cut_out": weight_grads("grads_out", [r["three_t"], r["two_t"]], (0,) * n + (1,) * n, both("oc") + both("o"), half, first_rows)}

    def bwd_self(i):
        out = attn_bwd(SPANS[i], r["qkv"], 0, r["qkv"], 6, r["qkv"], 12, r["do"], r[f"o{i}"], r[f"p{i}"], True)
        return dict(zip((f"dq{i}", f"dk{i}", f"dv{i}", f"diag{i}"), out))

    def grads_self(i):
        return {f"cut_self{i}": weight_grads("grads_self", [r["n1t"]], (0, 0, 0), [r[f"dq{i}"], r[f"dk{i}"], r[f"dv{i}"]], half, first_rows)}

    def last():
        out = call(last_kernel, "last", steps,
                   [rows_in(r["x"]), rows_in(r["dx2"]), entire(r["gain"])] + [piece(r["slab_self"], c) for c in range(3)] + [piece(r["slab_cross"], c) for c in (1, 2)]
                   + [rows_in(d) for name in ("dq", "dk", "dv", "dkc", "dvc") for d in both(name)],
                   [wide_f32(), wide_f32(), gain_out()], 5 * unit)
        return dict(zip(("dx1", "de", "gain1"), out))

    def cut(pair, turn):
        return Scatter(sizes, pair[0], pair[1], first, turn)

    r.step(prepare, [g_self])
    r.step(None, [g_self, g_cross])
    r.step(None, [g_self, g_cross])
    while g_self.plan:
        r.step(None, [g_self])
    r.step(take_self, [])
    r.step(proj, [g_cross, g_ffn0])
    r.step(lambda: fwd_self(0), [g_cross, g_ffn0])
    r.step(lambda: fwd_self(1), [g_cross, g_ffn0, g_ffn1])
    while g_cross.plan:
        r.step(None, [g_cross])
    r.step(lambda: {"slab_cross": g_cross.whole()}, [])
    r.step(mid, [g_ffn0, g_ffn1])
    r.step(lambda: fwd_cross(0), [g_ffn0, g_ffn1])
    r.step(lambda: fwd_cross(1), [g_ffn0, g_ffn1])
    r.step(third, [g_ffn0, g_ffn1])
    while g_ffn0.plan or g_ffn1.plan:
        r.step(None, [g_ffn0, g_ffn1])
    r.step(lambda: {"slab_ffn0": g_ffn0.whole(), "slab_ffn1": g_ffn1.whole()}, [])
    r.moving = []
    r.step(lambda: ffn(0), [])
    split = r.live.pop("split0")
    f0 = [cut(split[2 * i: 2 * i + 2], i) for i in range(2)]
    r.step(lambda: ffn(1), f0)
    split = r.live.pop("split1")
    f1 = [cut(split[2 * i: 2 * i + 2], i) for i in range(2)]
    r.step(top, f0 + f1)
    r.step(lambda: bwd_cross(0), f0 + f1)
    r.step(lambda: bwd_cross(1), f0 + f1)
    r.step(second, f0 + f1)
    r.step(grads_cross, f1)
    sc = cut(r.live.pop("cut_cross"), 0)
    r.step(grads_out, [sc])
    so = cut(r.live.pop("cut_out"), 1)
    r.step(lambda: bwd_self(0), f1 + [sc, so])
    r.step(lambda: grads_self(0), f1 + [sc, so])
    s0 = cut(r.live.pop("cut_self0"), 1)
    r.step(lambda: bwd_self(1), f1 + [sc, so, s0])
    r.step(lambda: grads_self(1), f1 + [sc, so, s0])
    s1 = cut(r.live.pop("cut_self1"), 0)
    r.step(last, [sc, so, s0, s1])

    def small():
        diag = jnp.concatenate(both("diag"), axis=0)
        bias_rows = bucket_sums(diag, buckets, rel_bias.shape[0])
        return {"small": jnp.concatenate([r["gain1"][0], r["gain2"][0], r["gain3"][0], bias_rows.reshape(-1)]).reshape(-1, 128)}

    r.step(small, [sc, so, s0, s1])
    total = Total(sizes, r.live.pop("small"))
    movers = f0 + f1 + [sc, so, s0, s1, total]
    while any(m.plan for m in movers):
        r.step(None, movers)

    summed = total.value.reshape(-1)
    shard = me * narrow + lax.axis_index(NARROW)
    own = width // (wide * narrow)
    gain_sum = lax.dynamic_slice_in_dim(summed[: 3 * width].reshape(3, width), shard * own, own, 1)
    bias_sum = summed[3 * width:].reshape(rel_bias.shape)

    def columns(sums, index, count):
        found = []
        for s in sums:
            n = s.keep.shape[-1] // count
            found.append(s.keep[0, :, n * index: n * (index + 1)])
        return jnp.concatenate(found, axis=1) if len(found) > 1 else found[0]

    shaped = lambda v: v.reshape(micro, per, length, width)
    selfs = [s0, s1]
    return (
        shaped(r["layer"]),
        shaped(r["dx1"]),
        shaped(r["de"]),
        gain_sum,
        bias_sum,
        columns(selfs, 0, 3),
        jnp.stack([columns(selfs, 1, 3), columns(selfs, 2, 3)]),
        columns([so], 1, 2).T,
        columns([sc], 0, 3),
        jnp.stack([columns([sc], 1, 3), columns([sc], 2, 3)]),
        columns([so], 0, 2).T,
        jnp.concatenate([f0[0].keep[0], f1[0].keep[0]], axis=1),
        jnp.concatenate([f0[1].keep[0], f1[1].keep[0]], axis=1).T,
    )


def solution(mesh):
    axes = (WIDE, NARROW)
    batch4, batch3 = P(None, axes, None, None), P(None, axes, None)
    first, second, middle = P(axes, None), P(None, axes), P(None, axes, None)
    sizes = (mesh.shape[WIDE], mesh.shape[NARROW])
    weights = (first, middle, second, first, middle, second, first, second)
    return jax.shard_map(
        functools.partial(body, sizes),
        mesh=mesh,
        in_specs=(batch4, batch4, batch3, batch3, P(), second, P()) + weights + (batch4,),
        out_specs=(batch4, batch4, batch4, second, P()) + weights,
        check_vma=False,
    )
```

```python
import functools
import jax
import jax.numpy as jnp
from jax import lax
from jax.sharding import PartitionSpec as P
from jax.experimental import pallas as pl
from jax.experimental.pallas import tpu as pltpu

DH = 64
NEGATIVE = -1e30
BF = jnp.bfloat16
F32 = jnp.float32
NN = (((1,), (0,)), ((), ()))
NT = (((1,), (1,)), ((), ()))
TN = (((0,), (0,)), ((), ()))
MB = 1 << 20


def dot(a, b, dims=NN):
    return lax.dot_general(a, b, dims, preferred_element_type=F32)


def segment_columns(query_seg, key_seg):
    ids = jnp.arange(128)
    other = (query_seg[..., None] != ids) & (ids < 4)
    query_cols = jnp.where(other, NEGATIVE, 0.0).astype(BF)
    key_cols = (key_seg[..., None] == ids).astype(BF)
    return query_cols, key_cols


def attn_fwd_kernel(causal, q_ref, k_ref, v_ref, qs_ref, ks_ref, *rest):
    if causal:
        t_ref, o_ref, p_ref, bias = rest
    else:
        o_ref, p_ref = rest
    length = q_ref.shape[0]
    if causal:
        @pl.when(pl.program_id(1) == 0)
        def _():
            for h in range(2):
                for d in range(length // 128):
                    row = jnp.concatenate([t_ref[h, :, pl.ds(128 * (d + 1), 128)], t_ref[h, :, pl.ds(128 * d, 128)]], axis=1)
                    tile = pltpu.roll(jnp.broadcast_to(row, (128, 256)), 0, 1, stride=1, stride_axis=0)
                    bias[h, d] = tile[:, :128]
    lane = lax.broadcasted_iota(jnp.int32, (1, 128), 1)
    q = q_ref[...]
    keys = jnp.concatenate([k_ref[...], ks_ref[...]], axis=1)
    v_t = v_ref[...].T
    parts = []
    for h in range(2):
        mine = (lane // DH) == h
        qa = jnp.concatenate([jnp.where(mine, q, 0).astype(BF), qs_ref[...]], axis=1)
        cols = []
        for c in range(length // 256):
            n = 256 * (c + 1) if causal else length
            s = dot(keys[:n], qa[256 * c: 256 * (c + 1)], NT)
            if causal:
                rows = []
                for kb in range(n // 128):
                    tiles = []
                    for qb in (2 * c, 2 * c + 1):
                        st = s[128 * kb:128 * (kb + 1), 128 * (qb - 2 * c):128 * (qb - 2 * c + 1)]
                        if qb >= kb:
                            tiles.append(st + bias[h, qb - kb])
                        else:
                            tiles.append(jnp.full((128, 128), NEGATIVE, F32))
                    rows.append(jnp.concatenate(tiles, axis=1))
                s = jnp.concatenate(rows, axis=0)
            top = jnp.max(s, axis=0, keepdims=True)
            e = jnp.exp(s - top)
            p = (e * (1.0 / jnp.sum(e, axis=0, keepdims=True))).astype(BF)
            p_ref[h, pl.ds(0, n), pl.ds(256 * c, 256)] = p
            if n < length:
                p_ref[h, pl.ds(n, length - n), pl.ds(256 * c, 256)] = jnp.zeros((length - n, 256), BF)
            cols.append(dot(v_t[DH * h: DH * (h + 1), :n], p))
        parts.append(jnp.concatenate(cols, axis=1))
    o_ref[...] = jnp.concatenate(parts, axis=0).T.astype(BF)


def attn_fwd(span, q_arr, q_col, k_arr, k_col, v_arr, v_col, q_seg, k_seg, table=None):
    rows, length = q_seg.shape[:2]
    begin, pairs = span
    causal = table is not None
    block = lambda col: pl.BlockSpec((length, 128), lambda h, b: (b, begin + col + h))
    seg = pl.BlockSpec((None, length, 128), lambda h, b: (b, 0, 0))
    in_specs = [block(q_col), block(k_col), block(v_col), seg, seg]
    args = [q_arr, k_arr, v_arr, q_seg, k_seg]
    scratch = []
    if causal:
        in_specs.append(pl.BlockSpec((2, 1, table.shape[2]), lambda h, b: (begin + h, 0, 0)))
        args.append(table)
        scratch = [pltpu.VMEM((2, length // 128, 128, 128), F32)]
    return pl.pallas_call(
        functools.partial(attn_fwd_kernel, causal),
        grid=(pairs, rows),
        in_specs=in_specs,
        out_specs=[pl.BlockSpec((length, 128), lambda h, b: (b, h)), pl.BlockSpec((None, 2, length, length), lambda h, b: (b, h, 0, 0))],
        out_shape=[jax.ShapeDtypeStruct((rows * length, pairs * 128), BF), jax.ShapeDtypeStruct((rows, 2 * pairs, length, length), BF)],
        scratch_shapes=scratch,
        compiler_params=pltpu.CompilerParams(vmem_limit_bytes=60 * MB),
        cost_estimate=pl.CostEstimate(flops=16 * rows * pairs * length * length * 256, bytes_accessed=4 * rows * pairs * length * length, transcendentals=0),
        name="attn_fwd_self" if causal else "attn_fwd_cross",
    )(*args)


def attn_bwd_kernel(causal, q_ref, k_ref, v_ref, g_ref, o_ref, p_ref, *rest):
    if causal:
        dq_ref, dk_ref, dv_ref, diag_ref, acc = rest
    else:
        dq_ref, dk_ref, dv_ref = rest
    length = q_ref.shape[0]
    lane = lax.broadcasted_iota(jnp.int32, (1, 128), 1)
    q = q_ref[...]
    g = g_ref[...]
    values = jnp.concatenate([v_ref[...], jnp.broadcast_to((lane < 2).astype(BF), (length, 128))], axis=1)
    k_t = k_ref[...].T
    prod = g.astype(F32) * o_ref[...].astype(F32)
    if causal:
        @pl.when(pl.program_id(1) == 0)
        def _():
            acc[...] = jnp.zeros_like(acc)
    dq_parts = []
    dk = [None] * (length // 256)
    dv = [None] * (length // 256)
    add = lambda old, new: new if old is None else old + new
    for h in range(2):
        mine = (lane // DH) == h
        delta = -jnp.sum(jnp.where(mine, prod, 0.0), axis=1, keepdims=True)
        high = delta.astype(BF)
        lowp = (delta - high.astype(F32)).astype(BF)
        extra = jnp.where(lane == 0, high, jnp.where(lane == 1, lowp, jnp.zeros_like(lowp)))
        gm = jnp.where(mine, g, 0).astype(BF)
        qm = jnp.where(mine, q, 0).astype(BF)
        ga = jnp.concatenate([gm, extra], axis=1)
        cols = []
        for c in range(length // 256):
            n = 256 * (c + 1) if causal else length
            qsl = slice(256 * c, 256 * (c + 1))
            p = p_ref[h, pl.ds(0, n), pl.ds(256 * c, 256)]
            dp = dot(values[:n], ga[qsl], NT)
            ds = (p.astype(F32) * dp).astype(BF)
            if causal:
                for kb in range(n // 128):
                    for qb in (2 * c, 2 * c + 1):
                        if qb >= kb:
                            acc[h, qb - kb] += ds[128 * kb:128 * (kb + 1), 128 * (qb - 2 * c):128 * (qb - 2 * c + 1)].astype(F32)
            cols.append(dot(k_t[DH * h: DH * (h + 1), :n], ds))
            dkn = dot(ds, qm[qsl])
            dvn = dot(p, gm[qsl])
            for kc in range(n // 256):
                ksl = slice(256 * kc, 256 * (kc + 1))
                dk[kc] = add(dk[kc], dkn[ksl])
                dv[kc] = add(dv[kc], dvn[ksl])
        dq_parts.append(jnp.concatenate(cols, axis=1))
    dq_ref[...] = jnp.concatenate(dq_parts, axis=0).T.astype(BF)
    dk_ref[...] = jnp.concatenate(dk, axis=0).astype(BF)
    dv_ref[...] = jnp.concatenate(dv, axis=0).astype(BF)
    if causal:
        @pl.when(pl.program_id(1) == pl.num_programs(1) - 1)
        def _():
            flip = (lax.broadcasted_iota(jnp.int32, (128, 128), 0) + lax.broadcasted_iota(jnp.int32, (128, 128), 1) == 127).astype(F32)
            for h in range(2):
                for d in range(length // 128):
                    upside = jnp.dot(flip, acc[h, d], precision=lax.Precision.HIGHEST, preferred_element_type=F32)
                    wide = jnp.concatenate([upside, jnp.zeros((128, 128), F32)], axis=1)
                    turned = pltpu.roll(wide, 0, 1, stride=1, stride_axis=0)
                    diag_ref[h, pl.ds(d, 1), :] = jnp.sum(turned, axis=0, keepdims=True)


def attn_bwd(span, q_arr, q_col, k_arr, k_col, v_arr, v_col, grad, out, probs, causal):
    rows, heads, length = probs.shape[:3]
    begin, pairs = span
    block = lambda col: pl.BlockSpec((length, 128), lambda h, b: (b, begin + col + h))
    own = pl.BlockSpec((length, 128), lambda h, b: (b, h))
    flat = jax.ShapeDtypeStruct((rows * length, pairs * 128), BF)
    out_specs = [own] * 3
    out_shape = [flat] * 3
    scratch = []
    if causal:
        out_specs.append(pl.BlockSpec((2, length // 128, 256), lambda h, b: (h, 0, 0)))
        out_shape.append(jax.ShapeDtypeStruct((heads, length // 128, 256), F32))
        scratch = [pltpu.VMEM((2, length // 128, 128, 128), F32)]
    return pl.pallas_call(
        functools.partial(attn_bwd_kernel, causal),
        grid=(pairs, rows),
        in_specs=[block(q_col), block(k_col), block(v_col), block(0), own, pl.BlockSpec((None, 2, length, length), lambda h, b: (b, h, 0, 0))],
        out_specs=out_specs,
        out_shape=out_shape,
        scratch_shapes=scratch,
        compiler_params=pltpu.CompilerParams(vmem_limit_bytes=60 * MB),
        cost_estimate=pl.CostEstimate(flops=16 * rows * pairs * length * length * 256, bytes_accessed=4 * rows * pairs * length * length, transcendentals=0),
        name="attn_bwd_self" if causal else "attn_bwd_cross",
    )(q_arr, k_arr, v_arr, grad, out, probs)


def score_table(rel_bias, buckets):
    hot = buckets[:, None] == jnp.arange(rel_bias.shape[0])[None, :]
    at = jnp.sum(jnp.where(hot[:, :, None], rel_bias[None], 0.0), axis=1)
    return jnp.concatenate([jnp.full((rel_bias.shape[1], 128), NEGATIVE, F32), at.T], axis=1)[:, None]


def bucket_sums(diag, buckets, count):
    heads, blocks, _ = diag.shape
    own = diag[:, :, 127:255]
    before = jnp.pad(diag[:, 1:, :127], ((0, 0), (0, 1), (1, 0)))
    at = (own + before).reshape(heads, blocks * 128)
    hot = buckets[:, None] == jnp.arange(count)[None, :]
    return jnp.sum(jnp.where(hot[:, :, None], at.T[:, None, :], 0.0), axis=0)


EPSILON = 1e-06
ROOT_HALF = 0.7071067811865476
INV_ROOT_TWO_PI = 0.3989422804014327
WIDE, NARROW = "wide", "narrow"
VMEM_LIMIT = 60 * MB


def flipped(size, bit):
    return [(i, i ^ bit) for i in range(size)]


def bits_of(size):
    return [1 << i for i in range(size.bit_length() - 1)]


def merge(blocks, at):
    count = len(blocks)
    slots = []
    for j in range(count):
        slot = blocks[j]
        for k in range(count):
            if k != 0:
                slot = jnp.where((at ^ k) == 0, blocks[j ^ k], slot)
        slots.append(slot)
    return jnp.concatenate(slots, axis=0)


def low_bits(wide, rows):
    low = []
    for bit in bits_of(wide):
        if (rows * bit) % 16 == 0:
            break
        low.append(bit)
    return low


def cross_bits(wide, rows, turn):
    bits = [b for b in bits_of(wide) if b not in low_bits(wide, rows)]
    first, rest = bits[:1], bits[1:]
    turn = turn % max(len(rest), 1)
    return rest[turn:] + rest[:turn] + first


class Gather:
    def __init__(self, sizes, block, cuts):
        self.wide, self.narrow = sizes
        self.cuts = cuts
        self.groups = [[block]]
        self.flight = None
        rows = block.shape[0] * self.narrow
        self.low = low_bits(self.wide, rows)
        self.orders = [cross_bits(self.wide, rows, i) for i in range(len(cuts))]
        self.plan = ["narrow"] + [("low", b) for b in self.low] + list(range(len(self.orders[0])))

    def go(self):
        step = self.plan[0]
        if step == "narrow":
            self.flight = [[lax.ppermute(g[0], NARROW, flipped(self.narrow, k)) for k in range(1, self.narrow)] for g in self.groups]
        elif isinstance(step, tuple):
            self.flight = [[lax.ppermute(g[0], WIDE, flipped(self.wide, step[1]))] for g in self.groups]
        else:
            self.flight = [[lax.ppermute(p, WIDE, flipped(self.wide, self.orders[i][step])) for p in g] for i, g in enumerate(self.groups)]

    def land(self):
        step = self.plan.pop(0)
        joined = lambda at: [[merge(g + f, at)] for g, f in zip(self.groups, self.flight)]
        if step == "narrow":
            self.groups = joined(lax.axis_index(NARROW))
        elif isinstance(step, tuple):
            self.groups = joined((lax.axis_index(WIDE) // step[1]) % 2)
        else:
            self.groups = [g + f for g, f in zip(self.groups, self.flight)]
            if step == 0:
                self.groups = [[jnp.concatenate(g, axis=0)] for g in self.groups]
        if self.plan and self.plan[0] == 0:
            block = self.groups[0][0]
            ends = [sum(self.cuts[:i]) for i in range(len(self.cuts) + 1)]
            self.groups = [[block[:, ends[i]: ends[i + 1]]] for i in range(len(self.cuts))]
        self.flight = None

    def state(self, landing):
        return (self.groups, self.flight if landing else None)

    def put(self, state, landing):
        self.groups = state[0]
        if landing:
            self.flight = state[1]

    def whole(self):
        skip = 1 << len(self.low)
        offsets = []
        for order in self.orders:
            found = [0]
            for bit in order:
                found = found + [f ^ (bit // skip) for f in found]
            offsets.append(found)
        place = (lax.axis_index(WIDE) // skip).astype(jnp.int32).reshape(1)
        return assemble(self.groups, offsets, place)


def assemble_kernel(offsets, columns, counts, me_ref, *refs):
    pieces, out = list(refs[:-1]), refs[-1]
    for g in range(len(columns)):
        found = iter(offsets[g])
        for _ in range(counts[g]):
            piece = pieces.pop(0)
            width = piece.shape[1]
            rows = out.shape[0] // len(offsets[g])
            for k in range(piece.shape[0] // rows):
                start = pl.multiple_of((me_ref[0] ^ next(found)) * rows, 16)
                out[pl.ds(start, rows), columns[g]: columns[g] + width] = piece[rows * k: rows * (k + 1), :]


def assemble(groups, offsets, place):
    widths = [g[0].shape[1] for g in groups]
    columns = [sum(widths[:i]) for i in range(len(groups))]
    flat = [p for g in groups for p in g]
    rows = sum(p.shape[0] for p in groups[0])
    return pl.pallas_call(
        functools.partial(assemble_kernel, offsets, columns, [len(g) for g in groups]),
        in_specs=[pl.BlockSpec(memory_space=pltpu.SMEM)] + [pl.BlockSpec(memory_space=pltpu.VMEM)] * len(flat),
        out_specs=pl.BlockSpec(memory_space=pltpu.VMEM),
        out_shape=jax.ShapeDtypeStruct((rows, sum(widths)), BF),
        compiler_params=pltpu.CompilerParams(vmem_limit_bytes=VMEM_LIMIT),
        cost_estimate=pl.CostEstimate(flops=0, bytes_accessed=4 * rows * sum(widths), transcendentals=0),
        name="assemble",
    )(place, *flat)


class Scatter:
    def __init__(self, sizes, keep, send, first, turn):
        self.wide, self.narrow = sizes
        self.keep, self.sends = keep, [send]
        self.columns, self.lead = keep.shape[-1], keep.shape[0]
        self.left = [b for b in bits_of(self.wide) if b != first]
        high, low = [b for b in self.left if b > first], [b for b in self.left if b < first]
        turn = turn % max(len(high), 1)
        self.plan = [first] + high[turn:] + high[:turn] + low[::-1] + ["narrow"]
        self.flight = None

    def go(self):
        step = self.plan[0]
        if step == "narrow":
            self.flight = [lax.ppermute(s, NARROW, flipped(self.narrow, k + 1)) for k, s in enumerate(self.sends)]
        else:
            self.flight = [lax.ppermute(self.sends[0], WIDE, flipped(self.wide, step))]

    def land(self):
        self.plan.pop(0)
        value = self.keep.astype(F32)
        for received in self.flight:
            value = value + received.astype(F32)
        self.flight = None
        if not self.plan:
            self.keep, self.sends = value.reshape(self.lead, -1, self.columns), []
            return
        value = value.astype(BF)
        step = self.plan[0]
        if step == "narrow":
            value = value.reshape(self.lead, self.narrow, -1, self.columns)
            at = lax.axis_index(NARROW)
            pick = lambda k: lax.dynamic_slice_in_dim(value, at ^ k, 1, 1)[:, 0]
            self.keep, self.sends = pick(0), [pick(k) for k in range(1, self.narrow)]
        else:
            parts = self.lead << sum(b > step for b in self.left)
            self.left.remove(step)
            value = value.reshape(parts, 2, -1, self.columns)
            mine = (lax.axis_index(WIDE) // step) % 2
            pick = lambda k: lax.dynamic_slice_in_dim(value, k, 1, 1)[:, 0]
            self.keep, self.sends = pick(mine), [pick(1 - mine)]

    def state(self, landing):
        return (self.keep, self.sends, self.flight if landing else None)

    def put(self, state, landing):
        self.keep, self.sends = state[0], state[1]
        if landing:
            self.flight = state[2]


class Total:
    def __init__(self, sizes, value):
        self.value = value
        self.flight = None
        self.narrow = sizes[1]
        self.plan = [(sizes[0], bit) for bit in bits_of(sizes[0])] + ["narrow"]

    def go(self):
        if self.plan[0] == "narrow":
            self.flight = [lax.ppermute(self.value, NARROW, flipped(self.narrow, k)) for k in range(1, self.narrow)]
        else:
            self.flight = [lax.ppermute(self.value, WIDE, flipped(*self.plan[0]))]

    def land(self):
        if self.plan.pop(0) == "narrow":
            at = lax.axis_index(NARROW)
            parts = [self.value] + self.flight
            total = None
            for j in range(self.narrow):
                term = parts[0]
                for k in range(1, self.narrow):
                    term = jnp.where((at ^ k) == j, parts[k], term)
                total = term if total is None else total + term
            self.value = total
        else:
            self.value = self.value + self.flight[0]
        self.flight = None

    def state(self, landing):
        return (self.value, self.flight if landing else None)

    def put(self, state, landing):
        self.value = state[0]
        if landing:
            self.flight = state[1]


class Rounds:
    def __init__(self):
        self.live = {}
        self.moving = []

    def __getitem__(self, name):
        return self.live[name]

    def run(self, work=None, go=(), land=()):
        for mover in go:
            mover.go()
            if mover not in self.moving:
                self.moving.append(mover)
        if work is not None:
            self.live.update(work())
        landing = [m for m in self.moving if m in land]
        known = [m for m in self.moving if m.flight is None or m in landing]
        live, states = lax.optimization_barrier((self.live, [m.state(m in landing) for m in known]))
        self.live = live
        for mover, state in zip(known, states):
            mover.put(state, mover in landing)
        for mover in landing:
            mover.land()

    def step(self, work=None, movers=()):
        movers = [m for m in movers if m.plan]
        self.run(work, movers, movers)


def store_halves(me, first_rows, result, keep_ref, send_ref, at):
    low = result.astype(BF)
    for part in range(result.shape[0] // (2 * first_rows)):
        even = low[2 * part * first_rows: (2 * part + 1) * first_rows]
        odd = low[(2 * part + 1) * first_rows: (2 * part + 2) * first_rows]
        index = at(part)
        keep_ref[index] = jnp.where(me == 0, even, odd)
        send_ref[index] = jnp.where(me == 0, odd, even)


def unit_of(value):
    inverse = lax.rsqrt(jnp.mean(value * value, axis=-1, keepdims=True) + EPSILON)
    return value * inverse, inverse


def norm_back(grad_norm, value, gain):
    unit, inverse = unit_of(value)
    grad_gain = jnp.sum(grad_norm * unit, axis=0, keepdims=True)
    grad_unit = grad_norm * gain
    return inverse * (grad_unit - unit * jnp.mean(grad_unit * unit, axis=-1, keepdims=True)), grad_gain


def call(kernel, name, grid, ins, outs, flops, scratch=(), limit=VMEM_LIMIT):
    spec = lambda block, index: pl.BlockSpec(block, index) if index is not None else pl.BlockSpec(memory_space=block)
    size = lambda shape, kind: jnp.dtype(kind).itemsize * functools.reduce(lambda a, b: a * b, shape, 1)
    moved = sum(size(a.shape, a.dtype) for a, _, _ in ins) + sum(size(o[0], o[1]) for o in outs)
    return pl.pallas_call(
        kernel,
        grid=grid,
        in_specs=[spec(b, i) for _, b, i in ins],
        out_specs=[spec(b, i) for _, _, b, i in outs],
        out_shape=[jax.ShapeDtypeStruct(s, d) for s, d, _, _ in outs],
        scratch_shapes=list(scratch),
        compiler_params=pltpu.CompilerParams(vmem_limit_bytes=limit),
        cost_estimate=pl.CostEstimate(flops=flops, bytes_accessed=moved, transcendentals=0),
        name=name,
    )(*[a for a, _, _ in ins])


ROWS = 256
row_map = lambda i: (i, 0)
col_map = lambda i: (0, i)
whole = lambda i: (0, 0)
at_col = lambda c: (lambda i: (0, c))


def proj_self_kernel(x_ref, gain_ref, w_ref, nt_ref, qkv_ref):
    unit, _ = unit_of(x_ref[...].astype(F32))
    n = (unit * gain_ref[0:1, :]).astype(BF)
    nt_ref[...] = n.T
    qkv_ref[...] = dot(n, w_ref[...]).astype(BF)


def spans_dot(refs, w, dims):
    total, at = None, 0
    for ref in refs:
        columns = ref.shape[1]
        term = dot(ref[...], w[:, at: at + columns], dims)
        total = term if total is None else total + term
        at += columns
    return total


def mid_kernel(x_ref, e_ref, gain_ref, wo_ref, wc_ref, *refs):
    o_refs, (x2_ref, nt_ref, qc_ref, kv_ref, et_ref) = refs[:-5], refs[-5:]
    width = x_ref.shape[1]
    e = e_ref[...]
    et_ref[...] = e.T
    kv_ref[...] = dot(e, wc_ref[:, width: 3 * width]).astype(BF)
    x2 = x_ref[...].astype(F32) + spans_dot(o_refs, wo_ref, NT)
    x2_ref[...] = x2
    unit, _ = unit_of(x2)
    n = (unit * gain_ref[1:2, :]).astype(BF)
    nt_ref[...] = n.T
    qc_ref[...] = dot(n, wc_ref[:, :width]).astype(BF)


def third_kernel(x2_ref, g_ref, gain_ref, wo_ref, *refs):
    o_refs, (x3_ref, n_ref, nt_ref, gt_ref) = refs[:-4], refs[-4:]
    x3 = x2_ref[...] + spans_dot(o_refs, wo_ref, NT)
    x3_ref[...] = x3
    unit, _ = unit_of(x3)
    n = (unit * gain_ref[2:3, :]).astype(BF)
    n_ref[...] = n
    nt_ref[...] = n.T
    gt_ref[...] = g_ref[...].T


def ffn_kernel(n_ref, nt_ref, g_ref, gt_ref, win_ref, wout_ref, y_ref, dn_ref, dw_ref):
    w_in, w_out = win_ref[...], wout_ref[...]
    tokens = n_ref.shape[0]

    @pl.when(pl.program_id(0) == 0)
    def _():
        y_ref[...] = jnp.zeros_like(y_ref)
        dn_ref[...] = jnp.zeros_like(dn_ref)

    acts, grads = [], []
    for r in range(tokens // ROWS):
        rows = pl.ds(ROWS * r, ROWS)
        a = dot(n_ref[rows, :], w_in)
        back = dot(g_ref[rows, :], w_out)
        phi = 0.5 * (1.0 + lax.erf(a * ROOT_HALF))
        act = (a * phi).astype(BF)
        slope = phi + a * jnp.exp(-0.5 * a * a) * INV_ROOT_TWO_PI
        da = (back * slope).astype(BF)
        y_ref[rows, :] += dot(act, w_out, NT)
        dn_ref[rows, :] += dot(da, w_in, NT)
        acts.append(act)
        grads.append(da)
    tile = w_in.shape[1]
    dw_ref[:, :tile] = dot(nt_ref[...], jnp.concatenate(grads, axis=0)).astype(BF)
    dw_ref[:, tile:] = dot(gt_ref[...], jnp.concatenate(acts, axis=0)).astype(BF)


def top_kernel(y_ref, dn_ref, x3_ref, g_ref, gain_ref, wo_ref, out_ref, dx_ref, lowt_ref, doc_ref, gg_ref):
    x3 = x3_ref[...]
    out_ref[...] = (x3 + y_ref[...]).astype(BF)
    grad, grad_gain = norm_back(dn_ref[...], x3, gain_ref[2:3, :])
    dx = g_ref[...].astype(F32) + grad
    dx_ref[...] = dx
    low = dx.astype(BF)
    lowt_ref[...] = low.T
    doc_ref[...] = dot(low, wo_ref[...]).astype(BF)

    @pl.when(pl.program_id(0) == 0)
    def _():
        gg_ref[...] = jnp.zeros_like(gg_ref)

    gg_ref[0:1, :] += grad_gain


def second_kernel(x2_ref, dx3_ref, gain_ref, wq_ref, wo_ref, *refs):
    dq_refs, (dx_ref, lowt_ref, do_ref, gg_ref) = refs[:-4], refs[-4:]
    grad, grad_gain = norm_back(spans_dot(dq_refs, wq_ref, NT), x2_ref[...], gain_ref[1:2, :])
    dx = dx3_ref[...] + grad
    dx_ref[...] = dx
    low = dx.astype(BF)
    lowt_ref[...] = low.T
    do_ref[...] = dot(low, wo_ref[...]).astype(BF)

    @pl.when(pl.program_id(0) == 0)
    def _():
        gg_ref[...] = jnp.zeros_like(gg_ref)

    gg_ref[0:1, :] += grad_gain


def last_kernel(x_ref, dx2_ref, gain_ref, wq_ref, wk_ref, wv_ref, *refs):
    d_refs, (dx_ref, gg_ref) = refs[:-2], refs[-2:]
    n = len(d_refs) // 3
    dq, dk, dv = (d_refs[n * i: n * (i + 1)] for i in range(3))
    dn = spans_dot(dq, wq_ref, NT) + spans_dot(dk, wk_ref, NT) + spans_dot(dv, wv_ref, NT)
    grad, grad_gain = norm_back(dn, x_ref[...].astype(F32), gain_ref[0:1, :])
    dx_ref[...] = dx2_ref[...] + grad

    @pl.when(pl.program_id(0) == 0)
    def _():
        gg_ref[...] = jnp.zeros_like(gg_ref)

    gg_ref[0:1, :] += grad_gain


def encoder_kernel(ck_ref, cv_ref, *refs):
    n = len(refs) // 2
    refs[-1][...] = spans_dot(refs[:n], ck_ref, NT) + spans_dot(refs[n: 2 * n], cv_ref, NT)


def grads_kernel(first_rows, lefts, groups, me_ref, *refs):
    count = sum(groups)
    n_left = max(lefts) + 1
    left_refs, right_refs = refs[:n_left], refs[n_left: n_left + count]
    outs = refs[n_left + count: n_left + count + 2 * len(groups)]
    left_buf, right_buf, sems = refs[n_left + count + 2 * len(groups):]
    width = right_buf.shape[2]
    tile = 384 if width % 256 else 256

    def copies(p):
        found = [pltpu.make_async_copy(right_refs[p], right_buf.at[p % 2], sems.at[p % 2])]
        if p == 0 or lefts[p] != lefts[p - 1]:
            found.append(pltpu.make_async_copy(left_refs[lefts[p]], left_buf.at[lefts[p] % 2], sems.at[2 + lefts[p] % 2]))
        return found

    for copy in copies(0):
        copy.start()
    for p in range(count):
        if p + 1 < count:
            for copy in copies(p + 1):
                copy.start()
        for copy in copies(p):
            copy.wait()
        group = next(g for g in range(len(groups)) if p < sum(groups[: g + 1]))
        base = (p - sum(groups[:group])) * width
        keep_ref, send_ref = outs[2 * group], outs[2 * group + 1]
        for col in range(0, width, tile):
            result = dot(left_buf[lefts[p] % 2], right_buf[p % 2, :, col: col + tile])
            out = slice(base + col, base + col + tile)
            store_halves(me_ref[0], first_rows, result, keep_ref, send_ref, lambda part: (0, part, slice(None), out))


def weight_grads(name, lefts_arrays, lefts, rights, groups, half, first_rows):
    width = lefts_arrays[0].shape[0]
    tokens = rights[0].shape[0]
    columns = rights[0].shape[1]
    count = len(rights)
    shapes = [(1, width // (2 * first_rows), first_rows, n * columns) for n in groups for _ in range(2)]
    flops = 2 * width * tokens * columns * count
    return pl.pallas_call(
        functools.partial(grads_kernel, first_rows, lefts, groups),
        in_specs=[pl.BlockSpec(memory_space=pltpu.SMEM)] + [pl.BlockSpec(memory_space=pl.ANY)] * (len(lefts_arrays) + count),
        out_specs=[pl.BlockSpec(memory_space=pltpu.VMEM)] * len(shapes),
        out_shape=[jax.ShapeDtypeStruct(shape, BF) for shape in shapes],
        scratch_shapes=[pltpu.VMEM((2, width, tokens), BF), pltpu.VMEM((2, tokens, columns), BF), pltpu.SemaphoreType.DMA((4,))],
        compiler_params=pltpu.CompilerParams(vmem_limit_bytes=VMEM_LIMIT),
        cost_estimate=pl.CostEstimate(flops=flops, bytes_accessed=2 * tokens * columns * count * 2, transcendentals=0),
        name=name,
    )(half, *lefts_arrays, *rights)


SPANS = ((0, 3), (3, 3))


def body(sizes, inputs, encoder_out, segments, enc_segments, buckets, gains, rel_bias, self_q, self_kv, self_out, cross_q, cross_kv, cross_out, ffn_in, ffn_out, out_grad):
    wide, narrow = sizes
    micro, per, length, width = inputs.shape
    rows = micro * per
    tokens = rows * length
    hidden = ffn_in.shape[1]
    flat = lambda v: v.reshape(tokens, width)
    x, enc, grad_out = flat(inputs), flat(encoder_out), flat(out_grad)
    seg, enc_seg = segments.reshape(rows, length), enc_segments.reshape(rows, length)
    me = lax.axis_index(WIDE)

    outer_t = ffn_out.T
    gain_cols = jnp.pad(gains.T, ((0, 0), (0, 125)))
    shard_self = jnp.concatenate([self_q, self_kv[0], self_kv[1], gain_cols], axis=1)
    shard_cross = jnp.concatenate([cross_q, cross_kv[0], cross_kv[1], cross_out.T, self_out.T], axis=1)
    g_self = Gather(sizes, shard_self, (9 * 128, 10 * 128))
    g_cross = Gather(sizes, shard_cross, (15 * 128, 15 * 128))
    shard_ffn = jnp.concatenate([ffn_in, outer_t], axis=1)
    block_rows = self_q.shape[0] * narrow
    first = 1 << len(low_bits(wide, block_rows))
    first_rows = block_rows * first
    half = ((me // first) % 2).astype(jnp.int32).reshape(1)
    parts = width // (2 * first_rows)

    steps = (tokens // ROWS,)
    wide_f32 = lambda: ((tokens, width), F32, (ROWS, width), row_map)
    wide_low = lambda n=1: ((tokens, n * width), BF, (ROWS, n * width), row_map)
    turned = lambda: ((width, tokens), BF, (width, ROWS), col_map)
    gain_out = lambda: ((8, width), F32, (8, width), whole)
    rows_in = lambda v: (v, (ROWS, v.shape[1]), row_map)
    entire = lambda v: (v, v.shape, whole)
    piece = lambda slab, c: (slab, (width, width), at_col(c))
    unit = 2 * tokens * width * width

    r = Rounds()
    movers = [g_self, g_cross]
    r.moving = list(movers)
    r.live = {"x": x, "enc": enc, "g": grad_out}

    def prepare():
        return {"self_seg": segment_columns(seg, seg), "cross_seg": segment_columns(seg, enc_seg), "table": score_table(rel_bias, buckets)}

    def take_self():
        slab = g_self.whole()
        return {"slab_self": slab, "gain": slab[:, 3 * width: 3 * width + 3].T.astype(F32)}

    def proj():
        n1t, qkv = call(proj_self_kernel, "proj_self", steps, [rows_in(r["x"]), entire(r["gain"]), (r["slab_self"], (width, 3 * width), whole)], [turned(), wide_low(3)], 3 * unit)
        return {"n1t": n1t, "qkv": qkv}

    def fwd_self(i):
        o, p = attn_fwd(SPANS[i], r["qkv"], 0, r["qkv"], 6, r["qkv"], 12, *r["self_seg"], r["table"])
        return {f"o{i}": o, f"p{i}": p}

    def both(name):
        return [r[f"{name}{i}"] for i in range(len(SPANS))]

    def mid():
        out = call(mid_kernel, "mid", steps,
                   [rows_in(r["x"]), rows_in(r["enc"]), entire(r["gain"]), piece(r["slab_cross"], 4), (r["slab_cross"], (width, 3 * width), whole)] + [rows_in(o) for o in both("o")],
                   [wide_f32(), turned(), wide_low(), wide_low(2), turned()], 4 * unit)
        return dict(zip(("x2", "n2t", "qc", "kvc", "et"), out))

    def fwd_cross(i):
        o, p = attn_fwd(SPANS[i], r["qc"], 0, r["kvc"], 0, r["kvc"], 6, *r["cross_seg"])
        return {f"oc{i}": o, f"pc{i}": p}

    def third():
        out = call(third_kernel, "third", steps,
                   [rows_in(r["x2"]), rows_in(r["g"]), entire(r["gain"]), piece(r["slab_cross"], 3)] + [rows_in(o) for o in both("oc")],
                   [wide_f32(), wide_low(), turned(), turned()], unit)
        return dict(zip(("x3", "n3", "n3t", "gt"), out))

    tile = 512
    tiles = hidden // tile
    acc_out = ((tokens, width), F32, (tokens, width), whole)

    def ffn():
        slab = r["slab_ffn"]
        y, dn, dw = call(
            ffn_kernel, "ffn", (tiles,),
            [entire(r["n3"]), entire(r["n3t"]), entire(r["g"]), entire(r["gt"]),
             (slab, (width, tile), lambda j: (0, j)), (slab, (width, tile), lambda j: (0, tiles + j))],
            [acc_out, acc_out, ((width, 2 * hidden), BF, (width, 2 * tile), lambda j: (0, j))], 12 * tokens * width * hidden)
        return {"y": y, "dn": dn, "dw": dw}

    def top():
        out = call(top_kernel, "top", steps,
                   [rows_in(r["y"]), rows_in(r["dn"]), rows_in(r["x3"]), rows_in(r["g"]), entire(r["gain"]), piece(r["slab_cross"], 3)],
                   [wide_low(), wide_f32(), turned(), wide_low(), gain_out()], unit)
        return dict(zip(("layer", "dx3", "three_t", "doc", "gain3"), out))

    def bwd_cross(i):
        out = attn_bwd(SPANS[i], r["qc"], 0, r["kvc"], 0, r["kvc"], 6, r["doc"], r[f"oc{i}"], r[f"pc{i}"], False)
        return dict(zip((f"dqc{i}", f"dkc{i}", f"dvc{i}"), out))

    def second():
        out = call(second_kernel, "second", steps,
                   [rows_in(r["x2"]), rows_in(r["dx3"]), entire(r["gain"]), piece(r["slab_cross"], 0), piece(r["slab_cross"], 4)] + [rows_in(d) for d in both("dqc")],
                   [wide_f32(), turned(), wide_low(), gain_out()], 2 * unit)
        return dict(zip(("dx2", "two_t", "do", "gain2"), out))

    def grads_cross():
        rights = both("dqc") + both("dkc") + both("dvc") + both("oc") + both("o")
        n = len(SPANS)
        lefts = [r["n2t"], r["et"], r["three_t"], r["two_t"]]
        return {"cut_cross": weight_grads("grads_cross", lefts, (0,) * n + (1,) * (2 * n) + (2,) * n + (3,) * n, rights, (3 * n, 2 * n), half, first_rows)}

    def bwd_self(i):
        out = attn_bwd(SPANS[i], r["qkv"], 0, r["qkv"], 6, r["qkv"], 12, r["do"], r[f"o{i}"], r[f"p{i}"], True)
        return dict(zip((f"dq{i}", f"dk{i}", f"dv{i}", f"diag{i}"), out))

    def grads_self(i):
        return {f"cut_self{i}": weight_grads("grads_self", [r["n1t"]], (0, 0, 0), [r[f"dq{i}"], r[f"dk{i}"], r[f"dv{i}"]], (3,), half, first_rows)}

    def last():
        out = call(last_kernel, "last", steps,
                   [rows_in(r["x"]), rows_in(r["dx2"]), entire(r["gain"])] + [piece(r["slab_self"], c) for c in range(3)]
                   + [rows_in(d) for name in ("dq", "dk", "dv") for d in both(name)],
                   [wide_f32(), gain_out()], 3 * unit)
        return dict(zip(("dx1", "gain1"), out))

    def encoder():
        out = call(encoder_kernel, "encoder_grad", steps,
                   [piece(r["slab_cross"], c) for c in (1, 2)] + [rows_in(d) for name in ("dkc", "dvc") for d in both(name)],
                   [wide_f32()], 2 * unit)
        return {"de": out[0]}

    def cut(pair, turn):
        return Scatter(sizes, pair[0], pair[1], first, turn)

    r.step(prepare, [g_self])
    r.step(None, [g_self, g_cross])
    while g_self.plan:
        r.step(None, [g_self])
    g_self.groups, shard_ffn = lax.optimization_barrier((g_self.groups, shard_ffn))
    slab_ffn = lax.all_gather(shard_ffn, (WIDE, NARROW), axis=0, tiled=True)
    r.step(take_self, [])
    r.step(proj, [g_cross])
    r.step(lambda: fwd_self(0), [g_cross])
    r.step(lambda: fwd_self(1), [g_cross])
    while g_cross.plan:
        r.step(None, [g_cross])
    r.step(lambda: {"slab_cross": g_cross.whole()}, [])
    r.step(mid, [])
    r.step(lambda: fwd_cross(0), [])
    r.step(lambda: fwd_cross(1), [])
    r.step(third, [])
    r.moving = []
    r.live["slab_ffn"] = slab_ffn
    r.step(None, [])
    r.step(ffn, [])
    ffn_sum = lax.psum_scatter(r.live.pop("dw"), (WIDE, NARROW), scatter_dimension=0, tiled=True).astype(F32)
    ffn_sum = ffn_sum.reshape(-1, tiles, 2, tile)
    r.step(top, [])
    r.step(lambda: bwd_cross(0), [])
    r.step(lambda: bwd_cross(1), [])
    r.step(second, [])
    r.step(grads_cross, [])
    pairs = r.live.pop("cut_cross")
    sc, so = cut(pairs[:2], 0), cut(pairs[2:], 1)
    r.step(lambda: bwd_self(0), [sc, so])
    r.run(lambda: grads_self(0), [sc, so], [])
    s0 = cut(r.live.pop("cut_self0"), 1)
    r.run(lambda: bwd_self(1), [s0], [s0, sc, so])
    r.run(lambda: grads_self(1), [sc, so, s0], [])
    s1 = cut(r.live.pop("cut_self1"), 0)
    r.run(last, [s1], [s1, sc, so, s0])

    def small():
        diag = jnp.concatenate(both("diag"), axis=0)
        bias_rows = bucket_sums(diag, buckets, rel_bias.shape[0])
        return {"small": jnp.concatenate([r["gain1"][0], r["gain2"][0], r["gain3"][0], bias_rows.reshape(-1)]).reshape(-1, 128)}

    r.live.update(small())
    total = Total(sizes, r.live.pop("small"))
    movers = [sc, so, s0, s1, total]
    r.live["ffn_sum"] = ffn_sum
    r.step(encoder, movers)
    ffn_sum = r.live.pop("ffn_sum")
    while any(m.plan for m in movers):
        r.step(None, movers)

    summed = total.value.reshape(-1)
    shard = me * narrow + lax.axis_index(NARROW)
    own = width // (wide * narrow)
    gain_sum = lax.dynamic_slice_in_dim(summed[: 3 * width].reshape(3, width), shard * own, own, 1)
    bias_sum = summed[3 * width:].reshape(rel_bias.shape)

    def columns(sums, index, count):
        found = []
        for s in sums:
            n = s.keep.shape[-1] // count
            found.append(s.keep[0, :, n * index: n * (index + 1)])
        return jnp.concatenate(found, axis=1) if len(found) > 1 else found[0]

    shaped = lambda v: v.reshape(micro, per, length, width)
    selfs = [s0, s1]
    return (
        shaped(r["layer"]),
        shaped(r["dx1"]),
        shaped(r["de"]),
        gain_sum,
        bias_sum,
        columns(selfs, 0, 3),
        jnp.stack([columns(selfs, 1, 3), columns(selfs, 2, 3)]),
        columns([so], 1, 2).T,
        columns([sc], 0, 3),
        jnp.stack([columns([sc], 1, 3), columns([sc], 2, 3)]),
        columns([so], 0, 2).T,
        ffn_sum[:, :, 0].reshape(-1, hidden),
        ffn_sum[:, :, 1].reshape(-1, hidden).T,
    )


def solution(mesh):
    axes = (WIDE, NARROW)
    batch4, batch3 = P(None, axes, None, None), P(None, axes, None)
    first, second, middle = P(axes, None), P(None, axes), P(None, axes, None)
    sizes = (mesh.shape[WIDE], mesh.shape[NARROW])
    weights = (first, middle, second, first, middle, second, first, second)
    return jax.shard_map(
        functools.partial(body, sizes),
        mesh=mesh,
        in_specs=(batch4, batch4, batch3, batch3, P(), second, P()) + weights + (batch4,),
        out_specs=(batch4, batch4, batch4, second, P()) + weights,
        check_vma=False,
    )
```

```python
import functools
import jax
import jax.numpy as jnp
from jax import lax
from jax.sharding import PartitionSpec as P
from jax.experimental import pallas as pl
from jax.experimental.pallas import tpu as pltpu

DH = 64
NEGATIVE = -1e30
BF = jnp.bfloat16
F32 = jnp.float32
NN = (((1,), (0,)), ((), ()))
NT = (((1,), (1,)), ((), ()))
TN = (((0,), (0,)), ((), ()))
MB = 1 << 20


def dot(a, b, dims=NN):
    return lax.dot_general(a, b, dims, preferred_element_type=F32)


def segment_columns(query_seg, key_seg):
    ids = jnp.arange(128)
    other = (query_seg[..., None] != ids) & (ids < 4)
    query_cols = jnp.where(other, NEGATIVE, 0.0).astype(BF)
    key_cols = (key_seg[..., None] == ids).astype(BF)
    return query_cols, key_cols


def fold(values, combine):
    rows = [values[8 * i: 8 * (i + 1)] for i in range(values.shape[0] // 8)]
    while len(rows) > 1:
        rows = [combine(rows[2 * i], rows[2 * i + 1]) for i in range(len(rows) // 2)] + rows[len(rows) - len(rows) % 2:]
    return rows[0]


CHUNK = 128
LANES = 256


def attn_fwd_kernel(causal, q_ref, k_ref, v_ref, qs_ref, ks_ref, *rest):
    if causal:
        t_ref, o_ref, e_ref, inv_ref, s_buf, bias = rest
    else:
        o_ref, e_ref, inv_ref, s_buf = rest
    length = q_ref.shape[0]
    if causal:
        @pl.when(pl.program_id(1) == 0)
        def _():
            for h in range(2):
                for d in range(length // 128):
                    row = jnp.concatenate([t_ref[h, :, pl.ds(128 * (d + 1), 128)], t_ref[h, :, pl.ds(128 * d, 128)]], axis=1)
                    tile = pltpu.roll(jnp.broadcast_to(row, (128, 256)), 0, 1, stride=1, stride_axis=0)
                    bias[h, d] = tile[:, :128]
    lane = lax.broadcasted_iota(jnp.int32, (1, 128), 1)
    q = q_ref[...]
    keys = jnp.concatenate([k_ref[...], ks_ref[...]], axis=1)
    v_t = v_ref[...].T
    qa = [jnp.concatenate([jnp.where((lane // DH) == h, q, 0).astype(BF), qs_ref[...]], axis=1) for h in range(2)]
    work = [(h, c) for h in range(2) for c in range(length // LANES)]
    reach = lambda c: LANES * (c + 1) if causal else length

    def scores(i):
        h, c = work[i]
        s_buf[i % 2, :reach(c), :] = dot(keys[:reach(c)], qa[h][LANES * c: LANES * (c + 1)], NT)

    def place(h, c, kb):
        if not causal:
            return [(0, LANES, None)]
        found = []
        for qb in range(LANES // 128):
            d = qb + LANES // 128 * c - kb
            if d >= 0:
                found.append((128 * qb, 128, (h, d)))
        return found

    def load(i, kb, lo, width, tile):
        value = s_buf[i % 2, CHUNK * kb: CHUNK * (kb + 1), lo: lo + width]
        return value if tile is None else value + bias[tile[0], tile[1]]

    scores(0)
    for i, (h, c) in enumerate(work):
        if i + 1 < len(work):
            scores(i + 1)
        blocks = reach(c) // CHUNK
        tops = {}
        for kb in range(blocks):
            for lo, width, tile in place(h, c, kb):
                new = fold(load(i, kb, lo, width, tile), jnp.maximum)
                tops[lo] = new if lo not in tops else jnp.maximum(tops[lo], new)
        tops = {lo: jnp.max(t, axis=0, keepdims=True) for lo, t in tops.items()}
        sums = {}
        for kb in range(blocks):
            seen = place(h, c, kb)
            for lo, width, tile in seen:
                e = jnp.exp(load(i, kb, lo, width, tile) - tops[lo])
                new = fold(e, jnp.add)
                sums[lo] = new if lo not in sums else sums[lo] + new
                e_ref[h, CHUNK * kb: CHUNK * (kb + 1), LANES * c + lo: LANES * c + lo + width] = e.astype(BF)
            for lo in range(0, LANES, 128):
                if causal and lo not in [x[0] for x in seen]:
                    e_ref[h, CHUNK * kb: CHUNK * (kb + 1), LANES * c + lo: LANES * c + lo + 128] = jnp.zeros((CHUNK, 128), BF)
        total = jnp.concatenate([jnp.sum(sums[lo], axis=0, keepdims=True) for lo in sorted(sums)], axis=1)
        inv = 1.0 / total
        inv_ref[h, :, LANES * c: LANES * (c + 1)] = jnp.broadcast_to(inv, (8, LANES))
    parts = []
    for h in range(2):
        mine = v_t[DH * h: DH * (h + 1)]
        if causal:
            mixed = [dot(mine[:, :reach(c)], e_ref[h, :reach(c), LANES * c: LANES * (c + 1)]) for c in range(length // LANES)]
        else:
            mixed = [dot(mine, e_ref[h])]
        parts.append(jnp.concatenate(mixed, axis=1) * inv_ref[h, 0:1, :])
    o_ref[...] = jnp.concatenate(parts, axis=0).T.astype(BF)


def attn_fwd(span, q_arr, q_col, k_arr, k_col, v_arr, v_col, q_seg, k_seg, table=None):
    rows, length = q_seg.shape[:2]
    begin, pairs = span
    causal = table is not None
    block = lambda col: pl.BlockSpec((length, 128), lambda h, b: (b, begin + col + h))
    seg = pl.BlockSpec((None, length, 128), lambda h, b: (b, 0, 0))
    in_specs = [block(q_col), block(k_col), block(v_col), seg, seg]
    args = [q_arr, k_arr, v_arr, q_seg, k_seg]
    scratch = []
    if causal:
        in_specs.append(pl.BlockSpec((2, 1, table.shape[2]), lambda h, b: (begin + h, 0, 0)))
        args.append(table)
        scratch = [pltpu.VMEM((2, length // 128, 128, 128), F32)]
    scratch = [pltpu.VMEM((2, length, LANES), F32)] + scratch
    stat = pl.BlockSpec((None, 2, 8, length), lambda h, b: (b, h, 0, 0))
    return pl.pallas_call(
        functools.partial(attn_fwd_kernel, causal),
        grid=(pairs, rows),
        in_specs=in_specs,
        out_specs=[pl.BlockSpec((length, 128), lambda h, b: (b, h)), pl.BlockSpec((None, 2, length, length), lambda h, b: (b, h, 0, 0)), stat],
        out_shape=[jax.ShapeDtypeStruct((rows * length, pairs * 128), BF), jax.ShapeDtypeStruct((rows, 2 * pairs, length, length), BF), jax.ShapeDtypeStruct((rows, 2 * pairs, 8, length), F32)],
        scratch_shapes=scratch,
        compiler_params=pltpu.CompilerParams(vmem_limit_bytes=60 * MB),
        cost_estimate=pl.CostEstimate(flops=1, bytes_accessed=1, transcendentals=0),
        name="attn_fwd_self" if causal else "attn_fwd_cross",
    )(*args)


def attn_bwd_kernel(causal, q_ref, k_ref, v_ref, g_ref, o_ref, e_ref, inv_ref, *rest):
    if causal:
        dq_ref, dk_ref, dv_ref, diag_ref, ds_buf, acc = rest
    else:
        dq_ref, dk_ref, dv_ref, ds_buf = rest
    length = q_ref.shape[0]
    lane = lax.broadcasted_iota(jnp.int32, (1, 128), 1)
    q = q_ref[...]
    values = jnp.concatenate([v_ref[...], jnp.broadcast_to((lane < 2).astype(BF), (length, 128))], axis=1)
    k_t = k_ref[...].T
    g_t = g_ref[...].T.astype(F32)
    o_t = o_ref[...].T.astype(F32)
    if causal:
        @pl.when(pl.program_id(1) == 0)
        def _():
            acc[...] = jnp.zeros_like(acc)

        @pl.when((pl.program_id(0) == 0) & (pl.program_id(1) == 0))
        def _():
            ds_buf[...] = jnp.zeros_like(ds_buf)

    gms, qms, gas = [], [], []
    blank = jnp.zeros((DH, length), BF)
    for h in range(2):
        rows = slice(DH * h, DH * (h + 1))
        gm = (g_t[rows] * inv_ref[h, 0:1, :]).astype(BF)
        delta = -jnp.sum(gm.astype(F32) * o_t[rows], axis=0, keepdims=True)
        high = delta.astype(BF).astype(F32)
        extra = jnp.concatenate([high, delta - high, jnp.zeros((14, length), F32)], axis=0).astype(BF)
        gms.append(jnp.concatenate([blank] * h + [gm] + [blank] * (1 - h), axis=0))
        qms.append(jnp.where((lane // DH) == h, q, 0).astype(BF))
        gas.append(jnp.concatenate([gms[h], extra, jnp.zeros((112, length), BF)], axis=0))
    for h in range(2):
        for c in range(length // LANES):
            n = LANES * (c + 1) if causal else length
            span = slice(LANES * c, LANES * (c + 1))
            dp = dot(values[:n], gas[h][:, span])
            for kb in range(n // CHUNK):
                rows = slice(CHUNK * kb, CHUNK * (kb + 1))
                for qb in range(LANES // 128):
                    d = qb + LANES // 128 * c - kb
                    if causal and d < 0:
                        continue
                    cols = slice(LANES * c + 128 * qb, LANES * c + 128 * (qb + 1))
                    ds = (e_ref[h, rows, cols].astype(F32) * dp[rows, 128 * qb: 128 * (qb + 1)]).astype(BF)
                    ds_buf[h, rows, cols] = ds
                    if causal:
                        acc[h, d] += ds.astype(F32)
    for kb in range(length // LANES):
        rows = slice(LANES * kb, LANES * (kb + 1))
        lo = LANES * kb if causal else 0
        dk, dv = None, None
        for h in range(2):
            a = dot(ds_buf[h, rows, lo:], qms[h][lo:])
            b = dot(e_ref[h, rows, lo:], gms[h][:, lo:], NT)
            dk = a if dk is None else dk + a
            dv = b if dv is None else dv + b
        dk_ref[rows, :] = dk.astype(BF)
        dv_ref[rows, :] = dv.astype(BF)
    dq_ref[...] = jnp.concatenate([dot(k_t[DH * h: DH * (h + 1)], ds_buf[h]) for h in range(2)], axis=0).T.astype(BF)
    if causal:
        @pl.when(pl.program_id(1) == pl.num_programs(1) - 1)
        def _():
            flip = (lax.broadcasted_iota(jnp.int32, (128, 128), 0) + lax.broadcasted_iota(jnp.int32, (128, 128), 1) == 127).astype(F32)
            for h in range(2):
                for d in range(length // 128):
                    upside = jnp.dot(flip, acc[h, d], precision=lax.Precision.HIGHEST, preferred_element_type=F32)
                    wide = jnp.concatenate([upside, jnp.zeros((128, 128), F32)], axis=1)
                    turned = pltpu.roll(wide, 0, 1, stride=1, stride_axis=0)
                    diag_ref[h, pl.ds(d, 1), :] = jnp.sum(turned, axis=0, keepdims=True)


def attn_bwd(span, q_arr, q_col, k_arr, k_col, v_arr, v_col, grad, out, probs, inverse, causal):
    rows, heads, length = probs.shape[:3]
    begin, pairs = span
    block = lambda col: pl.BlockSpec((length, 128), lambda h, b: (b, begin + col + h))
    own = pl.BlockSpec((length, 128), lambda h, b: (b, h))
    flat = jax.ShapeDtypeStruct((rows * length, pairs * 128), BF)
    out_specs = [own] * 3
    out_shape = [flat] * 3
    scratch = [pltpu.VMEM((2, length, length), BF)]
    if causal:
        out_specs.append(pl.BlockSpec((2, length // 128, 256), lambda h, b: (h, 0, 0)))
        out_shape.append(jax.ShapeDtypeStruct((heads, length // 128, 256), F32))
        scratch.append(pltpu.VMEM((2, length // 128, 128, 128), F32))
    return pl.pallas_call(
        functools.partial(attn_bwd_kernel, causal),
        grid=(pairs, rows),
        in_specs=[block(q_col), block(k_col), block(v_col), block(0), own, pl.BlockSpec((None, 2, length, length), lambda h, b: (b, h, 0, 0)), pl.BlockSpec((None, 2, 8, length), lambda h, b: (b, h, 0, 0))],
        out_specs=out_specs,
        out_shape=out_shape,
        scratch_shapes=scratch,
        compiler_params=pltpu.CompilerParams(vmem_limit_bytes=60 * MB),
        cost_estimate=pl.CostEstimate(flops=1, bytes_accessed=1, transcendentals=0),
        name="attn_bwd_self" if causal else "attn_bwd_cross",
    )(q_arr, k_arr, v_arr, grad, out, probs, inverse)


def score_table(rel_bias, buckets):
    hot = buckets[:, None] == jnp.arange(rel_bias.shape[0])[None, :]
    at = jnp.sum(jnp.where(hot[:, :, None], rel_bias[None], 0.0), axis=1)
    return jnp.concatenate([jnp.full((rel_bias.shape[1], 128), NEGATIVE, F32), at.T], axis=1)[:, None]


def bucket_sums(diag, buckets, count):
    heads, blocks, _ = diag.shape
    own = diag[:, :, 127:255]
    before = jnp.pad(diag[:, 1:, :127], ((0, 0), (0, 1), (1, 0)))
    at = (own + before).reshape(heads, blocks * 128)
    hot = buckets[:, None] == jnp.arange(count)[None, :]
    return jnp.sum(jnp.where(hot[:, :, None], at.T[:, None, :], 0.0), axis=0)


EPSILON = 1e-06
ROOT_HALF = 0.7071067811865476
INV_ROOT_TWO_PI = 0.3989422804014327
WIDE, NARROW = "wide", "narrow"
VMEM_LIMIT = 60 * MB


def flipped(size, bit):
    return [(i, i ^ bit) for i in range(size)]


def bits_of(size):
    return [1 << i for i in range(size.bit_length() - 1)]


def merge(blocks, at):
    count = len(blocks)
    slots = []
    for j in range(count):
        slot = blocks[j]
        for k in range(count):
            if k != 0:
                slot = jnp.where((at ^ k) == 0, blocks[j ^ k], slot)
        slots.append(slot)
    return jnp.concatenate(slots, axis=0)


def low_bits(wide, rows):
    low = []
    for bit in bits_of(wide):
        if (rows * bit) % 16 == 0:
            break
        low.append(bit)
    return low


def cross_bits(wide, rows, turn):
    bits = [b for b in bits_of(wide) if b not in low_bits(wide, rows)]
    first, rest = bits[:1], bits[1:]
    turn = turn % max(len(rest), 1)
    return rest[turn:] + rest[:turn] + first


class Gather:
    def __init__(self, sizes, block, cuts):
        self.wide, self.narrow = sizes
        self.cuts = cuts
        self.groups = [[block]]
        self.flight = None
        rows = block.shape[0] * self.narrow
        self.low = low_bits(self.wide, rows)
        self.orders = [cross_bits(self.wide, rows, i) for i in range(len(cuts))]
        self.plan = ["narrow"] + [("low", b) for b in self.low] + list(range(len(self.orders[0])))

    def go(self):
        step = self.plan[0]
        if step == "narrow":
            self.flight = [[lax.ppermute(g[0], NARROW, flipped(self.narrow, k)) for k in range(1, self.narrow)] for g in self.groups]
        elif isinstance(step, tuple):
            self.flight = [[lax.ppermute(g[0], WIDE, flipped(self.wide, step[1]))] for g in self.groups]
        else:
            self.flight = [[lax.ppermute(p, WIDE, flipped(self.wide, self.orders[i][step])) for p in g] for i, g in enumerate(self.groups)]

    def land(self):
        step = self.plan.pop(0)
        joined = lambda at: [[merge(g + f, at)] for g, f in zip(self.groups, self.flight)]
        if step == "narrow":
            self.groups = joined(lax.axis_index(NARROW))
        elif isinstance(step, tuple):
            self.groups = joined((lax.axis_index(WIDE) // step[1]) % 2)
        else:
            self.groups = [g + f for g, f in zip(self.groups, self.flight)]
            if step == 0:
                self.groups = [[jnp.concatenate(g, axis=0)] for g in self.groups]
        if self.plan and self.plan[0] == 0:
            block = self.groups[0][0]
            ends = [sum(self.cuts[:i]) for i in range(len(self.cuts) + 1)]
            self.groups = [[block[:, ends[i]: ends[i + 1]]] for i in range(len(self.cuts))]
        self.flight = None

    def state(self, landing):
        return (self.groups, self.flight if landing else None)

    def put(self, state, landing):
        self.groups = state[0]
        if landing:
            self.flight = state[1]

    def whole(self):
        skip = 1 << len(self.low)
        offsets = []
        for order in self.orders:
            found = [0]
            for bit in order:
                found = found + [f ^ (bit // skip) for f in found]
            offsets.append(found)
        place = (lax.axis_index(WIDE) // skip).astype(jnp.int32).reshape(1)
        return assemble(self.groups, offsets, place)


def assemble_kernel(offsets, columns, counts, me_ref, *refs):
    pieces, out = list(refs[:-1]), refs[-1]
    for g in range(len(columns)):
        found = iter(offsets[g])
        for _ in range(counts[g]):
            piece = pieces.pop(0)
            width = piece.shape[1]
            rows = out.shape[0] // len(offsets[g])
            for k in range(piece.shape[0] // rows):
                start = pl.multiple_of((me_ref[0] ^ next(found)) * rows, 16)
                out[pl.ds(start, rows), columns[g]: columns[g] + width] = piece[rows * k: rows * (k + 1), :]


def assemble(groups, offsets, place):
    widths = [g[0].shape[1] for g in groups]
    columns = [sum(widths[:i]) for i in range(len(groups))]
    flat = [p for g in groups for p in g]
    rows = sum(p.shape[0] for p in groups[0])
    return pl.pallas_call(
        functools.partial(assemble_kernel, offsets, columns, [len(g) for g in groups]),
        in_specs=[pl.BlockSpec(memory_space=pltpu.SMEM)] + [pl.BlockSpec(memory_space=pltpu.VMEM)] * len(flat),
        out_specs=pl.BlockSpec(memory_space=pltpu.VMEM),
        out_shape=jax.ShapeDtypeStruct((rows, sum(widths)), BF),
        compiler_params=pltpu.CompilerParams(vmem_limit_bytes=VMEM_LIMIT),
        cost_estimate=pl.CostEstimate(flops=1, bytes_accessed=1, transcendentals=0),
        name="assemble",
    )(place, *flat)


class Scatter:
    def __init__(self, sizes, keep, send, first, turn):
        self.wide, self.narrow = sizes
        self.keep, self.sends = keep, [send]
        self.columns, self.lead = keep.shape[-1], keep.shape[0]
        self.left = [b for b in bits_of(self.wide) if b != first]
        high, low = [b for b in self.left if b > first], [b for b in self.left if b < first]
        turn = turn % max(len(high), 1)
        self.plan = [first] + high[turn:] + high[:turn] + low[::-1] + ["narrow"]
        self.flight = None

    def go(self):
        step = self.plan[0]
        if step == "narrow":
            self.flight = [lax.ppermute(s, NARROW, flipped(self.narrow, k + 1)) for k, s in enumerate(self.sends)]
        else:
            self.flight = [lax.ppermute(self.sends[0], WIDE, flipped(self.wide, step))]

    def land(self):
        self.plan.pop(0)
        value = self.keep.astype(F32)
        for received in self.flight:
            value = value + received.astype(F32)
        self.flight = None
        if not self.plan:
            self.keep, self.sends = value.reshape(self.lead, -1, self.columns), []
            return
        value = value.astype(BF)
        step = self.plan[0]
        if step == "narrow":
            value = value.reshape(self.lead, self.narrow, -1, self.columns)
            at = lax.axis_index(NARROW)
            pick = lambda k: lax.dynamic_slice_in_dim(value, at ^ k, 1, 1)[:, 0]
            self.keep, self.sends = pick(0), [pick(k) for k in range(1, self.narrow)]
        else:
            parts = self.lead << sum(b > step for b in self.left)
            self.left.remove(step)
            value = value.reshape(parts, 2, -1, self.columns)
            mine = (lax.axis_index(WIDE) // step) % 2
            pick = lambda k: lax.dynamic_slice_in_dim(value, k, 1, 1)[:, 0]
            self.keep, self.sends = pick(mine), [pick(1 - mine)]

    def join(self, other):
        side = lambda a, b: jnp.concatenate([a, b], axis=-1)
        self.keep, self.sends = side(self.keep, other.keep), [side(a, b) for a, b in zip(self.sends, other.sends)]
        self.columns += other.columns

    def state(self, landing):
        return (self.keep, self.sends, self.flight if landing else None)

    def put(self, state, landing):
        self.keep, self.sends = state[0], state[1]
        if landing:
            self.flight = state[2]


class Total:
    def __init__(self, sizes, value):
        self.value = value
        self.flight = None
        self.narrow = sizes[1]
        self.plan = [(sizes[0], bit) for bit in bits_of(sizes[0])] + ["narrow"]

    def go(self):
        if self.plan[0] == "narrow":
            self.flight = [lax.ppermute(self.value, NARROW, flipped(self.narrow, k)) for k in range(1, self.narrow)]
        else:
            self.flight = [lax.ppermute(self.value, WIDE, flipped(*self.plan[0]))]

    def land(self):
        if self.plan.pop(0) == "narrow":
            at = lax.axis_index(NARROW)
            parts = [self.value] + self.flight
            total = None
            for j in range(self.narrow):
                term = parts[0]
                for k in range(1, self.narrow):
                    term = jnp.where((at ^ k) == j, parts[k], term)
                total = term if total is None else total + term
            self.value = total
        else:
            self.value = self.value + self.flight[0]
        self.flight = None

    def state(self, landing):
        return (self.value, self.flight if landing else None)

    def put(self, state, landing):
        self.value = state[0]
        if landing:
            self.flight = state[1]


class Rounds:
    def __init__(self):
        self.live = {}
        self.moving = []

    def __getitem__(self, name):
        return self.live[name]

    def run(self, work=None, go=(), land=()):
        for mover in go:
            if mover not in self.moving:
                self.moving.append(mover)
            if mover.plan and mover.flight is None:
                mover.go()
        if work is not None:
            self.live.update(work())
        landing = [m for m in self.moving if m in land and m.flight is not None]
        known = [m for m in self.moving if m.flight is None or m in landing]
        live, states = lax.optimization_barrier((self.live, [m.state(m in landing) for m in known]))
        self.live = live
        for mover, state in zip(known, states):
            mover.put(state, mover in landing)
        for mover in landing:
            mover.land()

    def step(self, work=None, movers=()):
        movers = [m for m in movers if m.plan]
        self.run(work, movers, movers)


def store_halves(me, first_rows, result, keep_ref, send_ref, at):
    low = result.astype(BF)
    for part in range(result.shape[0] // (2 * first_rows)):
        even = low[2 * part * first_rows: (2 * part + 1) * first_rows]
        odd = low[(2 * part + 1) * first_rows: (2 * part + 2) * first_rows]
        index = at(part)
        keep_ref[index] = jnp.where(me == 0, even, odd)
        send_ref[index] = jnp.where(me == 0, odd, even)


def unit_of(value):
    inverse = lax.rsqrt(jnp.mean(value * value, axis=-1, keepdims=True) + EPSILON)
    return value * inverse, inverse


def norm_back(grad_norm, value, gain):
    unit, inverse = unit_of(value)
    grad_gain = jnp.sum(grad_norm * unit, axis=0, keepdims=True)
    grad_unit = grad_norm * gain
    return inverse * (grad_unit - unit * jnp.mean(grad_unit * unit, axis=-1, keepdims=True)), grad_gain


def call(kernel, name, grid, ins, outs, flops, scratch=(), limit=VMEM_LIMIT):
    spec = lambda block, index: pl.BlockSpec(block, index) if index is not None else pl.BlockSpec(memory_space=block)
    size = lambda shape, kind: jnp.dtype(kind).itemsize * functools.reduce(lambda a, b: a * b, shape, 1)
    moved = sum(size(a.shape, a.dtype) for a, _, _ in ins) + sum(size(o[0], o[1]) for o in outs)
    return pl.pallas_call(
        kernel,
        grid=grid,
        in_specs=[spec(b, i) for _, b, i in ins],
        out_specs=[spec(b, i) for _, _, b, i in outs],
        out_shape=[jax.ShapeDtypeStruct(s, d) for s, d, _, _ in outs],
        scratch_shapes=list(scratch),
        compiler_params=pltpu.CompilerParams(vmem_limit_bytes=limit),
        cost_estimate=pl.CostEstimate(flops=1, bytes_accessed=1, transcendentals=0),
        name=name,
    )(*[a for a, _, _ in ins])


ROWS = 512
FFN_ROWS = 256
row_map = lambda i: (i, 0)
col_map = lambda i: (0, i)
whole = lambda i: (0, 0)
at_col = lambda c: (lambda i: (0, c))


def proj_self_kernel(x_ref, gain_ref, w_ref, nt_ref, qkv_ref):
    unit, _ = unit_of(x_ref[...].astype(F32))
    n = (unit * gain_ref[0:1, :]).astype(BF)
    nt_ref[...] = n.T
    qkv_ref[...] = dot(n, w_ref[...]).astype(BF)


def spans_dot(refs, w, dims):
    total, at = None, 0
    for ref in refs:
        columns = ref.shape[1]
        term = dot(ref[...], w[:, at: at + columns], dims)
        total = term if total is None else total + term
        at += columns
    return total


def mid_kernel(x_ref, e_ref, gain_ref, wo_ref, wc_ref, *refs):
    o_refs, (x2_ref, nt_ref, qc_ref, kv_ref, et_ref) = refs[:-5], refs[-5:]
    width = x_ref.shape[1]
    e = e_ref[...]
    et_ref[...] = e.T
    kv_ref[...] = dot(e, wc_ref[:, width: 3 * width]).astype(BF)
    x2 = x_ref[...].astype(F32) + spans_dot(o_refs, wo_ref, NT)
    x2_ref[...] = x2
    unit, _ = unit_of(x2)
    n = (unit * gain_ref[1:2, :]).astype(BF)
    nt_ref[...] = n.T
    qc_ref[...] = dot(n, wc_ref[:, :width]).astype(BF)


def third_kernel(x2_ref, g_ref, gain_ref, wo_ref, *refs):
    o_refs, (x3_ref, n_ref, nt_ref, gt_ref) = refs[:-4], refs[-4:]
    x3 = x2_ref[...] + spans_dot(o_refs, wo_ref, NT)
    x3_ref[...] = x3
    unit, _ = unit_of(x3)
    n = (unit * gain_ref[2:3, :]).astype(BF)
    n_ref[...] = n
    nt_ref[...] = n.T
    gt_ref[...] = g_ref[...].T


def ffn_kernel(n_ref, nt_ref, g_ref, gt_ref, win_ref, wout_ref, y_ref, dn_ref, dw_ref):
    w_in, w_out = win_ref[...], wout_ref[...]
    tokens = n_ref.shape[0]

    @pl.when(pl.program_id(0) == 0)
    def _():
        y_ref[...] = jnp.zeros_like(y_ref)
        dn_ref[...] = jnp.zeros_like(dn_ref)

    acts, grads = [], []
    for r in range(tokens // FFN_ROWS):
        rows = pl.ds(FFN_ROWS * r, FFN_ROWS)
        a = dot(n_ref[rows, :], w_in)
        back = dot(g_ref[rows, :], w_out)
        phi = 0.5 * (1.0 + lax.erf(a * ROOT_HALF))
        act = (a * phi).astype(BF)
        slope = phi + a * jnp.exp(-0.5 * a * a) * INV_ROOT_TWO_PI
        da = (back * slope).astype(BF)
        y_ref[rows, :] += dot(act, w_out, NT)
        dn_ref[rows, :] += dot(da, w_in, NT)
        acts.append(act)
        grads.append(da)
    tile = w_in.shape[1]
    dw_ref[:, :tile] = dot(nt_ref[...], jnp.concatenate(grads, axis=0)).astype(BF)
    dw_ref[:, tile:] = dot(gt_ref[...], jnp.concatenate(acts, axis=0)).astype(BF)


def top_kernel(y_ref, dn_ref, x3_ref, g_ref, gain_ref, wo_ref, out_ref, dx_ref, lowt_ref, doc_ref, gg_ref):
    x3 = x3_ref[...]
    out_ref[...] = (x3 + y_ref[...]).astype(BF)
    grad, grad_gain = norm_back(dn_ref[...], x3, gain_ref[2:3, :])
    dx = g_ref[...].astype(F32) + grad
    dx_ref[...] = dx
    low = dx.astype(BF)
    lowt_ref[...] = low.T
    doc_ref[...] = dot(low, wo_ref[...]).astype(BF)

    @pl.when(pl.program_id(0) == 0)
    def _():
        gg_ref[...] = jnp.zeros_like(gg_ref)

    gg_ref[0:1, :] += grad_gain


def second_kernel(x2_ref, dx3_ref, gain_ref, wq_ref, wo_ref, *refs):
    dq_refs, (dx_ref, lowt_ref, do_ref, gg_ref) = refs[:-4], refs[-4:]
    grad, grad_gain = norm_back(spans_dot(dq_refs, wq_ref, NT), x2_ref[...], gain_ref[1:2, :])
    dx = dx3_ref[...] + grad
    dx_ref[...] = dx
    low = dx.astype(BF)
    lowt_ref[...] = low.T
    do_ref[...] = dot(low, wo_ref[...]).astype(BF)

    @pl.when(pl.program_id(0) == 0)
    def _():
        gg_ref[...] = jnp.zeros_like(gg_ref)

    gg_ref[0:1, :] += grad_gain


def last_kernel(x_ref, dx2_ref, gain_ref, wq_ref, wk_ref, wv_ref, *refs):
    d_refs, (dx_ref, gg_ref) = refs[:-2], refs[-2:]
    n = len(d_refs) // 3
    dq, dk, dv = (d_refs[n * i: n * (i + 1)] for i in range(3))
    dn = spans_dot(dq, wq_ref, NT) + spans_dot(dk, wk_ref, NT) + spans_dot(dv, wv_ref, NT)
    grad, grad_gain = norm_back(dn, x_ref[...].astype(F32), gain_ref[0:1, :])
    dx_ref[...] = dx2_ref[...] + grad

    @pl.when(pl.program_id(0) == 0)
    def _():
        gg_ref[...] = jnp.zeros_like(gg_ref)

    gg_ref[0:1, :] += grad_gain


def encoder_kernel(ck_ref, cv_ref, *refs):
    n = len(refs) // 2
    refs[-1][...] = spans_dot(refs[:n], ck_ref, NT) + spans_dot(refs[n: 2 * n], cv_ref, NT)


def grads_kernel(first_rows, lefts, groups, me_ref, *refs):
    count = sum(groups)
    n_left = max(lefts) + 1
    left_refs, right_refs = refs[:n_left], refs[n_left: n_left + count]
    outs = refs[n_left + count: n_left + count + 2 * len(groups)]
    left_buf, right_buf, sems = refs[n_left + count + 2 * len(groups):]
    width = right_buf.shape[2]
    tile = 384 if width % 256 else 256

    def copies(p):
        found = [pltpu.make_async_copy(right_refs[p], right_buf.at[p % 2], sems.at[p % 2])]
        if p == 0 or lefts[p] != lefts[p - 1]:
            found.append(pltpu.make_async_copy(left_refs[lefts[p]], left_buf.at[lefts[p] % 2], sems.at[2 + lefts[p] % 2]))
        return found

    for copy in copies(0):
        copy.start()
    for p in range(count):
        if p + 1 < count:
            for copy in copies(p + 1):
                copy.start()
        for copy in copies(p):
            copy.wait()
        group = next(g for g in range(len(groups)) if p < sum(groups[: g + 1]))
        base = (p - sum(groups[:group])) * width
        keep_ref, send_ref = outs[2 * group], outs[2 * group + 1]
        for col in range(0, width, tile):
            result = dot(left_buf[lefts[p] % 2], right_buf[p % 2, :, col: col + tile])
            out = slice(base + col, base + col + tile)
            store_halves(me_ref[0], first_rows, result, keep_ref, send_ref, lambda part: (0, part, slice(None), out))


def weight_grads(name, lefts_arrays, lefts, rights, groups, half, first_rows):
    width = lefts_arrays[0].shape[0]
    tokens = rights[0].shape[0]
    columns = rights[0].shape[1]
    count = len(rights)
    shapes = [(1, width // (2 * first_rows), first_rows, n * columns) for n in groups for _ in range(2)]
    flops = 2 * width * tokens * columns * count
    return pl.pallas_call(
        functools.partial(grads_kernel, first_rows, lefts, groups),
        in_specs=[pl.BlockSpec(memory_space=pltpu.SMEM)] + [pl.BlockSpec(memory_space=pl.ANY)] * (len(lefts_arrays) + count),
        out_specs=[pl.BlockSpec(memory_space=pltpu.VMEM)] * len(shapes),
        out_shape=[jax.ShapeDtypeStruct(shape, BF) for shape in shapes],
        scratch_shapes=[pltpu.VMEM((2, width, tokens), BF), pltpu.VMEM((2, tokens, columns), BF), pltpu.SemaphoreType.DMA((4,))],
        compiler_params=pltpu.CompilerParams(vmem_limit_bytes=VMEM_LIMIT),
        cost_estimate=pl.CostEstimate(flops=1, bytes_accessed=1, transcendentals=0),
        name=name,
    )(half, *lefts_arrays, *rights)


SPANS = ((0, 3), (3, 3))


def body(sizes, inputs, encoder_out, segments, enc_segments, buckets, gains, rel_bias, self_q, self_kv, self_out, cross_q, cross_kv, cross_out, ffn_in, ffn_out, out_grad):
    wide, narrow = sizes
    micro, per, length, width = inputs.shape
    rows = micro * per
    tokens = rows * length
    hidden = ffn_in.shape[1]
    flat = lambda v: v.reshape(tokens, width)
    x, enc, grad_out = flat(inputs), flat(encoder_out), flat(out_grad)
    seg, enc_seg = segments.reshape(rows, length), enc_segments.reshape(rows, length)
    me = lax.axis_index(WIDE)

    outer_t = ffn_out.T
    gain_cols = jnp.pad(gains.T, ((0, 0), (0, 125)))
    shard_self = jnp.concatenate([self_q, self_kv[0], self_kv[1], gain_cols], axis=1)
    shard_cross = jnp.concatenate([cross_q, cross_kv[0], cross_kv[1], cross_out.T, self_out.T], axis=1)
    g_self = Gather(sizes, shard_self, (9 * 128, 10 * 128))
    g_cross = Gather(sizes, shard_cross, (15 * 128, 15 * 128))
    shard_ffn = jnp.concatenate([ffn_in, outer_t], axis=1)
    block_rows = self_q.shape[0] * narrow
    first = 1 << len(low_bits(wide, block_rows))
    first_rows = block_rows * first
    half = ((me // first) % 2).astype(jnp.int32).reshape(1)
    parts = width // (2 * first_rows)

    steps = (tokens // ROWS,)
    wide_f32 = lambda: ((tokens, width), F32, (ROWS, width), row_map)
    wide_low = lambda n=1: ((tokens, n * width), BF, (ROWS, n * width), row_map)
    turned = lambda: ((width, tokens), BF, (width, ROWS), col_map)
    gain_out = lambda: ((8, width), F32, (8, width), whole)
    rows_in = lambda v: (v, (ROWS, v.shape[1]), row_map)
    entire = lambda v: (v, v.shape, whole)
    piece = lambda slab, c: (slab, (width, width), at_col(c))
    unit = 2 * tokens * width * width

    r = Rounds()
    movers = [g_self, g_cross]
    r.moving = list(movers)
    r.live = {"x": x, "enc": enc, "g": grad_out}

    def prepare():
        return {"self_seg": segment_columns(seg, seg), "cross_seg": segment_columns(seg, enc_seg), "table": score_table(rel_bias, buckets)}

    def take_self():
        slab = g_self.whole()
        return {"slab_self": slab, "gain": slab[:, 3 * width: 3 * width + 3].T.astype(F32)}

    def proj():
        n1t, qkv = call(proj_self_kernel, "proj_self", steps, [rows_in(r["x"]), entire(r["gain"]), (r["slab_self"], (width, 3 * width), whole)], [turned(), wide_low(3)], 3 * unit)
        return {"n1t": n1t, "qkv": qkv}

    def fwd_self(i):
        o, p, s = attn_fwd(SPANS[i], r["qkv"], 0, r["qkv"], 6, r["qkv"], 12, *r["self_seg"], r["table"])
        return {f"o{i}": o, f"p{i}": p, f"s{i}": s}

    def both(name):
        return [r[f"{name}{i}"] for i in range(len(SPANS))]

    def mid():
        out = call(mid_kernel, "mid", steps,
                   [rows_in(r["x"]), rows_in(r["enc"]), entire(r["gain"]), piece(r["slab_cross"], 4), (r["slab_cross"], (width, 3 * width), whole)] + [rows_in(o) for o in both("o")],
                   [wide_f32(), turned(), wide_low(), wide_low(2), turned()], 4 * unit)
        return dict(zip(("x2", "n2t", "qc", "kvc", "et"), out))

    def fwd_cross(i):
        o, p, s = attn_fwd(SPANS[i], r["qc"], 0, r["kvc"], 0, r["kvc"], 6, *r["cross_seg"])
        return {f"oc{i}": o, f"pc{i}": p, f"sc{i}": s}

    def third():
        out = call(third_kernel, "third", steps,
                   [rows_in(r["x2"]), rows_in(r["g"]), entire(r["gain"]), piece(r["slab_cross"], 3)] + [rows_in(o) for o in both("oc")],
                   [wide_f32(), wide_low(), turned(), turned()], unit)
        return dict(zip(("x3", "n3", "n3t", "gt"), out))

    tile = 512
    tiles = hidden // tile
    acc_out = ((tokens, width), F32, (tokens, width), whole)

    def ffn():
        slab = r["slab_ffn"]
        y, dn, dw = call(
            ffn_kernel, "ffn", (tiles,),
            [entire(r["n3"]), entire(r["n3t"]), entire(r["g"]), entire(r["gt"]),
             (slab, (width, tile), lambda j: (0, j)), (slab, (width, tile), lambda j: (0, tiles + j))],
            [acc_out, acc_out, ((width, 2 * hidden), BF, (width, 2 * tile), lambda j: (0, j))], 12 * tokens * width * hidden)
        return {"y": y, "dn": dn, "dw": dw}

    def top():
        out = call(top_kernel, "top", steps,
                   [rows_in(r["y"]), rows_in(r["dn"]), rows_in(r["x3"]), rows_in(r["g"]), entire(r["gain"]), piece(r["slab_cross"], 3)],
                   [wide_low(), wide_f32(), turned(), wide_low(), gain_out()], unit)
        return dict(zip(("layer", "dx3", "three_t", "doc", "gain3"), out))

    def bwd_cross(i):
        out = attn_bwd(SPANS[i], r["qc"], 0, r["kvc"], 0, r["kvc"], 6, r["doc"], r[f"oc{i}"], r[f"pc{i}"], r[f"sc{i}"], False)
        return dict(zip((f"dqc{i}", f"dkc{i}", f"dvc{i}"), out))

    def second():
        out = call(second_kernel, "second", steps,
                   [rows_in(r["x2"]), rows_in(r["dx3"]), entire(r["gain"]), piece(r["slab_cross"], 0), piece(r["slab_cross"], 4)] + [rows_in(d) for d in both("dqc")],
                   [wide_f32(), turned(), wide_low(), gain_out()], 2 * unit)
        return dict(zip(("dx2", "two_t", "do", "gain2"), out))

    def grads_cross():
        rights = both("dqc") + both("dkc") + both("dvc")
        n = len(SPANS)
        return {"cut_cross": weight_grads("grads_cross", [r["n2t"], r["et"]], (0,) * n + (1,) * (2 * n), rights, (3 * n,), half, first_rows)}

    def grads_out():
        n = len(SPANS)
        return {"cut_out": weight_grads("grads_out", [r["three_t"], r["two_t"]], (0,) * n + (1,) * n, both("oc") + both("o"), (2 * n,), half, first_rows)}

    def bwd_self(i):
        out = attn_bwd(SPANS[i], r["qkv"], 0, r["qkv"], 6, r["qkv"], 12, r["do"], r[f"o{i}"], r[f"p{i}"], r[f"s{i}"], True)
        return dict(zip((f"dq{i}", f"dk{i}", f"dv{i}", f"diag{i}"), out))

    def grads_self(i):
        return {f"cut_self{i}": weight_grads("grads_self", [r["n1t"]], (0, 0, 0), [r[f"dq{i}"], r[f"dk{i}"], r[f"dv{i}"]], (3,), half, first_rows)}

    def last():
        out = call(last_kernel, "last", steps,
                   [rows_in(r["x"]), rows_in(r["dx2"]), entire(r["gain"])] + [piece(r["slab_self"], c) for c in range(3)]
                   + [rows_in(d) for name in ("dq", "dk", "dv") for d in both(name)],
                   [wide_f32(), gain_out()], 3 * unit)
        return dict(zip(("dx1", "gain1"), out))

    def encoder():
        out = call(encoder_kernel, "encoder_grad", steps,
                   [piece(r["slab_cross"], c) for c in (1, 2)] + [rows_in(d) for name in ("dkc", "dvc") for d in both(name)],
                   [wide_f32()], 2 * unit)
        return {"de": out[0]}

    def cut(pair, turn):
        return Scatter(sizes, pair[0], pair[1], first, turn)

    r.step(prepare, [g_self])
    r.run(None, [g_self, g_cross], [g_self])
    while len(g_self.plan) > 1:
        r.step(None, [g_self])
    r.run(None, [g_self], [g_self, g_cross])
    g_self.groups, shard_ffn = lax.optimization_barrier((g_self.groups, shard_ffn))
    slab_ffn = lax.all_gather(shard_ffn, (WIDE, NARROW), axis=0, tiled=True)
    r.run(take_self, [g_cross], [])
    r.run(proj, [], [g_cross])
    r.run(lambda: fwd_self(0), [g_cross], [])
    r.run(lambda: fwd_self(1), [], [g_cross])
    while g_cross.plan:
        r.step(None, [g_cross])
    r.step(lambda: {"slab_cross": g_cross.whole()}, [])
    r.step(mid, [])
    r.step(lambda: fwd_cross(0), [])
    r.step(lambda: fwd_cross(1), [])
    r.step(third, [])
    r.moving = []
    r.live["slab_ffn"] = slab_ffn
    r.step(None, [])
    r.step(ffn, [])
    ffn_sum = lax.psum_scatter(r.live.pop("dw"), (WIDE, NARROW), scatter_dimension=0, tiled=True).astype(F32)
    ffn_sum = ffn_sum.reshape(-1, tiles, 2, tile)
    r.step(top, [])
    r.step(lambda: bwd_cross(0), [])
    r.step(lambda: bwd_cross(1), [])
    r.step(grads_cross, [])
    sc = cut(r.live.pop("cut_cross"), 0)
    r.step(second, [sc])
    r.run(grads_out, [sc], [])
    so = cut(r.live.pop("cut_out"), 1)
    r.run(lambda: bwd_self(0), [so], [sc, so])
    r.run(lambda: grads_self(0), [sc, so], [])
    s0 = cut(r.live.pop("cut_self0"), 1)
    r.run(lambda: bwd_self(1), [s0], [s0, sc, so])
    r.run(lambda: grads_self(1), [so, s0], [so])
    while sc.plan != ["narrow"] or so.plan != ["narrow"]:
        r.step(None, [x for x in (sc, so) if x.plan != ["narrow"]])
    sc.join(so)
    r.moving.remove(so)
    s1 = cut(r.live.pop("cut_self1"), 0)
    r.live["ffn_sum"] = ffn_sum
    r.run(last, [s1, sc], [s1, sc, s0])
    ffn_sum = r.live.pop("ffn_sum")

    def small():
        diag = jnp.concatenate(both("diag"), axis=0)
        bias_rows = bucket_sums(diag, buckets, rel_bias.shape[0])
        return {"small": jnp.concatenate([r["gain1"][0], r["gain2"][0], r["gain3"][0], bias_rows.reshape(-1)]).reshape(-1, 128)}

    r.live.update(small())
    total = Total(sizes, r.live.pop("small"))
    movers = [x for x in (s0, s1) if x.plan != ["narrow"]] + [total]
    r.step(encoder, movers)
    while s0.plan != ["narrow"] or s1.plan != ["narrow"]:
        r.step(None, [x for x in (s0, s1) if x.plan != ["narrow"]] + [total])
    s0.join(s1)
    r.moving.remove(s1)
    movers = [sc, s0, total]
    while any(m.plan for m in movers):
        r.step(None, movers)

    summed = total.value.reshape(-1)
    shard = me * narrow + lax.axis_index(NARROW)
    own = width // (wide * narrow)
    gain_sum = lax.dynamic_slice_in_dim(summed[: 3 * width].reshape(3, width), shard * own, own, 1)
    bias_sum = summed[3 * width:].reshape(rel_bias.shape)

    own_rows = lambda value, at, n: value.keep[0, :, at: at + n]

    def self_part(index):
        found, at = [], 0
        for _, pairs in SPANS:
            n = 128 * pairs
            found.append(own_rows(s0, at + n * index, n))
            at += 3 * n
        return jnp.concatenate(found, axis=1)

    cross_part = lambda index: own_rows(sc, width * index, width)
    shaped = lambda v: v.reshape(micro, per, length, width)
    return (
        shaped(r["layer"]),
        shaped(r["dx1"]),
        shaped(r["de"]),
        gain_sum,
        bias_sum,
        self_part(0),
        jnp.stack([self_part(1), self_part(2)]),
        cross_part(4).T,
        cross_part(0),
        jnp.stack([cross_part(1), cross_part(2)]),
        cross_part(3).T,
        ffn_sum[:, :, 0].reshape(-1, hidden),
        ffn_sum[:, :, 1].reshape(-1, hidden).T,
    )


def solution(mesh):
    axes = (WIDE, NARROW)
    batch4, batch3 = P(None, axes, None, None), P(None, axes, None)
    first, second, middle = P(axes, None), P(None, axes), P(None, axes, None)
    sizes = (mesh.shape[WIDE], mesh.shape[NARROW])
    weights = (first, middle, second, first, middle, second, first, second)
    return jax.shard_map(
        functools.partial(body, sizes),
        mesh=mesh,
        in_specs=(batch4, batch4, batch3, batch3, P(), second, P()) + weights + (batch4,),
        out_specs=(batch4, batch4, batch4, second, P()) + weights,
        check_vma=False,
    )
```

```python
import functools
import jax
import jax.numpy as jnp
from jax import lax
from jax.sharding import PartitionSpec as P
from jax.experimental import pallas as pl
from jax.experimental.pallas import tpu as pltpu

DH = 64
NEGATIVE = -1e30
BF = jnp.bfloat16
F32 = jnp.float32
NN = (((1,), (0,)), ((), ()))
NT = (((1,), (1,)), ((), ()))
TN = (((0,), (0,)), ((), ()))
MB = 1 << 20


def dot(a, b, dims=NN):
    return lax.dot_general(a, b, dims, preferred_element_type=F32)


def segment_columns(query_seg, key_seg):
    ids = jnp.arange(128)
    other = (query_seg[..., None] != ids) & (ids < 4)
    query_cols = jnp.where(other, NEGATIVE, 0.0).astype(BF)
    key_cols = (key_seg[..., None] == ids).astype(BF)
    return query_cols, key_cols


def fold(values, combine):
    rows = [values[8 * i: 8 * (i + 1)] for i in range(values.shape[0] // 8)]
    while len(rows) > 1:
        rows = [combine(rows[2 * i], rows[2 * i + 1]) for i in range(len(rows) // 2)] + rows[len(rows) - len(rows) % 2:]
    return rows[0]


CHUNK = 128
LANES = 256


def attn_fwd_kernel(causal, q_ref, k_ref, v_ref, qs_ref, ks_ref, *rest):
    if causal:
        t_ref, o_ref, e_ref, inv_ref, s_buf, bias = rest
    else:
        o_ref, e_ref, inv_ref, s_buf = rest
    length = q_ref.shape[0]
    if causal:
        @pl.when(pl.program_id(1) == 0)
        def _():
            for h in range(2):
                for d in range(length // 128):
                    row = jnp.concatenate([t_ref[h, :, pl.ds(128 * (d + 1), 128)], t_ref[h, :, pl.ds(128 * d, 128)]], axis=1)
                    tile = pltpu.roll(jnp.broadcast_to(row, (128, 256)), 0, 1, stride=1, stride_axis=0)
                    bias[h, d] = tile[:, :128]
    lane = lax.broadcasted_iota(jnp.int32, (1, 128), 1)
    q = q_ref[...]
    keys = jnp.concatenate([k_ref[...], ks_ref[...]], axis=1)
    v_t = v_ref[...].T
    qa = [jnp.concatenate([jnp.where((lane // DH) == h, q, 0).astype(BF), qs_ref[...]], axis=1) for h in range(2)]
    work = [(h, c) for h in range(2) for c in range(length // LANES)]
    reach = lambda c: LANES * (c + 1) if causal else length

    def scores(i):
        h, c = work[i]
        s_buf[i % 2, :reach(c), :] = dot(keys[:reach(c)], qa[h][LANES * c: LANES * (c + 1)], NT)

    def place(h, c, kb):
        if not causal:
            return [(0, LANES, None)]
        found = []
        for qb in range(LANES // 128):
            d = qb + LANES // 128 * c - kb
            if d >= 0:
                found.append((128 * qb, 128, (h, d)))
        return found

    def load(i, kb, lo, width, tile):
        value = s_buf[i % 2, CHUNK * kb: CHUNK * (kb + 1), lo: lo + width]
        return value if tile is None else value + bias[tile[0], tile[1]]

    scores(0)
    for i, (h, c) in enumerate(work):
        if i + 1 < len(work):
            scores(i + 1)
        blocks = reach(c) // CHUNK
        tops = {}
        for kb in range(blocks):
            for lo, width, tile in place(h, c, kb):
                new = fold(load(i, kb, lo, width, tile), jnp.maximum)
                tops[lo] = new if lo not in tops else jnp.maximum(tops[lo], new)
        tops = {lo: jnp.max(t, axis=0, keepdims=True) for lo, t in tops.items()}
        sums = {}
        for kb in range(blocks):
            seen = place(h, c, kb)
            for lo, width, tile in seen:
                e = jnp.exp(load(i, kb, lo, width, tile) - tops[lo])
                new = fold(e, jnp.add)
                sums[lo] = new if lo not in sums else sums[lo] + new
                e_ref[h, CHUNK * kb: CHUNK * (kb + 1), LANES * c + lo: LANES * c + lo + width] = e.astype(BF)
            for lo in range(0, LANES, 128):
                if causal and lo not in [x[0] for x in seen]:
                    e_ref[h, CHUNK * kb: CHUNK * (kb + 1), LANES * c + lo: LANES * c + lo + 128] = jnp.zeros((CHUNK, 128), BF)
        total = jnp.concatenate([jnp.sum(sums[lo], axis=0, keepdims=True) for lo in sorted(sums)], axis=1)
        inv = 1.0 / total
        inv_ref[h, :, LANES * c: LANES * (c + 1)] = jnp.broadcast_to(inv, (8, LANES))
    parts = []
    for h in range(2):
        mine = v_t[DH * h: DH * (h + 1)]
        if causal:
            mixed = [dot(mine[:, :reach(c)], e_ref[h, :reach(c), LANES * c: LANES * (c + 1)]) for c in range(length // LANES)]
        else:
            mixed = [dot(mine, e_ref[h])]
        parts.append(jnp.concatenate(mixed, axis=1) * inv_ref[h, 0:1, :])
    o_ref[...] = jnp.concatenate(parts, axis=0).T.astype(BF)


def attn_fwd(span, q_arr, q_col, k_arr, k_col, v_arr, v_col, q_seg, k_seg, table=None):
    rows, length = q_seg.shape[:2]
    begin, pairs = span
    causal = table is not None
    block = lambda col: pl.BlockSpec((length, 128), lambda h, b: (b, begin + col + h))
    seg = pl.BlockSpec((None, length, 128), lambda h, b: (b, 0, 0))
    in_specs = [block(q_col), block(k_col), block(v_col), seg, seg]
    args = [q_arr, k_arr, v_arr, q_seg, k_seg]
    scratch = []
    if causal:
        in_specs.append(pl.BlockSpec((2, 1, table.shape[2]), lambda h, b: (begin + h, 0, 0)))
        args.append(table)
        scratch = [pltpu.VMEM((2, length // 128, 128, 128), F32)]
    scratch = [pltpu.VMEM((2, length, LANES), F32)] + scratch
    stat = pl.BlockSpec((None, 2, 8, length), lambda h, b: (b, h, 0, 0))
    return pl.pallas_call(
        functools.partial(attn_fwd_kernel, causal),
        grid=(pairs, rows),
        in_specs=in_specs,
        out_specs=[pl.BlockSpec((length, 128), lambda h, b: (b, h)), pl.BlockSpec((None, 2, length, length), lambda h, b: (b, h, 0, 0)), stat],
        out_shape=[jax.ShapeDtypeStruct((rows * length, pairs * 128), BF), jax.ShapeDtypeStruct((rows, 2 * pairs, length, length), BF), jax.ShapeDtypeStruct((rows, 2 * pairs, 8, length), F32)],
        scratch_shapes=scratch,
        compiler_params=pltpu.CompilerParams(vmem_limit_bytes=60 * MB),
        cost_estimate=pl.CostEstimate(flops=1, bytes_accessed=1, transcendentals=0),
        name="attn_fwd_self" if causal else "attn_fwd_cross",
    )(*args)


def attn_bwd_kernel(causal, q_ref, k_ref, v_ref, g_ref, o_ref, e_ref, inv_ref, *rest):
    if causal:
        dq_ref, dk_ref, dv_ref, diag_ref, ds_buf, acc = rest
    else:
        dq_ref, dk_ref, dv_ref, ds_buf = rest
    length = q_ref.shape[0]
    lane = lax.broadcasted_iota(jnp.int32, (1, 128), 1)
    q = q_ref[...]
    values = jnp.concatenate([v_ref[...], jnp.broadcast_to((lane < 2).astype(BF), (length, 128))], axis=1)
    k_t = k_ref[...].T
    g_t = g_ref[...].T.astype(F32)
    o_t = o_ref[...].T.astype(F32)
    if causal:
        @pl.when(pl.program_id(1) == 0)
        def _():
            acc[...] = jnp.zeros_like(acc)

        @pl.when((pl.program_id(0) == 0) & (pl.program_id(1) == 0))
        def _():
            ds_buf[...] = jnp.zeros_like(ds_buf)

    gms, qms, gas = [], [], []
    blank = jnp.zeros((DH, length), BF)
    for h in range(2):
        rows = slice(DH * h, DH * (h + 1))
        gm = (g_t[rows] * inv_ref[h, 0:1, :]).astype(BF)
        delta = -jnp.sum(gm.astype(F32) * o_t[rows], axis=0, keepdims=True)
        high = delta.astype(BF).astype(F32)
        extra = jnp.concatenate([high, delta - high, jnp.zeros((14, length), F32)], axis=0).astype(BF)
        gms.append(jnp.concatenate([blank] * h + [gm] + [blank] * (1 - h), axis=0))
        qms.append(jnp.where((lane // DH) == h, q, 0).astype(BF))
        gas.append(jnp.concatenate([gms[h], extra, jnp.zeros((112, length), BF)], axis=0))
    for h in range(2):
        for c in range(length // LANES):
            n = LANES * (c + 1) if causal else length
            span = slice(LANES * c, LANES * (c + 1))
            dp = dot(values[:n], gas[h][:, span])
            for kb in range(n // CHUNK):
                rows = slice(CHUNK * kb, CHUNK * (kb + 1))
                for qb in range(LANES // 128):
                    d = qb + LANES // 128 * c - kb
                    if causal and d < 0:
                        continue
                    cols = slice(LANES * c + 128 * qb, LANES * c + 128 * (qb + 1))
                    ds = (e_ref[h, rows, cols].astype(F32) * dp[rows, 128 * qb: 128 * (qb + 1)]).astype(BF)
                    ds_buf[h, rows, cols] = ds
                    if causal:
                        acc[h, d] += ds.astype(F32)
    for kb in range(length // LANES):
        rows = slice(LANES * kb, LANES * (kb + 1))
        lo = LANES * kb if causal else 0
        dk, dv = None, None
        for h in range(2):
            a = dot(ds_buf[h, rows, lo:], qms[h][lo:])
            b = dot(e_ref[h, rows, lo:], gms[h][:, lo:], NT)
            dk = a if dk is None else dk + a
            dv = b if dv is None else dv + b
        dk_ref[rows, :] = dk.astype(BF)
        dv_ref[rows, :] = dv.astype(BF)
    dq_ref[...] = jnp.concatenate([dot(k_t[DH * h: DH * (h + 1)], ds_buf[h]) for h in range(2)], axis=0).T.astype(BF)
    if causal:
        @pl.when(pl.program_id(1) == pl.num_programs(1) - 1)
        def _():
            flip = (lax.broadcasted_iota(jnp.int32, (128, 128), 0) + lax.broadcasted_iota(jnp.int32, (128, 128), 1) == 127).astype(F32)
            for h in range(2):
                for d in range(length // 128):
                    upside = jnp.dot(flip, acc[h, d], precision=lax.Precision.HIGHEST, preferred_element_type=F32)
                    wide = jnp.concatenate([upside, jnp.zeros((128, 128), F32)], axis=1)
                    turned = pltpu.roll(wide, 0, 1, stride=1, stride_axis=0)
                    diag_ref[h, pl.ds(d, 1), :] = jnp.sum(turned, axis=0, keepdims=True)


def attn_bwd(span, q_arr, q_col, k_arr, k_col, v_arr, v_col, grad, out, probs, inverse, causal):
    rows, heads, length = probs.shape[:3]
    begin, pairs = span
    block = lambda col: pl.BlockSpec((length, 128), lambda h, b: (b, begin + col + h))
    own = pl.BlockSpec((length, 128), lambda h, b: (b, h))
    flat = jax.ShapeDtypeStruct((rows * length, pairs * 128), BF)
    out_specs = [own] * 3
    out_shape = [flat] * 3
    scratch = [pltpu.VMEM((2, length, length), BF)]
    if causal:
        out_specs.append(pl.BlockSpec((2, length // 128, 256), lambda h, b: (h, 0, 0)))
        out_shape.append(jax.ShapeDtypeStruct((heads, length // 128, 256), F32))
        scratch.append(pltpu.VMEM((2, length // 128, 128, 128), F32))
    return pl.pallas_call(
        functools.partial(attn_bwd_kernel, causal),
        grid=(pairs, rows),
        in_specs=[block(q_col), block(k_col), block(v_col), block(0), own, pl.BlockSpec((None, 2, length, length), lambda h, b: (b, h, 0, 0)), pl.BlockSpec((None, 2, 8, length), lambda h, b: (b, h, 0, 0))],
        out_specs=out_specs,
        out_shape=out_shape,
        scratch_shapes=scratch,
        compiler_params=pltpu.CompilerParams(vmem_limit_bytes=60 * MB),
        cost_estimate=pl.CostEstimate(flops=1, bytes_accessed=1, transcendentals=0),
        name="attn_bwd_self" if causal else "attn_bwd_cross",
    )(q_arr, k_arr, v_arr, grad, out, probs, inverse)


def score_table(rel_bias, buckets):
    hot = buckets[:, None] == jnp.arange(rel_bias.shape[0])[None, :]
    at = jnp.sum(jnp.where(hot[:, :, None], rel_bias[None], 0.0), axis=1)
    return jnp.concatenate([jnp.full((rel_bias.shape[1], 128), NEGATIVE, F32), at.T], axis=1)[:, None]


def bucket_sums(diag, buckets, count):
    heads, blocks, _ = diag.shape
    own = diag[:, :, 127:255]
    before = jnp.pad(diag[:, 1:, :127], ((0, 0), (0, 1), (1, 0)))
    at = (own + before).reshape(heads, blocks * 128)
    hot = buckets[:, None] == jnp.arange(count)[None, :]
    return jnp.sum(jnp.where(hot[:, :, None], at.T[:, None, :], 0.0), axis=0)


EPSILON = 1e-06
ROOT_HALF = 0.7071067811865476
INV_ROOT_TWO_PI = 0.3989422804014327
WIDE, NARROW = "wide", "narrow"
VMEM_LIMIT = 60 * MB


def flipped(size, bit):
    return [(i, i ^ bit) for i in range(size)]


def bits_of(size):
    return [1 << i for i in range(size.bit_length() - 1)]


def merge(blocks, at):
    count = len(blocks)
    slots = []
    for j in range(count):
        slot = blocks[j]
        for k in range(count):
            if k != 0:
                slot = jnp.where((at ^ k) == 0, blocks[j ^ k], slot)
        slots.append(slot)
    return jnp.concatenate(slots, axis=0)


def low_bits(wide, rows):
    low = []
    for bit in bits_of(wide):
        if (rows * bit) % 16 == 0:
            break
        low.append(bit)
    return low


def cross_bits(wide, rows, turn):
    bits = [b for b in bits_of(wide) if b not in low_bits(wide, rows)]
    first, rest = bits[:1], bits[1:]
    turn = turn % max(len(rest), 1)
    return rest[turn:] + rest[:turn] + first


class Gather:
    def __init__(self, sizes, block, cuts):
        self.wide, self.narrow = sizes
        self.cuts = cuts
        self.groups = [[block]]
        self.flight = None
        rows = block.shape[0] * self.narrow
        self.low = low_bits(self.wide, rows)
        self.orders = [cross_bits(self.wide, rows, i) for i in range(len(cuts))]
        self.plan = ["narrow"] + [("low", b) for b in self.low] + list(range(len(self.orders[0])))

    def go(self):
        step = self.plan[0]
        if step == "narrow":
            self.flight = [[lax.ppermute(g[0], NARROW, flipped(self.narrow, k)) for k in range(1, self.narrow)] for g in self.groups]
        elif isinstance(step, tuple):
            self.flight = [[lax.ppermute(g[0], WIDE, flipped(self.wide, step[1]))] for g in self.groups]
        else:
            self.flight = [[lax.ppermute(p, WIDE, flipped(self.wide, self.orders[i][step])) for p in g] for i, g in enumerate(self.groups)]

    def land(self):
        step = self.plan.pop(0)
        joined = lambda at: [[merge(g + f, at)] for g, f in zip(self.groups, self.flight)]
        if step == "narrow":
            self.groups = joined(lax.axis_index(NARROW))
        elif isinstance(step, tuple):
            self.groups = joined((lax.axis_index(WIDE) // step[1]) % 2)
        else:
            self.groups = [g + f for g, f in zip(self.groups, self.flight)]
            if step == 0:
                self.groups = [[jnp.concatenate(g, axis=0)] for g in self.groups]
        if self.plan and self.plan[0] == 0:
            block = self.groups[0][0]
            ends = [sum(self.cuts[:i]) for i in range(len(self.cuts) + 1)]
            self.groups = [[block[:, ends[i]: ends[i + 1]]] for i in range(len(self.cuts))]
        self.flight = None

    def state(self, landing):
        return (self.groups, self.flight if landing else None)

    def put(self, state, landing):
        self.groups = state[0]
        if landing:
            self.flight = state[1]

    def whole(self):
        skip = 1 << len(self.low)
        offsets = []
        for order in self.orders:
            found = [0]
            for bit in order:
                found = found + [f ^ (bit // skip) for f in found]
            offsets.append(found)
        place = (lax.axis_index(WIDE) // skip).astype(jnp.int32).reshape(1)
        return assemble(self.groups, offsets, place)


def assemble_kernel(offsets, columns, counts, me_ref, *refs):
    pieces, out = list(refs[:-1]), refs[-1]
    for g in range(len(columns)):
        found = iter(offsets[g])
        for _ in range(counts[g]):
            piece = pieces.pop(0)
            width = piece.shape[1]
            rows = out.shape[0] // len(offsets[g])
            for k in range(piece.shape[0] // rows):
                start = pl.multiple_of((me_ref[0] ^ next(found)) * rows, 16)
                out[pl.ds(start, rows), columns[g]: columns[g] + width] = piece[rows * k: rows * (k + 1), :]


def assemble(groups, offsets, place):
    widths = [g[0].shape[1] for g in groups]
    columns = [sum(widths[:i]) for i in range(len(groups))]
    flat = [p for g in groups for p in g]
    rows = sum(p.shape[0] for p in groups[0])
    return pl.pallas_call(
        functools.partial(assemble_kernel, offsets, columns, [len(g) for g in groups]),
        in_specs=[pl.BlockSpec(memory_space=pltpu.SMEM)] + [pl.BlockSpec(memory_space=pltpu.VMEM)] * len(flat),
        out_specs=pl.BlockSpec(memory_space=pltpu.VMEM),
        out_shape=jax.ShapeDtypeStruct((rows, sum(widths)), BF),
        compiler_params=pltpu.CompilerParams(vmem_limit_bytes=VMEM_LIMIT),
        cost_estimate=pl.CostEstimate(flops=1, bytes_accessed=1, transcendentals=0),
        name="assemble",
    )(place, *flat)


class Scatter:
    def __init__(self, sizes, keep, send, first, turn, direct=False):
        self.wide, self.narrow = sizes
        self.first = first
        self.keep, self.sends = keep, [send]
        self.columns, self.lead = keep.shape[-1], keep.shape[0]
        self.left = [b for b in bits_of(self.wide) if b != first]
        high, low = [b for b in self.left if b > first], [b for b in self.left if b < first]
        turn = turn % max(len(high), 1)
        self.plan = [first] + (["high"] if direct else high[turn:] + high[:turn]) + low[::-1] + ["narrow"]
        self.flight = None

    def go(self):
        step = self.plan[0]
        if step == "narrow":
            self.flight = [lax.ppermute(s, NARROW, flipped(self.narrow, k + 1)) for k, s in enumerate(self.sends)]
        elif step == "high":
            self.flight = [lax.ppermute(s, WIDE, flipped(self.wide, 2 * self.first * (k + 1))) for k, s in enumerate(self.sends)]
        else:
            self.flight = [lax.ppermute(self.sends[0], WIDE, flipped(self.wide, step))]

    def land(self):
        self.plan.pop(0)
        value = self.keep.astype(F32)
        for received in self.flight:
            value = value + received.astype(F32)
        self.flight = None
        if not self.plan:
            self.keep, self.sends = value.reshape(self.lead, -1, self.columns), []
            return
        value = value.astype(BF)
        step = self.plan[0]
        if step == "narrow":
            value = value.reshape(self.lead, self.narrow, -1, self.columns)
            at = lax.axis_index(NARROW)
            pick = lambda k: lax.dynamic_slice_in_dim(value, at ^ k, 1, 1)[:, 0]
            self.keep, self.sends = pick(0), [pick(k) for k in range(1, self.narrow)]
        elif step == "high":
            count = self.wide // (2 * self.first)
            self.left = [b for b in self.left if b < self.first]
            value = value.reshape(self.lead, count, -1, self.columns)
            at = lax.axis_index(WIDE) // (2 * self.first)
            pick = lambda k: lax.dynamic_slice_in_dim(value, at ^ k, 1, 1)[:, 0]
            self.keep, self.sends = pick(0), [pick(k) for k in range(1, count)]
        else:
            parts = self.lead << sum(b > step for b in self.left)
            self.left.remove(step)
            value = value.reshape(parts, 2, -1, self.columns)
            mine = (lax.axis_index(WIDE) // step) % 2
            pick = lambda k: lax.dynamic_slice_in_dim(value, k, 1, 1)[:, 0]
            self.keep, self.sends = pick(mine), [pick(1 - mine)]

    def join(self, other):
        side = lambda a, b: jnp.concatenate([a, b], axis=-1)
        self.keep, self.sends = side(self.keep, other.keep), [side(a, b) for a, b in zip(self.sends, other.sends)]
        self.columns += other.columns

    def state(self, landing):
        return (self.keep, self.sends, self.flight if landing else None)

    def put(self, state, landing):
        self.keep, self.sends = state[0], state[1]
        if landing:
            self.flight = state[2]


class Total:
    def __init__(self, sizes, value):
        self.value = value
        self.flight = None
        self.narrow = sizes[1]
        self.plan = [(sizes[0], bit) for bit in bits_of(sizes[0])] + ["narrow"]

    def go(self):
        if self.plan[0] == "narrow":
            self.flight = [lax.ppermute(self.value, NARROW, flipped(self.narrow, k)) for k in range(1, self.narrow)]
        else:
            self.flight = [lax.ppermute(self.value, WIDE, flipped(*self.plan[0]))]

    def land(self):
        if self.plan.pop(0) == "narrow":
            at = lax.axis_index(NARROW)
            parts = [self.value] + self.flight
            total = None
            for j in range(self.narrow):
                term = parts[0]
                for k in range(1, self.narrow):
                    term = jnp.where((at ^ k) == j, parts[k], term)
                total = term if total is None else total + term
            self.value = total
        else:
            self.value = self.value + self.flight[0]
        self.flight = None

    def state(self, landing):
        return (self.value, self.flight if landing else None)

    def put(self, state, landing):
        self.value = state[0]
        if landing:
            self.flight = state[1]


class Rounds:
    def __init__(self):
        self.live = {}
        self.moving = []

    def __getitem__(self, name):
        return self.live[name]

    def run(self, work=None, go=(), land=()):
        for mover in go:
            if mover not in self.moving:
                self.moving.append(mover)
            if mover.plan and mover.flight is None:
                mover.go()
        if work is not None:
            self.live.update(work())
        landing = [m for m in self.moving if m in land and m.flight is not None]
        known = [m for m in self.moving if m.flight is None or m in landing]
        live, states = lax.optimization_barrier((self.live, [m.state(m in landing) for m in known]))
        self.live = live
        for mover, state in zip(known, states):
            mover.put(state, mover in landing)
        for mover in landing:
            mover.land()

    def step(self, work=None, movers=()):
        movers = [m for m in movers if m.plan]
        self.run(work, movers, movers)


def store_halves(me, first_rows, result, keep_ref, send_ref, at):
    low = result.astype(BF)
    for part in range(result.shape[0] // (2 * first_rows)):
        even = low[2 * part * first_rows: (2 * part + 1) * first_rows]
        odd = low[(2 * part + 1) * first_rows: (2 * part + 2) * first_rows]
        index = at(part)
        keep_ref[index] = jnp.where(me == 0, even, odd)
        send_ref[index] = jnp.where(me == 0, odd, even)


def unit_of(value):
    inverse = lax.rsqrt(jnp.mean(value * value, axis=-1, keepdims=True) + EPSILON)
    return value * inverse, inverse


def norm_back(grad_norm, value, gain):
    unit, inverse = unit_of(value)
    grad_gain = jnp.sum(grad_norm * unit, axis=0, keepdims=True)
    grad_unit = grad_norm * gain
    return inverse * (grad_unit - unit * jnp.mean(grad_unit * unit, axis=-1, keepdims=True)), grad_gain


def call(kernel, name, grid, ins, outs, flops, scratch=(), limit=VMEM_LIMIT):
    spec = lambda block, index: pl.BlockSpec(block, index) if index is not None else pl.BlockSpec(memory_space=block)
    size = lambda shape, kind: jnp.dtype(kind).itemsize * functools.reduce(lambda a, b: a * b, shape, 1)
    moved = sum(size(a.shape, a.dtype) for a, _, _ in ins) + sum(size(o[0], o[1]) for o in outs)
    return pl.pallas_call(
        kernel,
        grid=grid,
        in_specs=[spec(b, i) for _, b, i in ins],
        out_specs=[spec(b, i) for _, _, b, i in outs],
        out_shape=[jax.ShapeDtypeStruct(s, d) for s, d, _, _ in outs],
        scratch_shapes=list(scratch),
        compiler_params=pltpu.CompilerParams(vmem_limit_bytes=limit),
        cost_estimate=pl.CostEstimate(flops=1, bytes_accessed=1, transcendentals=0),
        name=name,
    )(*[a for a, _, _ in ins])


ROWS = 512
FFN_ROWS = 256
row_map = lambda i: (i, 0)
col_map = lambda i: (0, i)
whole = lambda i: (0, 0)
at_col = lambda c: (lambda i: (0, c))


def proj_self_kernel(x_ref, gain_ref, w_ref, nt_ref, qkv_ref):
    unit, _ = unit_of(x_ref[...].astype(F32))
    n = (unit * gain_ref[0:1, :]).astype(BF)
    nt_ref[...] = n.T
    qkv_ref[...] = dot(n, w_ref[...]).astype(BF)


def spans_dot(refs, w, dims):
    total, at = None, 0
    for ref in refs:
        columns = ref.shape[1]
        term = dot(ref[...], w[:, at: at + columns], dims)
        total = term if total is None else total + term
        at += columns
    return total


def mid_kernel(x_ref, e_ref, gain_ref, wo_ref, wc_ref, *refs):
    o_refs, (x2_ref, nt_ref, qc_ref, kv_ref, et_ref) = refs[:-5], refs[-5:]
    width = x_ref.shape[1]
    e = e_ref[...]
    et_ref[...] = e.T
    kv_ref[...] = dot(e, wc_ref[:, width: 3 * width]).astype(BF)
    x2 = x_ref[...].astype(F32) + spans_dot(o_refs, wo_ref, NT)
    x2_ref[...] = x2
    unit, _ = unit_of(x2)
    n = (unit * gain_ref[1:2, :]).astype(BF)
    nt_ref[...] = n.T
    qc_ref[...] = dot(n, wc_ref[:, :width]).astype(BF)


def third_kernel(x2_ref, g_ref, gain_ref, wo_ref, *refs):
    o_refs, (x3_ref, n_ref, nt_ref, gt_ref) = refs[:-4], refs[-4:]
    x3 = x2_ref[...] + spans_dot(o_refs, wo_ref, NT)
    x3_ref[...] = x3
    unit, _ = unit_of(x3)
    n = (unit * gain_ref[2:3, :]).astype(BF)
    n_ref[...] = n
    nt_ref[...] = n.T
    gt_ref[...] = g_ref[...].T


def ffn_kernel(n_ref, nt_ref, g_ref, gt_ref, win_ref, wout_ref, y_ref, dn_ref, dw_ref):
    w_in, w_out = win_ref[...], wout_ref[...]
    tokens = n_ref.shape[0]

    @pl.when(pl.program_id(0) == 0)
    def _():
        y_ref[...] = jnp.zeros_like(y_ref)
        dn_ref[...] = jnp.zeros_like(dn_ref)

    acts, grads = [], []
    for r in range(tokens // FFN_ROWS):
        rows = pl.ds(FFN_ROWS * r, FFN_ROWS)
        a = dot(n_ref[rows, :], w_in)
        back = dot(g_ref[rows, :], w_out)
        phi = 0.5 * (1.0 + lax.erf(a * ROOT_HALF))
        act = (a * phi).astype(BF)
        slope = phi + a * jnp.exp(-0.5 * a * a) * INV_ROOT_TWO_PI
        da = (back * slope).astype(BF)
        y_ref[rows, :] += dot(act, w_out, NT)
        dn_ref[rows, :] += dot(da, w_in, NT)
        acts.append(act)
        grads.append(da)
    tile = w_in.shape[1]
    dw_ref[:, :tile] = dot(nt_ref[...], jnp.concatenate(grads, axis=0)).astype(BF)
    dw_ref[:, tile:] = dot(gt_ref[...], jnp.concatenate(acts, axis=0)).astype(BF)


def top_kernel(y_ref, dn_ref, x3_ref, g_ref, gain_ref, wo_ref, out_ref, dx_ref, lowt_ref, doc_ref, gg_ref):
    x3 = x3_ref[...]
    out_ref[...] = (x3 + y_ref[...]).astype(BF)
    grad, grad_gain = norm_back(dn_ref[...], x3, gain_ref[2:3, :])
    dx = g_ref[...].astype(F32) + grad
    dx_ref[...] = dx
    low = dx.astype(BF)
    lowt_ref[...] = low.T
    doc_ref[...] = dot(low, wo_ref[...]).astype(BF)

    @pl.when(pl.program_id(0) == 0)
    def _():
        gg_ref[...] = jnp.zeros_like(gg_ref)

    gg_ref[0:1, :] += grad_gain


def second_kernel(x2_ref, dx3_ref, gain_ref, wq_ref, wo_ref, *refs):
    dq_refs, (dx_ref, lowt_ref, do_ref, gg_ref) = refs[:-4], refs[-4:]
    grad, grad_gain = norm_back(spans_dot(dq_refs, wq_ref, NT), x2_ref[...], gain_ref[1:2, :])
    dx = dx3_ref[...] + grad
    dx_ref[...] = dx
    low = dx.astype(BF)
    lowt_ref[...] = low.T
    do_ref[...] = dot(low, wo_ref[...]).astype(BF)

    @pl.when(pl.program_id(0) == 0)
    def _():
        gg_ref[...] = jnp.zeros_like(gg_ref)

    gg_ref[0:1, :] += grad_gain


def last_kernel(x_ref, dx2_ref, gain_ref, wq_ref, wk_ref, wv_ref, *refs):
    d_refs, (dx_ref, gg_ref) = refs[:-2], refs[-2:]
    n = len(d_refs) // 3
    dq, dk, dv = (d_refs[n * i: n * (i + 1)] for i in range(3))
    dn = spans_dot(dq, wq_ref, NT) + spans_dot(dk, wk_ref, NT) + spans_dot(dv, wv_ref, NT)
    grad, grad_gain = norm_back(dn, x_ref[...].astype(F32), gain_ref[0:1, :])
    dx_ref[...] = dx2_ref[...] + grad

    @pl.when(pl.program_id(0) == 0)
    def _():
        gg_ref[...] = jnp.zeros_like(gg_ref)

    gg_ref[0:1, :] += grad_gain


def encoder_kernel(ck_ref, cv_ref, *refs):
    n = len(refs) // 2
    refs[-1][...] = spans_dot(refs[:n], ck_ref, NT) + spans_dot(refs[n: 2 * n], cv_ref, NT)


def grads_kernel(first_rows, lefts, groups, me_ref, *refs):
    count = sum(groups)
    n_left = max(lefts) + 1
    left_refs, right_refs = refs[:n_left], refs[n_left: n_left + count]
    outs = refs[n_left + count: n_left + count + 2 * len(groups)]
    left_buf, right_buf, sems = refs[n_left + count + 2 * len(groups):]
    width = right_buf.shape[2]
    tile = 384 if width % 256 else 256

    def copies(p):
        found = [pltpu.make_async_copy(right_refs[p], right_buf.at[p % 2], sems.at[p % 2])]
        if p == 0 or lefts[p] != lefts[p - 1]:
            found.append(pltpu.make_async_copy(left_refs[lefts[p]], left_buf.at[lefts[p] % 2], sems.at[2 + lefts[p] % 2]))
        return found

    for copy in copies(0):
        copy.start()
    for p in range(count):
        if p + 1 < count:
            for copy in copies(p + 1):
                copy.start()
        for copy in copies(p):
            copy.wait()
        group = next(g for g in range(len(groups)) if p < sum(groups[: g + 1]))
        base = (p - sum(groups[:group])) * width
        keep_ref, send_ref = outs[2 * group], outs[2 * group + 1]
        for col in range(0, width, tile):
            result = dot(left_buf[lefts[p] % 2], right_buf[p % 2, :, col: col + tile])
            out = slice(base + col, base + col + tile)
            store_halves(me_ref[0], first_rows, result, keep_ref, send_ref, lambda part: (0, part, slice(None), out))


def weight_grads(name, lefts_arrays, lefts, rights, groups, half, first_rows):
    width = lefts_arrays[0].shape[0]
    tokens = rights[0].shape[0]
    columns = rights[0].shape[1]
    count = len(rights)
    shapes = [(1, width // (2 * first_rows), first_rows, n * columns) for n in groups for _ in range(2)]
    flops = 2 * width * tokens * columns * count
    return pl.pallas_call(
        functools.partial(grads_kernel, first_rows, lefts, groups),
        in_specs=[pl.BlockSpec(memory_space=pltpu.SMEM)] + [pl.BlockSpec(memory_space=pl.ANY)] * (len(lefts_arrays) + count),
        out_specs=[pl.BlockSpec(memory_space=pltpu.VMEM)] * len(shapes),
        out_shape=[jax.ShapeDtypeStruct(shape, BF) for shape in shapes],
        scratch_shapes=[pltpu.VMEM((2, width, tokens), BF), pltpu.VMEM((2, tokens, columns), BF), pltpu.SemaphoreType.DMA((4,))],
        compiler_params=pltpu.CompilerParams(vmem_limit_bytes=VMEM_LIMIT),
        cost_estimate=pl.CostEstimate(flops=1, bytes_accessed=1, transcendentals=0),
        name=name,
    )(half, *lefts_arrays, *rights)


SPANS = ((0, 3), (3, 3))


def body(sizes, inputs, encoder_out, segments, enc_segments, buckets, gains, rel_bias, self_q, self_kv, self_out, cross_q, cross_kv, cross_out, ffn_in, ffn_out, out_grad):
    wide, narrow = sizes
    micro, per, length, width = inputs.shape
    rows = micro * per
    tokens = rows * length
    hidden = ffn_in.shape[1]
    flat = lambda v: v.reshape(tokens, width)
    x, enc, grad_out = flat(inputs), flat(encoder_out), flat(out_grad)
    seg, enc_seg = segments.reshape(rows, length), enc_segments.reshape(rows, length)
    me = lax.axis_index(WIDE)

    outer_t = ffn_out.T
    gain_cols = jnp.pad(gains.T, ((0, 0), (0, 125)))
    shard_self = jnp.concatenate([self_q, self_kv[0], self_kv[1], gain_cols], axis=1)
    shard_cross = jnp.concatenate([cross_q, cross_kv[0], cross_kv[1], cross_out.T, self_out.T], axis=1)
    g_self = Gather(sizes, shard_self, (9 * 128, 10 * 128))
    g_cross = Gather(sizes, shard_cross, (15 * 128, 15 * 128))
    shard_ffn = jnp.concatenate([ffn_in, outer_t], axis=1)
    block_rows = self_q.shape[0] * narrow
    first = 1 << len(low_bits(wide, block_rows))
    first_rows = block_rows * first
    half = ((me // first) % 2).astype(jnp.int32).reshape(1)
    parts = width // (2 * first_rows)

    steps = (tokens // ROWS,)
    wide_f32 = lambda: ((tokens, width), F32, (ROWS, width), row_map)
    wide_low = lambda n=1: ((tokens, n * width), BF, (ROWS, n * width), row_map)
    turned = lambda: ((width, tokens), BF, (width, ROWS), col_map)
    gain_out = lambda: ((8, width), F32, (8, width), whole)
    rows_in = lambda v: (v, (ROWS, v.shape[1]), row_map)
    entire = lambda v: (v, v.shape, whole)
    piece = lambda slab, c: (slab, (width, width), at_col(c))
    unit = 2 * tokens * width * width

    r = Rounds()
    movers = [g_self, g_cross]
    r.moving = list(movers)
    r.live = {"x": x, "enc": enc, "g": grad_out}

    def prepare():
        return {"self_seg": segment_columns(seg, seg), "cross_seg": segment_columns(seg, enc_seg), "table": score_table(rel_bias, buckets)}

    def take_self():
        slab = g_self.whole()
        return {"slab_self": slab, "gain": slab[:, 3 * width: 3 * width + 3].T.astype(F32)}

    def proj():
        n1t, qkv = call(proj_self_kernel, "proj_self", steps, [rows_in(r["x"]), entire(r["gain"]), (r["slab_self"], (width, 3 * width), whole)], [turned(), wide_low(3)], 3 * unit)
        return {"n1t": n1t, "qkv": qkv}

    def fwd_self(i):
        o, p, s = attn_fwd(SPANS[i], r["qkv"], 0, r["qkv"], 6, r["qkv"], 12, *r["self_seg"], r["table"])
        return {f"o{i}": o, f"p{i}": p, f"s{i}": s}

    def both(name):
        return [r[f"{name}{i}"] for i in range(len(SPANS))]

    def mid():
        out = call(mid_kernel, "mid", steps,
                   [rows_in(r["x"]), rows_in(r["enc"]), entire(r["gain"]), piece(r["slab_cross"], 4), (r["slab_cross"], (width, 3 * width), whole)] + [rows_in(o) for o in both("o")],
                   [wide_f32(), turned(), wide_low(), wide_low(2), turned()], 4 * unit)
        return dict(zip(("x2", "n2t", "qc", "kvc", "et"), out))

    def fwd_cross(i):
        o, p, s = attn_fwd(SPANS[i], r["qc"], 0, r["kvc"], 0, r["kvc"], 6, *r["cross_seg"])
        return {f"oc{i}": o, f"pc{i}": p, f"sc{i}": s}

    def third():
        out = call(third_kernel, "third", steps,
                   [rows_in(r["x2"]), rows_in(r["g"]), entire(r["gain"]), piece(r["slab_cross"], 3)] + [rows_in(o) for o in both("oc")],
                   [wide_f32(), wide_low(), turned(), turned()], unit)
        return dict(zip(("x3", "n3", "n3t", "gt"), out))

    tile = 512
    tiles = hidden // tile
    acc_out = ((tokens, width), F32, (tokens, width), whole)

    def ffn():
        slab = r["slab_ffn"]
        y, dn, dw = call(
            ffn_kernel, "ffn", (tiles,),
            [entire(r["n3"]), entire(r["n3t"]), entire(r["g"]), entire(r["gt"]),
             (slab, (width, tile), lambda j: (0, j)), (slab, (width, tile), lambda j: (0, tiles + j))],
            [acc_out, acc_out, ((width, 2 * hidden), BF, (width, 2 * tile), lambda j: (0, j))], 12 * tokens * width * hidden)
        return {"y": y, "dn": dn, "dw": dw}

    def top():
        out = call(top_kernel, "top", steps,
                   [rows_in(r["y"]), rows_in(r["dn"]), rows_in(r["x3"]), rows_in(r["g"]), entire(r["gain"]), piece(r["slab_cross"], 3)],
                   [wide_low(), wide_f32(), turned(), wide_low(), gain_out()], unit)
        return dict(zip(("layer", "dx3", "three_t", "doc", "gain3"), out))

    def bwd_cross(i):
        out = attn_bwd(SPANS[i], r["qc"], 0, r["kvc"], 0, r["kvc"], 6, r["doc"], r[f"oc{i}"], r[f"pc{i}"], r[f"sc{i}"], False)
        return dict(zip((f"dqc{i}", f"dkc{i}", f"dvc{i}"), out))

    def second():
        out = call(second_kernel, "second", steps,
                   [rows_in(r["x2"]), rows_in(r["dx3"]), entire(r["gain"]), piece(r["slab_cross"], 0), piece(r["slab_cross"], 4)] + [rows_in(d) for d in both("dqc")],
                   [wide_f32(), turned(), wide_low(), gain_out()], 2 * unit)
        return dict(zip(("dx2", "two_t", "do", "gain2"), out))

    def grads_cross():
        rights = both("dqc") + both("dkc") + both("dvc")
        n = len(SPANS)
        return {"cut_cross": weight_grads("grads_cross", [r["n2t"], r["et"]], (0,) * n + (1,) * (2 * n), rights, (3 * n,), half, first_rows)}

    def grads_out():
        n = len(SPANS)
        return {"cut_out": weight_grads("grads_out", [r["three_t"], r["two_t"]], (0,) * n + (1,) * n, both("oc") + both("o"), (2 * n,), half, first_rows)}

    def bwd_self(i):
        out = attn_bwd(SPANS[i], r["qkv"], 0, r["qkv"], 6, r["qkv"], 12, r["do"], r[f"o{i}"], r[f"p{i}"], r[f"s{i}"], True)
        return dict(zip((f"dq{i}", f"dk{i}", f"dv{i}", f"diag{i}"), out))

    def grads_self(i):
        return {f"cut_self{i}": weight_grads("grads_self", [r["n1t"]], (0, 0, 0), [r[f"dq{i}"], r[f"dk{i}"], r[f"dv{i}"]], (3,), half, first_rows)}

    def last():
        out = call(last_kernel, "last", steps,
                   [rows_in(r["x"]), rows_in(r["dx2"]), entire(r["gain"])] + [piece(r["slab_self"], c) for c in range(3)]
                   + [rows_in(d) for name in ("dq", "dk", "dv") for d in both(name)],
                   [wide_f32(), gain_out()], 3 * unit)
        return dict(zip(("dx1", "gain1"), out))

    def encoder():
        out = call(encoder_kernel, "encoder_grad", steps,
                   [piece(r["slab_cross"], c) for c in (1, 2)] + [rows_in(d) for name in ("dkc", "dvc") for d in both(name)],
                   [wide_f32()], 2 * unit)
        return {"de": out[0]}

    def cut(pair, turn, direct=False):
        return Scatter(sizes, pair[0], pair[1], first, turn, direct)

    r.step(prepare, [g_self])
    r.run(None, [g_self, g_cross], [g_self])
    while len(g_self.plan) > 1:
        r.step(None, [g_self])
    r.run(None, [g_self], [g_self, g_cross])
    g_self.groups, shard_ffn = lax.optimization_barrier((g_self.groups, shard_ffn))
    slab_ffn = lax.all_gather(shard_ffn, (WIDE, NARROW), axis=0, tiled=True)
    r.run(take_self, [g_cross], [])
    r.run(proj, [], [g_cross])
    r.run(lambda: fwd_self(0), [g_cross], [])
    r.run(lambda: fwd_self(1), [], [g_cross])
    while g_cross.plan:
        r.step(None, [g_cross])
    r.step(lambda: {"slab_cross": g_cross.whole()}, [])
    r.step(mid, [])
    r.step(lambda: fwd_cross(0), [])
    r.step(lambda: fwd_cross(1), [])
    r.step(third, [])
    r.moving = []
    r.live["slab_ffn"] = slab_ffn
    r.step(None, [])
    r.step(ffn, [])
    ffn_sum = lax.psum_scatter(r.live.pop("dw"), (WIDE, NARROW), scatter_dimension=0, tiled=True).astype(F32)
    ffn_sum = ffn_sum.reshape(-1, tiles, 2, tile)
    r.step(top, [])
    r.step(lambda: bwd_cross(0), [])
    r.step(lambda: bwd_cross(1), [])
    r.step(grads_cross, [])
    sc = cut(r.live.pop("cut_cross"), 0)
    r.step(second, [sc])
    r.run(grads_out, [sc], [])
    so = cut(r.live.pop("cut_out"), 1)
    r.run(lambda: bwd_self(0), [so], [so])
    r.run(lambda: grads_self(0), [so], [sc])
    s0 = cut(r.live.pop("cut_self0"), 1, True)
    r.run(lambda: bwd_self(1), [sc, s0], [s0, sc, so])
    r.run(lambda: grads_self(1), [sc, so], [sc])
    s1 = cut(r.live.pop("cut_self1"), 0, True)
    r.run(last, [s0, s1], [s0, s1, so])

    def small():
        diag = jnp.concatenate(both("diag"), axis=0)
        bias_rows = bucket_sums(diag, buckets, rel_bias.shape[0])
        return {"small": jnp.concatenate([r["gain1"][0], r["gain2"][0], r["gain3"][0], bias_rows.reshape(-1)]).reshape(-1, 128)}

    r.live.update(small())
    total = Total(sizes, r.live.pop("small"))
    r.live["ffn_sum"] = ffn_sum
    r.step(encoder, [s1, total])
    ffn_sum = r.live.pop("ffn_sum")
    ends = [so, s0, s1]
    while any(s.plan != ["narrow"] for s in ends):
        r.step(None, [s for s in ends if s.plan != ["narrow"]])
    for other in (s0, s1):
        so.join(other)
        r.moving.remove(other)
    r.run(None, [so, total], [total])
    r.run(None, [total], [so, total])
    while any(s.plan for s in (sc, so, total)):
        r.step(None, [sc, so, total])

    summed = total.value.reshape(-1)
    shard = me * narrow + lax.axis_index(NARROW)
    own = width // (wide * narrow)
    gain_sum = lax.dynamic_slice_in_dim(summed[: 3 * width].reshape(3, width), shard * own, own, 1)
    bias_sum = summed[3 * width:].reshape(rel_bias.shape)

    own_rows = lambda value, at, n: value.keep[0, :, at: at + n]

    def self_part(index):
        found, at = [], 2 * width
        for _, pairs in SPANS:
            n = 128 * pairs
            found.append(own_rows(so, at + n * index, n))
            at += 3 * n
        return jnp.concatenate(found, axis=1)

    cross_part = lambda index: own_rows(sc, width * index, width)
    shaped = lambda v: v.reshape(micro, per, length, width)
    return (
        shaped(r["layer"]),
        shaped(r["dx1"]),
        shaped(r["de"]),
        gain_sum,
        bias_sum,
        self_part(0),
        jnp.stack([self_part(1), self_part(2)]),
        own_rows(so, width, width).T,
        cross_part(0),
        jnp.stack([cross_part(1), cross_part(2)]),
        own_rows(so, 0, width).T,
        ffn_sum[:, :, 0].reshape(-1, hidden),
        ffn_sum[:, :, 1].reshape(-1, hidden).T,
    )


def solution(mesh):
    axes = (WIDE, NARROW)
    batch4, batch3 = P(None, axes, None, None), P(None, axes, None)
    first, second, middle = P(axes, None), P(None, axes), P(None, axes, None)
    sizes = (mesh.shape[WIDE], mesh.shape[NARROW])
    weights = (first, middle, second, first, middle, second, first, second)
    return jax.shard_map(
        functools.partial(body, sizes),
        mesh=mesh,
        in_specs=(batch4, batch4, batch3, batch3, P(), second, P()) + weights + (batch4,),
        out_specs=(batch4, batch4, batch4, second, P()) + weights,
        check_vma=False,
    )
```

```python
import functools
import jax
import jax.numpy as jnp
from jax import lax
from jax.sharding import PartitionSpec as P
from jax.experimental import pallas as pl
from jax.experimental.pallas import tpu as pltpu

DH = 64
NEGATIVE = -1e30
BF = jnp.bfloat16
F32 = jnp.float32
NN = (((1,), (0,)), ((), ()))
NT = (((1,), (1,)), ((), ()))
TN = (((0,), (0,)), ((), ()))
MB = 1 << 20


def dot(a, b, dims=NN):
    return lax.dot_general(a, b, dims, preferred_element_type=F32)


def segment_columns(query_seg, key_seg):
    ids = jnp.arange(128)
    other = (query_seg[..., None] != ids) & (ids < 4)
    query_cols = jnp.where(other, NEGATIVE, 0.0).astype(BF)
    key_cols = (key_seg[..., None] == ids).astype(BF)
    return query_cols, key_cols


def fold(values, combine):
    rows = [values[8 * i: 8 * (i + 1)] for i in range(values.shape[0] // 8)]
    while len(rows) > 1:
        rows = [combine(rows[2 * i], rows[2 * i + 1]) for i in range(len(rows) // 2)] + rows[len(rows) - len(rows) % 2:]
    return rows[0]


CHUNK = 128
LANES = 256


def attn_fwd_kernel(causal, q_ref, k_ref, v_ref, qs_ref, ks_ref, *rest):
    if causal:
        t_ref, o_ref, e_ref, inv_ref, s_buf, bias = rest
    else:
        o_ref, e_ref, inv_ref, s_buf = rest
    length = q_ref.shape[0]
    if causal:
        @pl.when(pl.program_id(1) == 0)
        def _():
            for h in range(2):
                for d in range(length // 128):
                    row = jnp.concatenate([t_ref[h, :, pl.ds(128 * (d + 1), 128)], t_ref[h, :, pl.ds(128 * d, 128)]], axis=1)
                    tile = pltpu.roll(jnp.broadcast_to(row, (128, 256)), 0, 1, stride=1, stride_axis=0)
                    bias[h, d] = tile[:, :128]
    lane = lax.broadcasted_iota(jnp.int32, (1, 128), 1)
    q = q_ref[...]
    keys = jnp.concatenate([k_ref[...], ks_ref[...]], axis=1)
    v_t = v_ref[...].T
    qa = [jnp.concatenate([jnp.where((lane // DH) == h, q, 0).astype(BF), qs_ref[...]], axis=1) for h in range(2)]
    work = [(h, c) for h in range(2) for c in range(length // LANES)]
    reach = lambda c: LANES * (c + 1) if causal else length

    def scores(i):
        h, c = work[i]
        s_buf[i % 2, :reach(c), :] = dot(keys[:reach(c)], qa[h][LANES * c: LANES * (c + 1)], NT)

    def place(h, c, kb):
        if not causal:
            return [(0, LANES, None)]
        found = []
        for qb in range(LANES // 128):
            d = qb + LANES // 128 * c - kb
            if d >= 0:
                found.append((128 * qb, 128, (h, d)))
        return found

    def load(i, kb, lo, width, tile):
        value = s_buf[i % 2, CHUNK * kb: CHUNK * (kb + 1), lo: lo + width]
        return value if tile is None else value + bias[tile[0], tile[1]]

    scores(0)
    for i, (h, c) in enumerate(work):
        if i + 1 < len(work):
            scores(i + 1)
        blocks = reach(c) // CHUNK
        tops = {}
        for kb in range(blocks):
            for lo, width, tile in place(h, c, kb):
                new = fold(load(i, kb, lo, width, tile), jnp.maximum)
                tops[lo] = new if lo not in tops else jnp.maximum(tops[lo], new)
        tops = {lo: jnp.max(t, axis=0, keepdims=True) for lo, t in tops.items()}
        sums = {}
        for kb in range(blocks):
            seen = place(h, c, kb)
            for lo, width, tile in seen:
                e = jnp.exp(load(i, kb, lo, width, tile) - tops[lo])
                new = fold(e, jnp.add)
                sums[lo] = new if lo not in sums else sums[lo] + new
                e_ref[h, CHUNK * kb: CHUNK * (kb + 1), LANES * c + lo: LANES * c + lo + width] = e.astype(BF)
            for lo in range(0, LANES, 128):
                if causal and lo not in [x[0] for x in seen]:
                    e_ref[h, CHUNK * kb: CHUNK * (kb + 1), LANES * c + lo: LANES * c + lo + 128] = jnp.zeros((CHUNK, 128), BF)
        total = jnp.concatenate([jnp.sum(sums[lo], axis=0, keepdims=True) for lo in sorted(sums)], axis=1)
        inv = 1.0 / total
        inv_ref[h, :, LANES * c: LANES * (c + 1)] = jnp.broadcast_to(inv, (8, LANES))
    parts = []
    for h in range(2):
        mine = v_t[DH * h: DH * (h + 1)]
        if causal:
            mixed = [dot(mine[:, :reach(c)], e_ref[h, :reach(c), LANES * c: LANES * (c + 1)]) for c in range(length // LANES)]
        else:
            mixed = [dot(mine, e_ref[h])]
        parts.append(jnp.concatenate(mixed, axis=1) * inv_ref[h, 0:1, :])
    o_ref[...] = jnp.concatenate(parts, axis=0).T.astype(BF)


def attn_fwd(span, q_arr, q_col, k_arr, k_col, v_arr, v_col, q_seg, k_seg, table=None):
    rows, length = q_seg.shape[:2]
    begin, pairs = span
    causal = table is not None
    block = lambda col: pl.BlockSpec((length, 128), lambda h, b: (b, begin + col + h))
    seg = pl.BlockSpec((None, length, 128), lambda h, b: (b, 0, 0))
    in_specs = [block(q_col), block(k_col), block(v_col), seg, seg]
    args = [q_arr, k_arr, v_arr, q_seg, k_seg]
    scratch = []
    if causal:
        in_specs.append(pl.BlockSpec((2, 1, table.shape[2]), lambda h, b: (begin + h, 0, 0)))
        args.append(table)
        scratch = [pltpu.VMEM((2, length // 128, 128, 128), F32)]
    scratch = [pltpu.VMEM((2, length, LANES), F32)] + scratch
    stat = pl.BlockSpec((None, 2, 8, length), lambda h, b: (b, h, 0, 0))
    return pl.pallas_call(
        functools.partial(attn_fwd_kernel, causal),
        grid=(pairs, rows),
        in_specs=in_specs,
        out_specs=[pl.BlockSpec((length, 128), lambda h, b: (b, h)), pl.BlockSpec((None, 2, length, length), lambda h, b: (b, h, 0, 0)), stat],
        out_shape=[jax.ShapeDtypeStruct((rows * length, pairs * 128), BF), jax.ShapeDtypeStruct((rows, 2 * pairs, length, length), BF), jax.ShapeDtypeStruct((rows, 2 * pairs, 8, length), F32)],
        scratch_shapes=scratch,
        compiler_params=pltpu.CompilerParams(vmem_limit_bytes=60 * MB),
        cost_estimate=pl.CostEstimate(flops=1, bytes_accessed=1, transcendentals=0),
        name="attn_fwd_self" if causal else "attn_fwd_cross",
    )(*args)


def attn_bwd_kernel(causal, q_ref, k_ref, v_ref, g_ref, o_ref, e_ref, inv_ref, *rest):
    if causal:
        dq_ref, dk_ref, dv_ref, diag_ref, ds_buf, acc = rest
    else:
        dq_ref, dk_ref, dv_ref, ds_buf = rest
    length = q_ref.shape[0]
    lane = lax.broadcasted_iota(jnp.int32, (1, 128), 1)
    q = q_ref[...]
    values = jnp.concatenate([v_ref[...], jnp.broadcast_to((lane < 2).astype(BF), (length, 128))], axis=1)
    k_t = k_ref[...].T
    g_t = g_ref[...].T.astype(F32)
    o_t = o_ref[...].T.astype(F32)
    if causal:
        @pl.when(pl.program_id(1) == 0)
        def _():
            acc[...] = jnp.zeros_like(acc)

        @pl.when((pl.program_id(0) == 0) & (pl.program_id(1) == 0))
        def _():
            ds_buf[...] = jnp.zeros_like(ds_buf)

    gms, qms, gas = [], [], []
    blank = jnp.zeros((DH, length), BF)
    for h in range(2):
        rows = slice(DH * h, DH * (h + 1))
        gm = (g_t[rows] * inv_ref[h, 0:1, :]).astype(BF)
        delta = -jnp.sum(gm.astype(F32) * o_t[rows], axis=0, keepdims=True)
        high = delta.astype(BF).astype(F32)
        extra = jnp.concatenate([high, delta - high, jnp.zeros((14, length), F32)], axis=0).astype(BF)
        gms.append(jnp.concatenate([blank] * h + [gm] + [blank] * (1 - h), axis=0))
        qms.append(jnp.where((lane // DH) == h, q, 0).astype(BF))
        gas.append(jnp.concatenate([gms[h], extra, jnp.zeros((112, length), BF)], axis=0))
    for h in range(2):
        for c in range(length // LANES):
            n = LANES * (c + 1) if causal else length
            span = slice(LANES * c, LANES * (c + 1))
            dp = dot(values[:n], gas[h][:, span])
            for kb in range(n // CHUNK):
                rows = slice(CHUNK * kb, CHUNK * (kb + 1))
                for qb in range(LANES // 128):
                    d = qb + LANES // 128 * c - kb
                    if causal and d < 0:
                        continue
                    cols = slice(LANES * c + 128 * qb, LANES * c + 128 * (qb + 1))
                    ds = (e_ref[h, rows, cols].astype(F32) * dp[rows, 128 * qb: 128 * (qb + 1)]).astype(BF)
                    ds_buf[h, rows, cols] = ds
                    if causal:
                        acc[h, d] += ds.astype(F32)
    for kb in range(length // LANES):
        rows = slice(LANES * kb, LANES * (kb + 1))
        lo = LANES * kb if causal else 0
        dk, dv = None, None
        for h in range(2):
            a = dot(ds_buf[h, rows, lo:], qms[h][lo:])
            b = dot(e_ref[h, rows, lo:], gms[h][:, lo:], NT)
            dk = a if dk is None else dk + a
            dv = b if dv is None else dv + b
        dk_ref[rows, :] = dk.astype(BF)
        dv_ref[rows, :] = dv.astype(BF)
    dq_ref[...] = jnp.concatenate([dot(k_t[DH * h: DH * (h + 1)], ds_buf[h]) for h in range(2)], axis=0).T.astype(BF)
    if causal:
        @pl.when(pl.program_id(1) == pl.num_programs(1) - 1)
        def _():
            flip = (lax.broadcasted_iota(jnp.int32, (128, 128), 0) + lax.broadcasted_iota(jnp.int32, (128, 128), 1) == 127).astype(F32)
            for h in range(2):
                for d in range(length // 128):
                    upside = jnp.dot(flip, acc[h, d], precision=lax.Precision.HIGHEST, preferred_element_type=F32)
                    wide = jnp.concatenate([upside, jnp.zeros((128, 128), F32)], axis=1)
                    turned = pltpu.roll(wide, 0, 1, stride=1, stride_axis=0)
                    diag_ref[h, pl.ds(d, 1), :] = jnp.sum(turned, axis=0, keepdims=True)


def attn_bwd(span, q_arr, q_col, k_arr, k_col, v_arr, v_col, grad, out, probs, inverse, causal):
    rows, heads, length = probs.shape[:3]
    begin, pairs = span
    block = lambda col: pl.BlockSpec((length, 128), lambda h, b: (b, begin + col + h))
    own = pl.BlockSpec((length, 128), lambda h, b: (b, h))
    flat = jax.ShapeDtypeStruct((rows * length, pairs * 128), BF)
    out_specs = [own] * 3
    out_shape = [flat] * 3
    scratch = [pltpu.VMEM((2, length, length), BF)]
    if causal:
        out_specs.append(pl.BlockSpec((2, length // 128, 256), lambda h, b: (h, 0, 0)))
        out_shape.append(jax.ShapeDtypeStruct((heads, length // 128, 256), F32))
        scratch.append(pltpu.VMEM((2, length // 128, 128, 128), F32))
    return pl.pallas_call(
        functools.partial(attn_bwd_kernel, causal),
        grid=(pairs, rows),
        in_specs=[block(q_col), block(k_col), block(v_col), block(0), own, pl.BlockSpec((None, 2, length, length), lambda h, b: (b, h, 0, 0)), pl.BlockSpec((None, 2, 8, length), lambda h, b: (b, h, 0, 0))],
        out_specs=out_specs,
        out_shape=out_shape,
        scratch_shapes=scratch,
        compiler_params=pltpu.CompilerParams(vmem_limit_bytes=60 * MB),
        cost_estimate=pl.CostEstimate(flops=1, bytes_accessed=1, transcendentals=0),
        name="attn_bwd_self" if causal else "attn_bwd_cross",
    )(q_arr, k_arr, v_arr, grad, out, probs, inverse)


def score_table(rel_bias, buckets):
    hot = buckets[:, None] == jnp.arange(rel_bias.shape[0])[None, :]
    at = jnp.sum(jnp.where(hot[:, :, None], rel_bias[None], 0.0), axis=1)
    return jnp.concatenate([jnp.full((rel_bias.shape[1], 128), NEGATIVE, F32), at.T], axis=1)[:, None]


def bucket_sums(diag, buckets, count):
    heads, blocks, _ = diag.shape
    own = diag[:, :, 127:255]
    before = jnp.pad(diag[:, 1:, :127], ((0, 0), (0, 1), (1, 0)))
    at = (own + before).reshape(heads, blocks * 128)
    hot = buckets[:, None] == jnp.arange(count)[None, :]
    return jnp.sum(jnp.where(hot[:, :, None], at.T[:, None, :], 0.0), axis=0)


EPSILON = 1e-06
ROOT_HALF = 0.7071067811865476
INV_ROOT_TWO_PI = 0.3989422804014327
WIDE, NARROW = "wide", "narrow"
VMEM_LIMIT = 60 * MB


def flipped(size, bit):
    return [(i, i ^ bit) for i in range(size)]


def bits_of(size):
    return [1 << i for i in range(size.bit_length() - 1)]


def merge(blocks, at):
    count = len(blocks)
    slots = []
    for j in range(count):
        slot = blocks[j]
        for k in range(count):
            if k != 0:
                slot = jnp.where((at ^ k) == 0, blocks[j ^ k], slot)
        slots.append(slot)
    return jnp.concatenate(slots, axis=0)


def low_bits(wide, rows):
    low = []
    for bit in bits_of(wide):
        if (rows * bit) % 16 == 0:
            break
        low.append(bit)
    return low


def cross_bits(wide, rows, turn):
    bits = [b for b in bits_of(wide) if b not in low_bits(wide, rows)]
    first, rest = bits[:1], bits[1:]
    turn = turn % max(len(rest), 1)
    return rest[turn:] + rest[:turn] + first


class Gather:
    def __init__(self, sizes, block, cuts):
        self.wide, self.narrow = sizes
        self.cuts = cuts
        self.groups = [[block]]
        self.flight = None
        rows = block.shape[0] * self.narrow
        self.low = low_bits(self.wide, rows)
        self.orders = [cross_bits(self.wide, rows, i) for i in range(len(cuts))]
        self.plan = ["narrow"] + [("low", b) for b in self.low] + list(range(len(self.orders[0])))

    def go(self):
        step = self.plan[0]
        if step == "narrow":
            self.flight = [[lax.ppermute(g[0], NARROW, flipped(self.narrow, k)) for k in range(1, self.narrow)] for g in self.groups]
        elif isinstance(step, tuple):
            self.flight = [[lax.ppermute(g[0], WIDE, flipped(self.wide, step[1]))] for g in self.groups]
        else:
            self.flight = [[lax.ppermute(p, WIDE, flipped(self.wide, self.orders[i][step])) for p in g] for i, g in enumerate(self.groups)]

    def land(self):
        step = self.plan.pop(0)
        joined = lambda at: [[merge(g + f, at)] for g, f in zip(self.groups, self.flight)]
        if step == "narrow":
            self.groups = joined(lax.axis_index(NARROW))
        elif isinstance(step, tuple):
            self.groups = joined((lax.axis_index(WIDE) // step[1]) % 2)
        else:
            self.groups = [g + f for g, f in zip(self.groups, self.flight)]
            if step == 0:
                self.groups = [[jnp.concatenate(g, axis=0)] for g in self.groups]
        if self.plan and self.plan[0] == 0:
            block = self.groups[0][0]
            ends = [sum(self.cuts[:i]) for i in range(len(self.cuts) + 1)]
            self.groups = [[block[:, ends[i]: ends[i + 1]]] for i in range(len(self.cuts))]
        self.flight = None

    def state(self, landing):
        return (self.groups, self.flight if landing else None)

    def put(self, state, landing):
        self.groups = state[0]
        if landing:
            self.flight = state[1]

    def whole(self):
        skip = 1 << len(self.low)
        offsets = []
        for order in self.orders:
            found = [0]
            for bit in order:
                found = found + [f ^ (bit // skip) for f in found]
            offsets.append(found)
        place = (lax.axis_index(WIDE) // skip).astype(jnp.int32).reshape(1)
        return assemble(self.groups, offsets, place)


def assemble_kernel(offsets, columns, counts, me_ref, *refs):
    pieces, out = list(refs[:-1]), refs[-1]
    for g in range(len(columns)):
        found = iter(offsets[g])
        for _ in range(counts[g]):
            piece = pieces.pop(0)
            width = piece.shape[1]
            rows = out.shape[0] // len(offsets[g])
            for k in range(piece.shape[0] // rows):
                start = pl.multiple_of((me_ref[0] ^ next(found)) * rows, 16)
                out[pl.ds(start, rows), columns[g]: columns[g] + width] = piece[rows * k: rows * (k + 1), :]


def assemble(groups, offsets, place):
    widths = [g[0].shape[1] for g in groups]
    columns = [sum(widths[:i]) for i in range(len(groups))]
    flat = [p for g in groups for p in g]
    rows = sum(p.shape[0] for p in groups[0])
    return pl.pallas_call(
        functools.partial(assemble_kernel, offsets, columns, [len(g) for g in groups]),
        in_specs=[pl.BlockSpec(memory_space=pltpu.SMEM)] + [pl.BlockSpec(memory_space=pltpu.VMEM)] * len(flat),
        out_specs=pl.BlockSpec(memory_space=pltpu.VMEM),
        out_shape=jax.ShapeDtypeStruct((rows, sum(widths)), BF),
        compiler_params=pltpu.CompilerParams(vmem_limit_bytes=VMEM_LIMIT),
        cost_estimate=pl.CostEstimate(flops=1, bytes_accessed=1, transcendentals=0),
        name="assemble",
    )(place, *flat)


class Scatter:
    def __init__(self, sizes, keep, send, first, turn, direct=False):
        self.wide, self.narrow = sizes
        self.first = first
        self.keep, self.sends = keep, [send]
        self.columns, self.lead = keep.shape[-1], keep.shape[0]
        self.left = [b for b in bits_of(self.wide) if b != first]
        high, low = [b for b in self.left if b > first], [b for b in self.left if b < first]
        turn = turn % max(len(high), 1)
        self.plan = [first] + (["high"] if direct else high[turn:] + high[:turn]) + low[::-1] + ["narrow"]
        self.flight = None

    def go(self):
        step = self.plan[0]
        if step == "narrow":
            self.flight = [lax.ppermute(s, NARROW, flipped(self.narrow, k + 1)) for k, s in enumerate(self.sends)]
        elif step == "high":
            self.flight = [lax.ppermute(s, WIDE, flipped(self.wide, 2 * self.first * (k + 1))) for k, s in enumerate(self.sends)]
        else:
            self.flight = [lax.ppermute(self.sends[0], WIDE, flipped(self.wide, step))]

    def land(self):
        self.plan.pop(0)
        value = self.keep.astype(F32)
        for received in self.flight:
            value = value + received.astype(F32)
        self.flight = None
        if not self.plan:
            self.keep, self.sends = value.reshape(self.lead, -1, self.columns), []
            return
        value = value.astype(BF)
        step = self.plan[0]
        if step == "narrow":
            value = value.reshape(self.lead, self.narrow, -1, self.columns)
            at = lax.axis_index(NARROW)
            pick = lambda k: lax.dynamic_slice_in_dim(value, at ^ k, 1, 1)[:, 0]
            self.keep, self.sends = pick(0), [pick(k) for k in range(1, self.narrow)]
        elif step == "high":
            count = self.wide // (2 * self.first)
            self.left = [b for b in self.left if b < self.first]
            value = value.reshape(self.lead, count, -1, self.columns)
            at = lax.axis_index(WIDE) // (2 * self.first)
            pick = lambda k: lax.dynamic_slice_in_dim(value, at ^ k, 1, 1)[:, 0]
            self.keep, self.sends = pick(0), [pick(k) for k in range(1, count)]
        else:
            parts = self.lead << sum(b > step for b in self.left)
            self.left.remove(step)
            value = value.reshape(parts, 2, -1, self.columns)
            mine = (lax.axis_index(WIDE) // step) % 2
            pick = lambda k: lax.dynamic_slice_in_dim(value, k, 1, 1)[:, 0]
            self.keep, self.sends = pick(mine), [pick(1 - mine)]

    def join(self, other):
        side = lambda a, b: jnp.concatenate([a, b], axis=-1)
        self.keep, self.sends = side(self.keep, other.keep), [side(a, b) for a, b in zip(self.sends, other.sends)]
        self.columns += other.columns

    def state(self, landing):
        return (self.keep, self.sends, self.flight if landing else None)

    def put(self, state, landing):
        self.keep, self.sends = state[0], state[1]
        if landing:
            self.flight = state[2]


class Total:
    def __init__(self, sizes, value):
        self.value = value
        self.flight = None
        self.narrow = sizes[1]
        self.plan = [(sizes[0], bit) for bit in bits_of(sizes[0])] + ["narrow"]

    def go(self):
        if self.plan[0] == "narrow":
            self.flight = [lax.ppermute(self.value, NARROW, flipped(self.narrow, k)) for k in range(1, self.narrow)]
        else:
            self.flight = [lax.ppermute(self.value, WIDE, flipped(*self.plan[0]))]

    def land(self):
        if self.plan.pop(0) == "narrow":
            at = lax.axis_index(NARROW)
            parts = [self.value] + self.flight
            total = None
            for j in range(self.narrow):
                term = parts[0]
                for k in range(1, self.narrow):
                    term = jnp.where((at ^ k) == j, parts[k], term)
                total = term if total is None else total + term
            self.value = total
        else:
            self.value = self.value + self.flight[0]
        self.flight = None

    def state(self, landing):
        return (self.value, self.flight if landing else None)

    def put(self, state, landing):
        self.value = state[0]
        if landing:
            self.flight = state[1]


class Rounds:
    def __init__(self):
        self.live = {}
        self.moving = []

    def __getitem__(self, name):
        return self.live[name]

    def run(self, work=None, go=(), land=()):
        for mover in go:
            if mover not in self.moving:
                self.moving.append(mover)
            if mover.plan and mover.flight is None:
                mover.go()
        if work is not None:
            self.live.update(work())
        landing = [m for m in self.moving if m in land and m.flight is not None]
        known = [m for m in self.moving if m.flight is None or m in landing]
        live, states = lax.optimization_barrier((self.live, [m.state(m in landing) for m in known]))
        self.live = live
        for mover, state in zip(known, states):
            mover.put(state, mover in landing)
        for mover in landing:
            mover.land()

    def step(self, work=None, movers=()):
        movers = [m for m in movers if m.plan]
        self.run(work, movers, movers)


def store_halves(me, first_rows, result, keep_ref, send_ref, at):
    low = result.astype(BF)
    for part in range(result.shape[0] // (2 * first_rows)):
        even = low[2 * part * first_rows: (2 * part + 1) * first_rows]
        odd = low[(2 * part + 1) * first_rows: (2 * part + 2) * first_rows]
        index = at(part)
        keep_ref[index] = jnp.where(me == 0, even, odd)
        send_ref[index] = jnp.where(me == 0, odd, even)


def unit_of(value):
    inverse = lax.rsqrt(jnp.mean(value * value, axis=-1, keepdims=True) + EPSILON)
    return value * inverse, inverse


def norm_back(grad_norm, value, gain):
    unit, inverse = unit_of(value)
    grad_gain = jnp.sum(grad_norm * unit, axis=0, keepdims=True)
    grad_unit = grad_norm * gain
    return inverse * (grad_unit - unit * jnp.mean(grad_unit * unit, axis=-1, keepdims=True)), grad_gain


def call(kernel, name, grid, ins, outs, flops, scratch=(), limit=VMEM_LIMIT):
    spec = lambda block, index: pl.BlockSpec(block, index) if index is not None else pl.BlockSpec(memory_space=block)
    size = lambda shape, kind: jnp.dtype(kind).itemsize * functools.reduce(lambda a, b: a * b, shape, 1)
    moved = sum(size(a.shape, a.dtype) for a, _, _ in ins) + sum(size(o[0], o[1]) for o in outs)
    return pl.pallas_call(
        kernel,
        grid=grid,
        in_specs=[spec(b, i) for _, b, i in ins],
        out_specs=[spec(b, i) for _, _, b, i in outs],
        out_shape=[jax.ShapeDtypeStruct(s, d) for s, d, _, _ in outs],
        scratch_shapes=list(scratch),
        compiler_params=pltpu.CompilerParams(vmem_limit_bytes=limit),
        cost_estimate=pl.CostEstimate(flops=1, bytes_accessed=1, transcendentals=0),
        name=name,
    )(*[a for a, _, _ in ins])


ROWS = 512
FFN_ROWS = 256
row_map = lambda i: (i, 0)
col_map = lambda i: (0, i)
whole = lambda i: (0, 0)
at_col = lambda c: (lambda i: (0, c))


def proj_self_kernel(x_ref, gain_ref, w_ref, nt_ref, qkv_ref):
    unit, _ = unit_of(x_ref[...].astype(F32))
    n = (unit * gain_ref[0:1, :]).astype(BF)
    nt_ref[...] = n.T
    qkv_ref[...] = dot(n, w_ref[...]).astype(BF)


def spans_dot(refs, w, dims):
    total, at = None, 0
    for ref in refs:
        columns = ref.shape[1]
        term = dot(ref[...], w[:, at: at + columns], dims)
        total = term if total is None else total + term
        at += columns
    return total


def mid_kernel(x_ref, e_ref, gain_ref, wo_ref, wc_ref, *refs):
    o_refs, (x2_ref, nt_ref, qc_ref, kv_ref, et_ref) = refs[:-5], refs[-5:]
    width = x_ref.shape[1]
    e = e_ref[...]
    et_ref[...] = e.T
    kv_ref[...] = dot(e, wc_ref[:, width: 3 * width]).astype(BF)
    x2 = x_ref[...].astype(F32) + spans_dot(o_refs, wo_ref, NT)
    x2_ref[...] = x2
    unit, _ = unit_of(x2)
    n = (unit * gain_ref[1:2, :]).astype(BF)
    nt_ref[...] = n.T
    qc_ref[...] = dot(n, wc_ref[:, :width]).astype(BF)


def third_kernel(x2_ref, g_ref, gain_ref, wo_ref, *refs):
    o_refs, (x3_ref, n_ref, nt_ref, gt_ref) = refs[:-4], refs[-4:]
    x3 = x2_ref[...] + spans_dot(o_refs, wo_ref, NT)
    x3_ref[...] = x3
    unit, _ = unit_of(x3)
    n = (unit * gain_ref[2:3, :]).astype(BF)
    n_ref[...] = n
    nt_ref[...] = n.T
    gt_ref[...] = g_ref[...].T


def ffn_kernel(n_ref, nt_ref, g_ref, gt_ref, win_ref, wout_ref, y_ref, dn_ref, dw_ref):
    w_in, w_out = win_ref[...], wout_ref[...]
    tokens = n_ref.shape[0]

    @pl.when(pl.program_id(0) == 0)
    def _():
        y_ref[...] = jnp.zeros_like(y_ref)
        dn_ref[...] = jnp.zeros_like(dn_ref)

    acts, grads = [], []
    for r in range(tokens // FFN_ROWS):
        rows = pl.ds(FFN_ROWS * r, FFN_ROWS)
        a = dot(n_ref[rows, :], w_in)
        back = dot(g_ref[rows, :], w_out)
        phi = 0.5 * (1.0 + lax.erf(a * ROOT_HALF))
        act = (a * phi).astype(BF)
        slope = phi + a * jnp.exp(-0.5 * a * a) * INV_ROOT_TWO_PI
        da = (back * slope).astype(BF)
        y_ref[rows, :] += dot(act, w_out, NT)
        dn_ref[rows, :] += dot(da, w_in, NT)
        acts.append(act)
        grads.append(da)
    tile = w_in.shape[1]
    dw_ref[:, :tile] = dot(nt_ref[...], jnp.concatenate(grads, axis=0)).astype(BF)
    dw_ref[:, tile:] = dot(gt_ref[...], jnp.concatenate(acts, axis=0)).astype(BF)


def top_kernel(y_ref, dn_ref, x3_ref, g_ref, gain_ref, wo_ref, out_ref, dx_ref, lowt_ref, doc_ref, gg_ref):
    x3 = x3_ref[...]
    out_ref[...] = (x3 + y_ref[...]).astype(BF)
    grad, grad_gain = norm_back(dn_ref[...], x3, gain_ref[2:3, :])
    dx = g_ref[...].astype(F32) + grad
    dx_ref[...] = dx
    low = dx.astype(BF)
    lowt_ref[...] = low.T
    doc_ref[...] = dot(low, wo_ref[...]).astype(BF)

    @pl.when(pl.program_id(0) == 0)
    def _():
        gg_ref[...] = jnp.zeros_like(gg_ref)

    gg_ref[0:1, :] += grad_gain


def second_kernel(x2_ref, dx3_ref, gain_ref, wq_ref, wo_ref, *refs):
    dq_refs, (dx_ref, lowt_ref, do_ref, gg_ref) = refs[:-4], refs[-4:]
    grad, grad_gain = norm_back(spans_dot(dq_refs, wq_ref, NT), x2_ref[...], gain_ref[1:2, :])
    dx = dx3_ref[...] + grad
    dx_ref[...] = dx
    low = dx.astype(BF)
    lowt_ref[...] = low.T
    do_ref[...] = dot(low, wo_ref[...]).astype(BF)

    @pl.when(pl.program_id(0) == 0)
    def _():
        gg_ref[...] = jnp.zeros_like(gg_ref)

    gg_ref[0:1, :] += grad_gain


def last_kernel(x_ref, dx2_ref, gain_ref, wq_ref, wk_ref, wv_ref, *refs):
    d_refs, (dx_ref, gg_ref) = refs[:-2], refs[-2:]
    n = len(d_refs) // 3
    dq, dk, dv = (d_refs[n * i: n * (i + 1)] for i in range(3))
    dn = spans_dot(dq, wq_ref, NT) + spans_dot(dk, wk_ref, NT) + spans_dot(dv, wv_ref, NT)
    grad, grad_gain = norm_back(dn, x_ref[...].astype(F32), gain_ref[0:1, :])
    dx_ref[...] = dx2_ref[...] + grad

    @pl.when(pl.program_id(0) == 0)
    def _():
        gg_ref[...] = jnp.zeros_like(gg_ref)

    gg_ref[0:1, :] += grad_gain


def encoder_kernel(ck_ref, cv_ref, *refs):
    n = len(refs) // 2
    refs[-1][...] = spans_dot(refs[:n], ck_ref, NT) + spans_dot(refs[n: 2 * n], cv_ref, NT)


def grads_kernel(first_rows, lefts, groups, me_ref, *refs):
    count = sum(groups)
    n_left = max(lefts) + 1
    left_refs, right_refs = refs[:n_left], refs[n_left: n_left + count]
    outs = refs[n_left + count: n_left + count + 2 * len(groups)]
    left_buf, right_buf, sems = refs[n_left + count + 2 * len(groups):]
    widths = [ref.shape[1] for ref in right_refs]

    def copies(p):
        found = [pltpu.make_async_copy(right_refs[p], right_buf.at[p % 2, :, pl.ds(0, widths[p])], sems.at[p % 2])]
        if p == 0 or lefts[p] != lefts[p - 1]:
            found.append(pltpu.make_async_copy(left_refs[lefts[p]], left_buf.at[lefts[p] % 2], sems.at[2 + lefts[p] % 2]))
        return found

    for copy in copies(0):
        copy.start()
    for p in range(count):
        if p + 1 < count:
            for copy in copies(p + 1):
                copy.start()
        for copy in copies(p):
            copy.wait()
        group = next(g for g in range(len(groups)) if p < sum(groups[: g + 1]))
        base = sum(widths[sum(groups[:group]): p])
        width = widths[p]
        tile = 384 if width % 256 else 256
        keep_ref, send_ref = outs[2 * group], outs[2 * group + 1]
        for col in range(0, width, tile):
            result = dot(left_buf[lefts[p] % 2], right_buf[p % 2, :, col: col + tile])
            out = slice(base + col, base + col + tile)
            store_halves(me_ref[0], first_rows, result, keep_ref, send_ref, lambda part: (0, part, slice(None), out))


def weight_grads(name, lefts_arrays, lefts, rights, groups, half, first_rows):
    width = lefts_arrays[0].shape[0]
    tokens = rights[0].shape[0]
    columns = max(v.shape[1] for v in rights)
    count = len(rights)
    ends = [sum(groups[:g]) for g in range(len(groups) + 1)]
    sizes = [sum(v.shape[1] for v in rights[ends[g]: ends[g + 1]]) for g in range(len(groups))]
    shapes = [(1, width // (2 * first_rows), first_rows, n) for n in sizes for _ in range(2)]
    flops = 2 * width * tokens * columns * count
    return pl.pallas_call(
        functools.partial(grads_kernel, first_rows, lefts, groups),
        in_specs=[pl.BlockSpec(memory_space=pltpu.SMEM)] + [pl.BlockSpec(memory_space=pl.ANY)] * (len(lefts_arrays) + count),
        out_specs=[pl.BlockSpec(memory_space=pltpu.VMEM)] * len(shapes),
        out_shape=[jax.ShapeDtypeStruct(shape, BF) for shape in shapes],
        scratch_shapes=[pltpu.VMEM((2, width, tokens), BF), pltpu.VMEM((2, tokens, columns), BF), pltpu.SemaphoreType.DMA((4,))],
        compiler_params=pltpu.CompilerParams(vmem_limit_bytes=VMEM_LIMIT),
        cost_estimate=pl.CostEstimate(flops=1, bytes_accessed=1, transcendentals=0),
        name=name,
    )(half, *lefts_arrays, *rights)


SPANS = ((0, 3), (3, 3))
CROSS_SPANS = ((0, 6),)


def body(sizes, inputs, encoder_out, segments, enc_segments, buckets, gains, rel_bias, self_q, self_kv, self_out, cross_q, cross_kv, cross_out, ffn_in, ffn_out, out_grad):
    wide, narrow = sizes
    micro, per, length, width = inputs.shape
    rows = micro * per
    tokens = rows * length
    hidden = ffn_in.shape[1]
    flat = lambda v: v.reshape(tokens, width)
    x, enc, grad_out = flat(inputs), flat(encoder_out), flat(out_grad)
    seg, enc_seg = segments.reshape(rows, length), enc_segments.reshape(rows, length)
    me = lax.axis_index(WIDE)

    outer_t = ffn_out.T
    gain_cols = jnp.pad(gains.T, ((0, 0), (0, 125)))
    shard_self = jnp.concatenate([self_q, self_kv[0], self_kv[1], gain_cols], axis=1)
    shard_cross = jnp.concatenate([cross_q, cross_kv[0], cross_kv[1], cross_out.T, self_out.T], axis=1)
    g_self = Gather(sizes, shard_self, (9 * 128, 10 * 128))
    g_cross = Gather(sizes, shard_cross, (15 * 128, 15 * 128))
    shard_ffn = jnp.concatenate([ffn_in, outer_t], axis=1)
    block_rows = self_q.shape[0] * narrow
    first = 1 << len(low_bits(wide, block_rows))
    first_rows = block_rows * first
    half = ((me // first) % 2).astype(jnp.int32).reshape(1)
    parts = width // (2 * first_rows)

    steps = (tokens // ROWS,)
    wide_f32 = lambda: ((tokens, width), F32, (ROWS, width), row_map)
    wide_low = lambda n=1: ((tokens, n * width), BF, (ROWS, n * width), row_map)
    turned = lambda: ((width, tokens), BF, (width, ROWS), col_map)
    gain_out = lambda: ((8, width), F32, (8, width), whole)
    rows_in = lambda v: (v, (ROWS, v.shape[1]), row_map)
    entire = lambda v: (v, v.shape, whole)
    piece = lambda slab, c: (slab, (width, width), at_col(c))
    unit = 2 * tokens * width * width

    r = Rounds()
    movers = [g_self, g_cross]
    r.moving = list(movers)
    r.live = {"x": x, "enc": enc, "g": grad_out}

    def prepare():
        return {"self_seg": segment_columns(seg, seg), "cross_seg": segment_columns(seg, enc_seg), "table": score_table(rel_bias, buckets)}

    def take_self():
        slab = g_self.whole()
        return {"slab_self": slab, "gain": slab[:, 3 * width: 3 * width + 3].T.astype(F32)}

    def proj():
        n1t, qkv = call(proj_self_kernel, "proj_self", steps, [rows_in(r["x"]), entire(r["gain"]), (r["slab_self"], (width, 3 * width), whole)], [turned(), wide_low(3)], 3 * unit)
        return {"n1t": n1t, "qkv": qkv}

    def fwd_self(i):
        o, p, s = attn_fwd(SPANS[i], r["qkv"], 0, r["qkv"], 6, r["qkv"], 12, *r["self_seg"], r["table"])
        return {f"o{i}": o, f"p{i}": p, f"s{i}": s}

    def both(name):
        return [r[f"{name}{i}"] for i in range(2) if f"{name}{i}" in r.live]

    def mid():
        out = call(mid_kernel, "mid", steps,
                   [rows_in(r["x"]), rows_in(r["enc"]), entire(r["gain"]), piece(r["slab_cross"], 4), (r["slab_cross"], (width, 3 * width), whole)] + [rows_in(o) for o in both("o")],
                   [wide_f32(), turned(), wide_low(), wide_low(2), turned()], 4 * unit)
        return dict(zip(("x2", "n2t", "qc", "kvc", "et"), out))

    def fwd_cross(i):
        o, p, s = attn_fwd(CROSS_SPANS[i], r["qc"], 0, r["kvc"], 0, r["kvc"], 6, *r["cross_seg"])
        return {f"oc{i}": o, f"pc{i}": p, f"sc{i}": s}

    def third():
        out = call(third_kernel, "third", steps,
                   [rows_in(r["x2"]), rows_in(r["g"]), entire(r["gain"]), piece(r["slab_cross"], 3)] + [rows_in(o) for o in both("oc")],
                   [wide_f32(), wide_low(), turned(), turned()], unit)
        return dict(zip(("x3", "n3", "n3t", "gt"), out))

    tile = 512
    tiles = hidden // tile
    acc_out = ((tokens, width), F32, (tokens, width), whole)

    def ffn():
        slab = r["slab_ffn"]
        y, dn, dw = call(
            ffn_kernel, "ffn", (tiles,),
            [entire(r["n3"]), entire(r["n3t"]), entire(r["g"]), entire(r["gt"]),
             (slab, (width, tile), lambda j: (0, j)), (slab, (width, tile), lambda j: (0, tiles + j))],
            [acc_out, acc_out, ((width, 2 * hidden), BF, (width, 2 * tile), lambda j: (0, j))], 12 * tokens * width * hidden)
        return {"y": y, "dn": dn, "dw": dw}

    def top():
        out = call(top_kernel, "top", steps,
                   [rows_in(r["y"]), rows_in(r["dn"]), rows_in(r["x3"]), rows_in(r["g"]), entire(r["gain"]), piece(r["slab_cross"], 3)],
                   [wide_low(), wide_f32(), turned(), wide_low(), gain_out()], unit)
        return dict(zip(("layer", "dx3", "three_t", "doc", "gain3"), out))

    def bwd_cross(i):
        out = attn_bwd(CROSS_SPANS[i], r["qc"], 0, r["kvc"], 0, r["kvc"], 6, r["doc"], r[f"oc{i}"], r[f"pc{i}"], r[f"sc{i}"], False)
        return dict(zip((f"dqc{i}", f"dkc{i}", f"dvc{i}"), out))

    def second():
        out = call(second_kernel, "second", steps,
                   [rows_in(r["x2"]), rows_in(r["dx3"]), entire(r["gain"]), piece(r["slab_cross"], 0), piece(r["slab_cross"], 4)] + [rows_in(d) for d in both("dqc")],
                   [wide_f32(), turned(), wide_low(), gain_out()], 2 * unit)
        return dict(zip(("dx2", "two_t", "do", "gain2"), out))

    def grads_cross():
        rights = both("dqc") + both("dkc") + both("dvc")
        n = len(CROSS_SPANS)
        return {"cut_cross": weight_grads("grads_cross", [r["n2t"], r["et"]], (0,) * n + (1,) * (2 * n), rights, (3 * n,), half, first_rows)}

    def grads_out():
        lefts = (0,) * len(CROSS_SPANS) + (1,) * len(SPANS)
        return {"cut_out": weight_grads("grads_out", [r["three_t"], r["two_t"]], lefts, both("oc") + both("o"), (len(lefts),), half, first_rows)}

    def bwd_self(i):
        out = attn_bwd(SPANS[i], r["qkv"], 0, r["qkv"], 6, r["qkv"], 12, r["do"], r[f"o{i}"], r[f"p{i}"], r[f"s{i}"], True)
        return dict(zip((f"dq{i}", f"dk{i}", f"dv{i}", f"diag{i}"), out))

    def grads_self(i):
        return {f"cut_self{i}": weight_grads("grads_self", [r["n1t"]], (0, 0, 0), [r[f"dq{i}"], r[f"dk{i}"], r[f"dv{i}"]], (3,), half, first_rows)}

    def last():
        out = call(last_kernel, "last", steps,
                   [rows_in(r["x"]), rows_in(r["dx2"]), entire(r["gain"])] + [piece(r["slab_self"], c) for c in range(3)]
                   + [rows_in(d) for name in ("dq", "dk", "dv") for d in both(name)],
                   [wide_f32(), gain_out()], 3 * unit)
        return dict(zip(("dx1", "gain1"), out))

    def encoder():
        out = call(encoder_kernel, "encoder_grad", steps,
                   [piece(r["slab_cross"], c) for c in (1, 2)] + [rows_in(d) for name in ("dkc", "dvc") for d in both(name)],
                   [wide_f32()], 2 * unit)
        return {"de": out[0]}

    def cut(pair, turn, direct=False):
        return Scatter(sizes, pair[0], pair[1], first, turn, direct)

    r.step(prepare, [g_self])
    r.run(None, [g_self, g_cross], [g_self])
    while len(g_self.plan) > 1:
        r.step(None, [g_self])
    r.run(None, [g_self], [g_self, g_cross])
    g_self.groups, shard_ffn = lax.optimization_barrier((g_self.groups, shard_ffn))
    slab_ffn = lax.all_gather(shard_ffn, (WIDE, NARROW), axis=0, tiled=True)
    r.run(take_self, [g_cross], [])
    r.run(proj, [], [g_cross])
    r.run(lambda: fwd_self(0), [g_cross], [])
    r.run(lambda: fwd_self(1), [], [g_cross])
    while g_cross.plan:
        r.step(None, [g_cross])
    r.step(lambda: {"slab_cross": g_cross.whole()}, [])
    r.step(mid, [])
    r.step(lambda: fwd_cross(0), [])
    r.step(third, [])
    r.moving = []
    r.live["slab_ffn"] = slab_ffn
    r.step(None, [])
    r.step(ffn, [])
    ffn_sum = lax.psum_scatter(r.live.pop("dw"), (WIDE, NARROW), scatter_dimension=0, tiled=True).astype(F32)
    ffn_sum = ffn_sum.reshape(-1, tiles, 2, tile)
    r.step(top, [])
    r.step(lambda: bwd_cross(0), [])
    r.step(grads_cross, [])
    sc = cut(r.live.pop("cut_cross"), 0)
    r.step(second, [sc])
    r.run(grads_out, [sc], [])
    so = cut(r.live.pop("cut_out"), 1)
    r.run(lambda: bwd_self(0), [so], [so])
    r.run(lambda: grads_self(0), [so], [sc])
    s0 = cut(r.live.pop("cut_self0"), 1, True)
    r.run(lambda: bwd_self(1), [sc, s0], [s0, sc, so])
    r.run(lambda: grads_self(1), [sc, so], [sc])
    s1 = cut(r.live.pop("cut_self1"), 0, True)
    r.run(last, [s0, s1], [s0, s1, so])

    def small():
        diag = jnp.concatenate(both("diag"), axis=0)
        bias_rows = bucket_sums(diag, buckets, rel_bias.shape[0])
        return {"small": jnp.concatenate([r["gain1"][0], r["gain2"][0], r["gain3"][0], bias_rows.reshape(-1)]).reshape(-1, 128)}

    r.live.update(small())
    total = Total(sizes, r.live.pop("small"))
    r.live["ffn_sum"] = ffn_sum
    r.step(encoder, [s1, total])
    ffn_sum = r.live.pop("ffn_sum")
    ends = [so, s0, s1]
    while any(s.plan != ["narrow"] for s in ends):
        r.step(None, [s for s in ends if s.plan != ["narrow"]])
    for other in (s0, s1):
        so.join(other)
        r.moving.remove(other)
    r.run(None, [so, total], [total])
    r.run(None, [total], [so, total])
    while any(s.plan for s in (sc, so, total)):
        r.step(None, [sc, so, total])

    summed = total.value.reshape(-1)
    shard = me * narrow + lax.axis_index(NARROW)
    own = width // (wide * narrow)
    gain_sum = lax.dynamic_slice_in_dim(summed[: 3 * width].reshape(3, width), shard * own, own, 1)
    bias_sum = summed[3 * width:].reshape(rel_bias.shape)

    own_rows = lambda value, at, n: value.keep[0, :, at: at + n]

    def self_part(index):
        found, at = [], 2 * width
        for _, pairs in SPANS:
            n = 128 * pairs
            found.append(own_rows(so, at + n * index, n))
            at += 3 * n
        return jnp.concatenate(found, axis=1)

    cross_part = lambda index: own_rows(sc, width * index, width)
    shaped = lambda v: v.reshape(micro, per, length, width)
    return (
        shaped(r["layer"]),
        shaped(r["dx1"]),
        shaped(r["de"]),
        gain_sum,
        bias_sum,
        self_part(0),
        jnp.stack([self_part(1), self_part(2)]),
        own_rows(so, width, width).T,
        cross_part(0),
        jnp.stack([cross_part(1), cross_part(2)]),
        own_rows(so, 0, width).T,
        ffn_sum[:, :, 0].reshape(-1, hidden),
        ffn_sum[:, :, 1].reshape(-1, hidden).T,
    )


def solution(mesh):
    axes = (WIDE, NARROW)
    batch4, batch3 = P(None, axes, None, None), P(None, axes, None)
    first, second, middle = P(axes, None), P(None, axes), P(None, axes, None)
    sizes = (mesh.shape[WIDE], mesh.shape[NARROW])
    weights = (first, middle, second, first, middle, second, first, second)
    return jax.shard_map(
        functools.partial(body, sizes),
        mesh=mesh,
        in_specs=(batch4, batch4, batch3, batch3, P(), second, P()) + weights + (batch4,),
        out_specs=(batch4, batch4, batch4, second, P()) + weights,
        check_vma=False,
    )
```

```python
import functools
import jax
import jax.numpy as jnp
from jax import lax
from jax.sharding import PartitionSpec as P
from jax.experimental import pallas as pl
from jax.experimental.pallas import tpu as pltpu

DH = 64
NEGATIVE = -1e30
BF = jnp.bfloat16
F32 = jnp.float32
NN = (((1,), (0,)), ((), ()))
NT = (((1,), (1,)), ((), ()))
TN = (((0,), (0,)), ((), ()))
MB = 1 << 20


def dot(a, b, dims=NN):
    return lax.dot_general(a, b, dims, preferred_element_type=F32)


def segment_columns(query_seg, key_seg):
    ids = jnp.arange(128)
    other = (query_seg[..., None] != ids) & (ids < 4)
    query_cols = jnp.where(other, NEGATIVE, 0.0).astype(BF)
    key_cols = (key_seg[..., None] == ids).astype(BF)
    return query_cols, key_cols


def fold(values, combine):
    rows = [values[8 * i: 8 * (i + 1)] for i in range(values.shape[0] // 8)]
    while len(rows) > 1:
        rows = [combine(rows[2 * i], rows[2 * i + 1]) for i in range(len(rows) // 2)] + rows[len(rows) - len(rows) % 2:]
    return rows[0]


CHUNK = 128
LANES = 256


def attn_fwd_kernel(causal, q_ref, k_ref, v_ref, qs_ref, ks_ref, *rest):
    if causal:
        t_ref, o_ref, e_ref, inv_ref, s_buf, bias = rest
    else:
        o_ref, e_ref, inv_ref, s_buf = rest
    length = q_ref.shape[0]
    if causal:
        @pl.when(pl.program_id(1) == 0)
        def _():
            for h in range(2):
                for d in range(length // 128):
                    row = jnp.concatenate([t_ref[h, :, pl.ds(128 * (d + 1), 128)], t_ref[h, :, pl.ds(128 * d, 128)]], axis=1)
                    tile = pltpu.roll(jnp.broadcast_to(row, (128, 256)), 0, 1, stride=1, stride_axis=0)
                    bias[h, d] = tile[:, :128]
    lane = lax.broadcasted_iota(jnp.int32, (1, 128), 1)
    q = q_ref[...]
    keys = jnp.concatenate([k_ref[...], ks_ref[...]], axis=1)
    v_t = v_ref[...].T
    qa = [jnp.concatenate([jnp.where((lane // DH) == h, q, 0).astype(BF), qs_ref[...]], axis=1) for h in range(2)]
    work = [(h, c) for h in range(2) for c in range(length // LANES)]
    reach = lambda c: LANES * (c + 1) if causal else length

    def scores(i):
        h, c = work[i]
        s_buf[i % 2, :reach(c), :] = dot(keys[:reach(c)], qa[h][LANES * c: LANES * (c + 1)], NT)

    def place(h, c, kb):
        if not causal:
            return [(0, LANES, None)]
        found = []
        for qb in range(LANES // 128):
            d = qb + LANES // 128 * c - kb
            if d >= 0:
                found.append((128 * qb, 128, (h, d)))
        return found

    def load(i, kb, lo, width, tile):
        value = s_buf[i % 2, CHUNK * kb: CHUNK * (kb + 1), lo: lo + width]
        return value if tile is None else value + bias[tile[0], tile[1]]

    scores(0)
    for i, (h, c) in enumerate(work):
        if i + 1 < len(work):
            scores(i + 1)
        blocks = reach(c) // CHUNK
        tops = {}
        for kb in range(blocks):
            for lo, width, tile in place(h, c, kb):
                new = fold(load(i, kb, lo, width, tile), jnp.maximum)
                tops[lo] = new if lo not in tops else jnp.maximum(tops[lo], new)
        tops = {lo: jnp.max(t, axis=0, keepdims=True) for lo, t in tops.items()}
        sums = {}
        for kb in range(blocks):
            seen = place(h, c, kb)
            for lo, width, tile in seen:
                e = jnp.exp(load(i, kb, lo, width, tile) - tops[lo])
                new = fold(e, jnp.add)
                sums[lo] = new if lo not in sums else sums[lo] + new
                e_ref[h, CHUNK * kb: CHUNK * (kb + 1), LANES * c + lo: LANES * c + lo + width] = e.astype(BF)
            for lo in range(0, LANES, 128):
                if causal and lo not in [x[0] for x in seen]:
                    e_ref[h, CHUNK * kb: CHUNK * (kb + 1), LANES * c + lo: LANES * c + lo + 128] = jnp.zeros((CHUNK, 128), BF)
        total = jnp.concatenate([jnp.sum(sums[lo], axis=0, keepdims=True) for lo in sorted(sums)], axis=1)
        inv = 1.0 / total
        inv_ref[h, :, LANES * c: LANES * (c + 1)] = jnp.broadcast_to(inv, (8, LANES))
    parts = []
    for h in range(2):
        mine = v_t[DH * h: DH * (h + 1)]
        if causal:
            mixed = [dot(mine[:, :reach(c)], e_ref[h, :reach(c), LANES * c: LANES * (c + 1)]) for c in range(length // LANES)]
        else:
            mixed = [dot(mine, e_ref[h])]
        parts.append(jnp.concatenate(mixed, axis=1) * inv_ref[h, 0:1, :])
    o_ref[...] = jnp.concatenate(parts, axis=0).T.astype(BF)


def attn_fwd(span, q_arr, q_col, k_arr, k_col, v_arr, v_col, q_seg, k_seg, table=None):
    rows, length = q_seg.shape[:2]
    begin, pairs = span
    causal = table is not None
    block = lambda col: pl.BlockSpec((length, 128), lambda h, b: (b, begin + col + h))
    seg = pl.BlockSpec((None, length, 128), lambda h, b: (b, 0, 0))
    in_specs = [block(q_col), block(k_col), block(v_col), seg, seg]
    args = [q_arr, k_arr, v_arr, q_seg, k_seg]
    scratch = []
    if causal:
        in_specs.append(pl.BlockSpec((2, 1, table.shape[2]), lambda h, b: (begin + h, 0, 0)))
        args.append(table)
        scratch = [pltpu.VMEM((2, length // 128, 128, 128), F32)]
    scratch = [pltpu.VMEM((2, length, LANES), F32)] + scratch
    stat = pl.BlockSpec((None, 2, 8, length), lambda h, b: (b, h, 0, 0))
    return pl.pallas_call(
        functools.partial(attn_fwd_kernel, causal),
        grid=(pairs, rows),
        in_specs=in_specs,
        out_specs=[pl.BlockSpec((length, 128), lambda h, b: (b, h)), pl.BlockSpec((None, 2, length, length), lambda h, b: (b, h, 0, 0)), stat],
        out_shape=[jax.ShapeDtypeStruct((rows * length, pairs * 128), BF), jax.ShapeDtypeStruct((rows, 2 * pairs, length, length), BF), jax.ShapeDtypeStruct((rows, 2 * pairs, 8, length), F32)],
        scratch_shapes=scratch,
        compiler_params=pltpu.CompilerParams(vmem_limit_bytes=60 * MB),
        cost_estimate=pl.CostEstimate(flops=1, bytes_accessed=1, transcendentals=0),
        name="attn_fwd_self" if causal else "attn_fwd_cross",
    )(*args)


def attn_bwd_kernel(causal, q_ref, k_ref, v_ref, g_ref, o_ref, e_ref, inv_ref, *rest):
    if causal:
        dq_ref, dk_ref, dv_ref, diag_ref, ds_buf, acc = rest
    else:
        dq_ref, dk_ref, dv_ref, ds_buf = rest
    length = q_ref.shape[0]
    lane = lax.broadcasted_iota(jnp.int32, (1, 128), 1)
    q = q_ref[...]
    values = jnp.concatenate([v_ref[...], jnp.broadcast_to((lane < 2).astype(BF), (length, 128))], axis=1)
    k_t = k_ref[...].T
    g_t = g_ref[...].T.astype(F32)
    o_t = o_ref[...].T.astype(F32)
    if causal:
        @pl.when(pl.program_id(1) == 0)
        def _():
            acc[...] = jnp.zeros_like(acc)

        @pl.when((pl.program_id(0) == 0) & (pl.program_id(1) == 0))
        def _():
            ds_buf[...] = jnp.zeros_like(ds_buf)

    gms, qms, gas = [], [], []
    blank = jnp.zeros((DH, length), BF)
    for h in range(2):
        rows = slice(DH * h, DH * (h + 1))
        gm = (g_t[rows] * inv_ref[h, 0:1, :]).astype(BF)
        delta = -jnp.sum(gm.astype(F32) * o_t[rows], axis=0, keepdims=True)
        high = delta.astype(BF).astype(F32)
        extra = jnp.concatenate([high, delta - high, jnp.zeros((14, length), F32)], axis=0).astype(BF)
        gms.append(jnp.concatenate([blank] * h + [gm] + [blank] * (1 - h), axis=0))
        qms.append(jnp.where((lane // DH) == h, q, 0).astype(BF))
        gas.append(jnp.concatenate([gms[h], extra, jnp.zeros((112, length), BF)], axis=0))
    for h in range(2):
        for c in range(length // LANES):
            n = LANES * (c + 1) if causal else length
            span = slice(LANES * c, LANES * (c + 1))
            dp = dot(values[:n], gas[h][:, span])
            for kb in range(n // CHUNK):
                rows = slice(CHUNK * kb, CHUNK * (kb + 1))
                for qb in range(LANES // 128):
                    d = qb + LANES // 128 * c - kb
                    if causal and d < 0:
                        continue
                    cols = slice(LANES * c + 128 * qb, LANES * c + 128 * (qb + 1))
                    ds = (e_ref[h, rows, cols].astype(F32) * dp[rows, 128 * qb: 128 * (qb + 1)]).astype(BF)
                    ds_buf[h, rows, cols] = ds
                    if causal:
                        acc[h, d] += ds.astype(F32)
    for kb in range(length // LANES):
        rows = slice(LANES * kb, LANES * (kb + 1))
        lo = LANES * kb if causal else 0
        dk, dv = None, None
        for h in range(2):
            a = dot(ds_buf[h, rows, lo:], qms[h][lo:])
            b = dot(e_ref[h, rows, lo:], gms[h][:, lo:], NT)
            dk = a if dk is None else dk + a
            dv = b if dv is None else dv + b
        dk_ref[rows, :] = dk.astype(BF)
        dv_ref[rows, :] = dv.astype(BF)
    dq_ref[...] = jnp.concatenate([dot(k_t[DH * h: DH * (h + 1)], ds_buf[h]) for h in range(2)], axis=0).T.astype(BF)
    if causal:
        @pl.when(pl.program_id(1) == pl.num_programs(1) - 1)
        def _():
            flip = (lax.broadcasted_iota(jnp.int32, (128, 128), 0) + lax.broadcasted_iota(jnp.int32, (128, 128), 1) == 127).astype(F32)
            for h in range(2):
                for d in range(length // 128):
                    upside = jnp.dot(flip, acc[h, d], precision=lax.Precision.HIGHEST, preferred_element_type=F32)
                    wide = jnp.concatenate([upside, jnp.zeros((128, 128), F32)], axis=1)
                    turned = pltpu.roll(wide, 0, 1, stride=1, stride_axis=0)
                    diag_ref[h, pl.ds(d, 1), :] = jnp.sum(turned, axis=0, keepdims=True)


def attn_bwd(span, q_arr, q_col, k_arr, k_col, v_arr, v_col, grad, out, probs, inverse, causal):
    rows, heads, length = probs.shape[:3]
    begin, pairs = span
    block = lambda col: pl.BlockSpec((length, 128), lambda h, b: (b, begin + col + h))
    own = pl.BlockSpec((length, 128), lambda h, b: (b, h))
    flat = jax.ShapeDtypeStruct((rows * length, pairs * 128), BF)
    out_specs = [own] * 3
    out_shape = [flat] * 3
    scratch = [pltpu.VMEM((2, length, length), BF)]
    if causal:
        out_specs.append(pl.BlockSpec((2, length // 128, 256), lambda h, b: (h, 0, 0)))
        out_shape.append(jax.ShapeDtypeStruct((heads, length // 128, 256), F32))
        scratch.append(pltpu.VMEM((2, length // 128, 128, 128), F32))
    return pl.pallas_call(
        functools.partial(attn_bwd_kernel, causal),
        grid=(pairs, rows),
        in_specs=[block(q_col), block(k_col), block(v_col), block(0), own, pl.BlockSpec((None, 2, length, length), lambda h, b: (b, h, 0, 0)), pl.BlockSpec((None, 2, 8, length), lambda h, b: (b, h, 0, 0))],
        out_specs=out_specs,
        out_shape=out_shape,
        scratch_shapes=scratch,
        compiler_params=pltpu.CompilerParams(vmem_limit_bytes=60 * MB),
        cost_estimate=pl.CostEstimate(flops=1, bytes_accessed=1, transcendentals=0),
        name="attn_bwd_self" if causal else "attn_bwd_cross",
    )(q_arr, k_arr, v_arr, grad, out, probs, inverse)


def score_table(rel_bias, buckets):
    hot = buckets[:, None] == jnp.arange(rel_bias.shape[0])[None, :]
    at = jnp.sum(jnp.where(hot[:, :, None], rel_bias[None], 0.0), axis=1)
    return jnp.concatenate([jnp.full((rel_bias.shape[1], 128), NEGATIVE, F32), at.T], axis=1)[:, None]


def bucket_sums(diag, buckets, count):
    heads, blocks, _ = diag.shape
    own = diag[:, :, 127:255]
    before = jnp.pad(diag[:, 1:, :127], ((0, 0), (0, 1), (1, 0)))
    at = (own + before).reshape(heads, blocks * 128)
    hot = buckets[:, None] == jnp.arange(count)[None, :]
    return jnp.sum(jnp.where(hot[:, :, None], at.T[:, None, :], 0.0), axis=0)


EPSILON = 1e-06
ROOT_HALF = 0.7071067811865476
INV_ROOT_TWO_PI = 0.3989422804014327
WIDE, NARROW = "wide", "narrow"
VMEM_LIMIT = 60 * MB


def flipped(size, bit):
    return [(i, i ^ bit) for i in range(size)]


def bits_of(size):
    return [1 << i for i in range(size.bit_length() - 1)]


def merge(blocks, at):
    count = len(blocks)
    slots = []
    for j in range(count):
        slot = blocks[j]
        for k in range(count):
            if k != 0:
                slot = jnp.where((at ^ k) == 0, blocks[j ^ k], slot)
        slots.append(slot)
    return jnp.concatenate(slots, axis=0)


def low_bits(wide, rows):
    low = []
    for bit in bits_of(wide):
        if (rows * bit) % 16 == 0:
            break
        low.append(bit)
    return low


def cross_bits(wide, rows, turn):
    bits = [b for b in bits_of(wide) if b not in low_bits(wide, rows)]
    first, rest = bits[:1], bits[1:]
    turn = turn % max(len(rest), 1)
    return rest[turn:] + rest[:turn] + first


class Gather:
    def __init__(self, sizes, block, cuts):
        self.wide, self.narrow = sizes
        self.cuts = cuts
        self.groups = [[block]]
        self.flight = None
        rows = block.shape[0] * self.narrow
        self.low = low_bits(self.wide, rows)
        self.orders = [cross_bits(self.wide, rows, i) for i in range(len(cuts))]
        self.plan = ["narrow"] + [("low", b) for b in self.low] + list(range(len(self.orders[0])))

    def go(self):
        step = self.plan[0]
        if step == "narrow":
            self.flight = [[lax.ppermute(g[0], NARROW, flipped(self.narrow, k)) for k in range(1, self.narrow)] for g in self.groups]
        elif isinstance(step, tuple):
            self.flight = [[lax.ppermute(g[0], WIDE, flipped(self.wide, step[1]))] for g in self.groups]
        else:
            self.flight = [[lax.ppermute(p, WIDE, flipped(self.wide, self.orders[i][step])) for p in g] for i, g in enumerate(self.groups)]

    def land(self):
        step = self.plan.pop(0)
        joined = lambda at: [[merge(g + f, at)] for g, f in zip(self.groups, self.flight)]
        if step == "narrow":
            self.groups = joined(lax.axis_index(NARROW))
        elif isinstance(step, tuple):
            self.groups = joined((lax.axis_index(WIDE) // step[1]) % 2)
        else:
            self.groups = [g + f for g, f in zip(self.groups, self.flight)]
            if step == 0:
                self.groups = [[jnp.concatenate(g, axis=0)] for g in self.groups]
        if self.plan and self.plan[0] == 0:
            block = self.groups[0][0]
            ends = [sum(self.cuts[:i]) for i in range(len(self.cuts) + 1)]
            self.groups = [[block[:, ends[i]: ends[i + 1]]] for i in range(len(self.cuts))]
        self.flight = None

    def state(self, landing):
        return (self.groups, self.flight if landing else None)

    def put(self, state, landing):
        self.groups = state[0]
        if landing:
            self.flight = state[1]

    def whole(self):
        skip = 1 << len(self.low)
        offsets = []
        for order in self.orders:
            found = [0]
            for bit in order:
                found = found + [f ^ (bit // skip) for f in found]
            offsets.append(found)
        place = (lax.axis_index(WIDE) // skip).astype(jnp.int32).reshape(1)
        return assemble(self.groups, offsets, place)


def assemble_kernel(offsets, columns, counts, me_ref, *refs):
    pieces, out = list(refs[:-1]), refs[-1]
    for g in range(len(columns)):
        found = iter(offsets[g])
        for _ in range(counts[g]):
            piece = pieces.pop(0)
            width = piece.shape[1]
            rows = out.shape[0] // len(offsets[g])
            for k in range(piece.shape[0] // rows):
                start = pl.multiple_of((me_ref[0] ^ next(found)) * rows, 16)
                out[pl.ds(start, rows), columns[g]: columns[g] + width] = piece[rows * k: rows * (k + 1), :]


def assemble(groups, offsets, place):
    widths = [g[0].shape[1] for g in groups]
    columns = [sum(widths[:i]) for i in range(len(groups))]
    flat = [p for g in groups for p in g]
    rows = sum(p.shape[0] for p in groups[0])
    return pl.pallas_call(
        functools.partial(assemble_kernel, offsets, columns, [len(g) for g in groups]),
        in_specs=[pl.BlockSpec(memory_space=pltpu.SMEM)] + [pl.BlockSpec(memory_space=pltpu.VMEM)] * len(flat),
        out_specs=pl.BlockSpec(memory_space=pltpu.VMEM),
        out_shape=jax.ShapeDtypeStruct((rows, sum(widths)), BF),
        compiler_params=pltpu.CompilerParams(vmem_limit_bytes=VMEM_LIMIT),
        cost_estimate=pl.CostEstimate(flops=1, bytes_accessed=1, transcendentals=0),
        name="assemble",
    )(place, *flat)


class Scatter:
    def __init__(self, sizes, keep, send, first, turn, direct=False):
        self.wide, self.narrow = sizes
        self.first = first
        self.keep, self.sends = keep, [send]
        self.columns, self.lead = keep.shape[-1], keep.shape[0]
        self.left = [b for b in bits_of(self.wide) if b != first]
        high, low = [b for b in self.left if b > first], [b for b in self.left if b < first]
        turn = turn % max(len(high), 1)
        self.plan = [first] + (["high"] if direct else high[turn:] + high[:turn]) + low[::-1] + ["narrow"]
        self.flight = None

    def go(self):
        step = self.plan[0]
        if step == "narrow":
            self.flight = [lax.ppermute(s, NARROW, flipped(self.narrow, k + 1)) for k, s in enumerate(self.sends)]
        elif step == "high":
            self.flight = [lax.ppermute(s, WIDE, flipped(self.wide, 2 * self.first * (k + 1))) for k, s in enumerate(self.sends)]
        else:
            self.flight = [lax.ppermute(self.sends[0], WIDE, flipped(self.wide, step))]

    def land(self):
        self.plan.pop(0)
        value = self.keep.astype(F32)
        for received in self.flight:
            value = value + received.astype(F32)
        self.flight = None
        if not self.plan:
            self.keep, self.sends = value.reshape(self.lead, -1, self.columns), []
            return
        value = value.astype(BF)
        step = self.plan[0]
        if step == "narrow":
            value = value.reshape(self.lead, self.narrow, -1, self.columns)
            at = lax.axis_index(NARROW)
            pick = lambda k: lax.dynamic_slice_in_dim(value, at ^ k, 1, 1)[:, 0]
            self.keep, self.sends = pick(0), [pick(k) for k in range(1, self.narrow)]
        elif step == "high":
            count = self.wide // (2 * self.first)
            self.left = [b for b in self.left if b < self.first]
            value = value.reshape(self.lead, count, -1, self.columns)
            at = lax.axis_index(WIDE) // (2 * self.first)
            pick = lambda k: lax.dynamic_slice_in_dim(value, at ^ k, 1, 1)[:, 0]
            self.keep, self.sends = pick(0), [pick(k) for k in range(1, count)]
        else:
            parts = self.lead << sum(b > step for b in self.left)
            self.left.remove(step)
            value = value.reshape(parts, 2, -1, self.columns)
            mine = (lax.axis_index(WIDE) // step) % 2
            pick = lambda k: lax.dynamic_slice_in_dim(value, k, 1, 1)[:, 0]
            self.keep, self.sends = pick(mine), [pick(1 - mine)]

    def join(self, other):
        side = lambda a, b: jnp.concatenate([a, b], axis=-1)
        self.keep, self.sends = side(self.keep, other.keep), [side(a, b) for a, b in zip(self.sends, other.sends)]
        self.columns += other.columns

    def state(self, landing):
        return (self.keep, self.sends, self.flight if landing else None)

    def put(self, state, landing):
        self.keep, self.sends = state[0], state[1]
        if landing:
            self.flight = state[2]


class Total:
    def __init__(self, sizes, value):
        self.value = value
        self.flight = None
        self.plan = [(name, size, bit) for name, size in ((NARROW, sizes[1]), (WIDE, sizes[0])) for bit in bits_of(size)]

    def go(self):
        name, size, bit = self.plan[0]
        self.flight = lax.ppermute(self.value, name, flipped(size, bit))

    def land(self):
        self.plan.pop(0)
        self.value, self.flight = self.value + self.flight, None

    def state(self, landing):
        return (self.value, self.flight if landing else None)

    def put(self, state, landing):
        self.value = state[0]
        if landing:
            self.flight = state[1]


class Rounds:
    def __init__(self):
        self.live = {}
        self.moving = []

    def __getitem__(self, name):
        return self.live[name]

    def run(self, work=None, go=(), land=()):
        for mover in go:
            if mover not in self.moving:
                self.moving.append(mover)
            if mover.plan and mover.flight is None:
                mover.go()
        if work is not None:
            self.live.update(work())
        landing = [m for m in self.moving if m in land and m.flight is not None]
        known = [m for m in self.moving if m.flight is None or m in landing]
        live, states = lax.optimization_barrier((self.live, [m.state(m in landing) for m in known]))
        self.live = live
        for mover, state in zip(known, states):
            mover.put(state, mover in landing)
        for mover in landing:
            mover.land()

    def step(self, work=None, movers=()):
        movers = [m for m in movers if m.plan]
        self.run(work, movers, movers)


def store_halves(me, first_rows, result, keep_ref, send_ref, at):
    low = result.astype(BF)
    for part in range(result.shape[0] // (2 * first_rows)):
        even = low[2 * part * first_rows: (2 * part + 1) * first_rows]
        odd = low[(2 * part + 1) * first_rows: (2 * part + 2) * first_rows]
        index = at(part)
        keep_ref[index] = jnp.where(me == 0, even, odd)
        send_ref[index] = jnp.where(me == 0, odd, even)


def unit_of(value):
    inverse = lax.rsqrt(jnp.mean(value * value, axis=-1, keepdims=True) + EPSILON)
    return value * inverse, inverse


def norm_back(grad_norm, value, gain):
    unit, inverse = unit_of(value)
    grad_gain = jnp.sum(grad_norm * unit, axis=0, keepdims=True)
    grad_unit = grad_norm * gain
    return inverse * (grad_unit - unit * jnp.mean(grad_unit * unit, axis=-1, keepdims=True)), grad_gain


def call(kernel, name, grid, ins, outs, flops, scratch=(), limit=VMEM_LIMIT):
    spec = lambda block, index: pl.BlockSpec(block, index) if index is not None else pl.BlockSpec(memory_space=block)
    size = lambda shape, kind: jnp.dtype(kind).itemsize * functools.reduce(lambda a, b: a * b, shape, 1)
    moved = sum(size(a.shape, a.dtype) for a, _, _ in ins) + sum(size(o[0], o[1]) for o in outs)
    return pl.pallas_call(
        kernel,
        grid=grid,
        in_specs=[spec(b, i) for _, b, i in ins],
        out_specs=[spec(b, i) for _, _, b, i in outs],
        out_shape=[jax.ShapeDtypeStruct(s, d) for s, d, _, _ in outs],
        scratch_shapes=list(scratch),
        compiler_params=pltpu.CompilerParams(vmem_limit_bytes=limit),
        cost_estimate=pl.CostEstimate(flops=1, bytes_accessed=1, transcendentals=0),
        name=name,
    )(*[a for a, _, _ in ins])


ROWS = 512
FFN_ROWS = 256
row_map = lambda i: (i, 0)
col_map = lambda i: (0, i)
whole = lambda i: (0, 0)
at_col = lambda c: (lambda i: (0, c))


def proj_self_kernel(x_ref, gain_ref, w_ref, nt_ref, qkv_ref):
    unit, _ = unit_of(x_ref[...].astype(F32))
    n = (unit * gain_ref[0:1, :]).astype(BF)
    nt_ref[...] = n.T
    qkv_ref[...] = dot(n, w_ref[...]).astype(BF)


def spans_dot(refs, w, dims):
    total, at = None, 0
    for ref in refs:
        columns = ref.shape[1]
        term = dot(ref[...], w[:, at: at + columns], dims)
        total = term if total is None else total + term
        at += columns
    return total


def mid_kernel(x_ref, e_ref, gain_ref, wo_ref, wc_ref, *refs):
    o_refs, (x2_ref, nt_ref, qc_ref, kv_ref, et_ref) = refs[:-5], refs[-5:]
    width = x_ref.shape[1]
    e = e_ref[...]
    et_ref[...] = e.T
    kv_ref[...] = dot(e, wc_ref[:, width: 3 * width]).astype(BF)
    x2 = x_ref[...].astype(F32) + spans_dot(o_refs, wo_ref, NT)
    x2_ref[...] = x2
    unit, _ = unit_of(x2)
    n = (unit * gain_ref[1:2, :]).astype(BF)
    nt_ref[...] = n.T
    qc_ref[...] = dot(n, wc_ref[:, :width]).astype(BF)


def third_kernel(x2_ref, g_ref, gain_ref, wo_ref, *refs):
    o_refs, (x3_ref, n_ref, nt_ref, gt_ref) = refs[:-4], refs[-4:]
    x3 = x2_ref[...] + spans_dot(o_refs, wo_ref, NT)
    x3_ref[...] = x3
    unit, _ = unit_of(x3)
    n = (unit * gain_ref[2:3, :]).astype(BF)
    n_ref[...] = n
    nt_ref[...] = n.T
    gt_ref[...] = g_ref[...].T


def ffn_kernel(n_ref, nt_ref, g_ref, gt_ref, win_ref, wout_ref, y_ref, dn_ref, dw_ref):
    w_in, w_out = win_ref[...], wout_ref[...]
    tokens = n_ref.shape[0]

    @pl.when(pl.program_id(0) == 0)
    def _():
        y_ref[...] = jnp.zeros_like(y_ref)
        dn_ref[...] = jnp.zeros_like(dn_ref)

    acts, grads = [], []
    for r in range(tokens // FFN_ROWS):
        rows = pl.ds(FFN_ROWS * r, FFN_ROWS)
        a = dot(n_ref[rows, :], w_in)
        back = dot(g_ref[rows, :], w_out)
        phi = 0.5 * (1.0 + lax.erf(a * ROOT_HALF))
        act = (a * phi).astype(BF)
        slope = phi + a * jnp.exp(-0.5 * a * a) * INV_ROOT_TWO_PI
        da = (back * slope).astype(BF)
        y_ref[rows, :] += dot(act, w_out, NT)
        dn_ref[rows, :] += dot(da, w_in, NT)
        acts.append(act)
        grads.append(da)
    tile = w_in.shape[1]
    dw_ref[:, :tile] = dot(nt_ref[...], jnp.concatenate(grads, axis=0)).astype(BF)
    dw_ref[:, tile:] = dot(gt_ref[...], jnp.concatenate(acts, axis=0)).astype(BF)


def top_kernel(y_ref, dn_ref, x3_ref, g_ref, gain_ref, wo_ref, out_ref, dx_ref, lowt_ref, doc_ref, gg_ref):
    x3 = x3_ref[...]
    out_ref[...] = (x3 + y_ref[...]).astype(BF)
    grad, grad_gain = norm_back(dn_ref[...], x3, gain_ref[2:3, :])
    dx = g_ref[...].astype(F32) + grad
    dx_ref[...] = dx
    low = dx.astype(BF)
    lowt_ref[...] = low.T
    doc_ref[...] = dot(low, wo_ref[...]).astype(BF)

    @pl.when(pl.program_id(0) == 0)
    def _():
        gg_ref[...] = jnp.zeros_like(gg_ref)

    gg_ref[0:1, :] += grad_gain


def second_kernel(x2_ref, dx3_ref, gain_ref, wq_ref, wo_ref, *refs):
    dq_refs, (dx_ref, lowt_ref, do_ref, gg_ref) = refs[:-4], refs[-4:]
    grad, grad_gain = norm_back(spans_dot(dq_refs, wq_ref, NT), x2_ref[...], gain_ref[1:2, :])
    dx = dx3_ref[...] + grad
    dx_ref[...] = dx
    low = dx.astype(BF)
    lowt_ref[...] = low.T
    do_ref[...] = dot(low, wo_ref[...]).astype(BF)

    @pl.when(pl.program_id(0) == 0)
    def _():
        gg_ref[...] = jnp.zeros_like(gg_ref)

    gg_ref[0:1, :] += grad_gain


def last_kernel(x_ref, dx2_ref, gain_ref, wq_ref, wk_ref, wv_ref, *refs):
    d_refs, (dx_ref, gg_ref) = refs[:-2], refs[-2:]
    n = len(d_refs) // 3
    dq, dk, dv = (d_refs[n * i: n * (i + 1)] for i in range(3))
    dn = spans_dot(dq, wq_ref, NT) + spans_dot(dk, wk_ref, NT) + spans_dot(dv, wv_ref, NT)
    grad, grad_gain = norm_back(dn, x_ref[...].astype(F32), gain_ref[0:1, :])
    dx_ref[...] = dx2_ref[...] + grad

    @pl.when(pl.program_id(0) == 0)
    def _():
        gg_ref[...] = jnp.zeros_like(gg_ref)

    gg_ref[0:1, :] += grad_gain


def encoder_kernel(ck_ref, cv_ref, *refs):
    n = len(refs) // 2
    refs[-1][...] = spans_dot(refs[:n], ck_ref, NT) + spans_dot(refs[n: 2 * n], cv_ref, NT)


def grads_kernel(first_rows, lefts, groups, me_ref, *refs):
    count = sum(groups)
    n_left = max(lefts) + 1
    left_refs, right_refs = refs[:n_left], refs[n_left: n_left + count]
    outs = refs[n_left + count: n_left + count + 2 * len(groups)]
    left_buf, right_buf, sems = refs[n_left + count + 2 * len(groups):]
    widths = [ref.shape[1] for ref in right_refs]

    def copies(p):
        found = [pltpu.make_async_copy(right_refs[p], right_buf.at[p % 2, :, pl.ds(0, widths[p])], sems.at[p % 2])]
        if p == 0 or lefts[p] != lefts[p - 1]:
            found.append(pltpu.make_async_copy(left_refs[lefts[p]], left_buf.at[lefts[p] % 2], sems.at[2 + lefts[p] % 2]))
        return found

    for copy in copies(0):
        copy.start()
    for p in range(count):
        if p + 1 < count:
            for copy in copies(p + 1):
                copy.start()
        for copy in copies(p):
            copy.wait()
        group = next(g for g in range(len(groups)) if p < sum(groups[: g + 1]))
        base = sum(widths[sum(groups[:group]): p])
        width = widths[p]
        tile = 384 if width % 256 else 256
        keep_ref, send_ref = outs[2 * group], outs[2 * group + 1]
        for col in range(0, width, tile):
            result = dot(left_buf[lefts[p] % 2], right_buf[p % 2, :, col: col + tile])
            out = slice(base + col, base + col + tile)
            store_halves(me_ref[0], first_rows, result, keep_ref, send_ref, lambda part: (0, part, slice(None), out))


def weight_grads(name, lefts_arrays, lefts, rights, groups, half, first_rows):
    width = lefts_arrays[0].shape[0]
    tokens = rights[0].shape[0]
    columns = max(v.shape[1] for v in rights)
    count = len(rights)
    ends = [sum(groups[:g]) for g in range(len(groups) + 1)]
    sizes = [sum(v.shape[1] for v in rights[ends[g]: ends[g + 1]]) for g in range(len(groups))]
    shapes = [(1, width // (2 * first_rows), first_rows, n) for n in sizes for _ in range(2)]
    flops = 2 * width * tokens * columns * count
    return pl.pallas_call(
        functools.partial(grads_kernel, first_rows, lefts, groups),
        in_specs=[pl.BlockSpec(memory_space=pltpu.SMEM)] + [pl.BlockSpec(memory_space=pl.ANY)] * (len(lefts_arrays) + count),
        out_specs=[pl.BlockSpec(memory_space=pltpu.VMEM)] * len(shapes),
        out_shape=[jax.ShapeDtypeStruct(shape, BF) for shape in shapes],
        scratch_shapes=[pltpu.VMEM((2, width, tokens), BF), pltpu.VMEM((2, tokens, columns), BF), pltpu.SemaphoreType.DMA((4,))],
        compiler_params=pltpu.CompilerParams(vmem_limit_bytes=VMEM_LIMIT),
        cost_estimate=pl.CostEstimate(flops=1, bytes_accessed=1, transcendentals=0),
        name=name,
    )(half, *lefts_arrays, *rights)


SPANS = ((0, 3), (3, 3))
CROSS_SPANS = ((0, 6),)


def body(sizes, inputs, encoder_out, segments, enc_segments, buckets, gains, rel_bias, self_q, self_kv, self_out, cross_q, cross_kv, cross_out, ffn_in, ffn_out, out_grad):
    wide, narrow = sizes
    micro, per, length, width = inputs.shape
    rows = micro * per
    tokens = rows * length
    hidden = ffn_in.shape[1]
    flat = lambda v: v.reshape(tokens, width)
    x, enc, grad_out = flat(inputs), flat(encoder_out), flat(out_grad)
    seg, enc_seg = segments.reshape(rows, length), enc_segments.reshape(rows, length)
    me = lax.axis_index(WIDE)

    outer_t = ffn_out.T
    gain_cols = jnp.pad(gains.T, ((0, 0), (0, 125)))
    shard_self = jnp.concatenate([self_q, self_kv[0], self_kv[1], gain_cols], axis=1)
    shard_cross = jnp.concatenate([cross_q, cross_kv[0], cross_kv[1], cross_out.T, self_out.T], axis=1)
    g_self = Gather(sizes, shard_self, (9 * 128, 10 * 128))
    g_cross = Gather(sizes, shard_cross, (15 * 128, 15 * 128))
    shard_ffn = jnp.concatenate([ffn_in, outer_t], axis=1)
    block_rows = self_q.shape[0] * narrow
    first = 1 << len(low_bits(wide, block_rows))
    first_rows = block_rows * first
    half = ((me // first) % 2).astype(jnp.int32).reshape(1)
    parts = width // (2 * first_rows)

    steps = (tokens // ROWS,)
    wide_f32 = lambda: ((tokens, width), F32, (ROWS, width), row_map)
    wide_low = lambda n=1: ((tokens, n * width), BF, (ROWS, n * width), row_map)
    turned = lambda: ((width, tokens), BF, (width, ROWS), col_map)
    gain_out = lambda: ((8, width), F32, (8, width), whole)
    rows_in = lambda v: (v, (ROWS, v.shape[1]), row_map)
    entire = lambda v: (v, v.shape, whole)
    piece = lambda slab, c: (slab, (width, width), at_col(c))
    unit = 2 * tokens * width * width

    r = Rounds()
    movers = [g_self, g_cross]
    r.moving = list(movers)
    r.live = {"x": x, "enc": enc, "g": grad_out}

    def prepare():
        return {"self_seg": segment_columns(seg, seg), "cross_seg": segment_columns(seg, enc_seg), "table": score_table(rel_bias, buckets)}

    def take_self():
        slab = g_self.whole()
        return {"slab_self": slab, "gain": slab[:, 3 * width: 3 * width + 3].T.astype(F32)}

    def proj():
        n1t, qkv = call(proj_self_kernel, "proj_self", steps, [rows_in(r["x"]), entire(r["gain"]), (r["slab_self"], (width, 3 * width), whole)], [turned(), wide_low(3)], 3 * unit)
        return {"n1t": n1t, "qkv": qkv}

    def fwd_self(i):
        o, p, s = attn_fwd(SPANS[i], r["qkv"], 0, r["qkv"], 6, r["qkv"], 12, *r["self_seg"], r["table"])
        return {f"o{i}": o, f"p{i}": p, f"s{i}": s}

    def both(name):
        return [r[f"{name}{i}"] for i in range(2) if f"{name}{i}" in r.live]

    def mid():
        out = call(mid_kernel, "mid", steps,
                   [rows_in(r["x"]), rows_in(r["enc"]), entire(r["gain"]), piece(r["slab_cross"], 4), (r["slab_cross"], (width, 3 * width), whole)] + [rows_in(o) for o in both("o")],
                   [wide_f32(), turned(), wide_low(), wide_low(2), turned()], 4 * unit)
        return dict(zip(("x2", "n2t", "qc", "kvc", "et"), out))

    def fwd_cross(i):
        o, p, s = attn_fwd(CROSS_SPANS[i], r["qc"], 0, r["kvc"], 0, r["kvc"], 6, *r["cross_seg"])
        return {f"oc{i}": o, f"pc{i}": p, f"sc{i}": s}

    def third():
        out = call(third_kernel, "third", steps,
                   [rows_in(r["x2"]), rows_in(r["g"]), entire(r["gain"]), piece(r["slab_cross"], 3)] + [rows_in(o) for o in both("oc")],
                   [wide_f32(), wide_low(), turned(), turned()], unit)
        return dict(zip(("x3", "n3", "n3t", "gt"), out))

    tile = 512
    tiles = hidden // tile
    acc_out = ((tokens, width), F32, (tokens, width), whole)

    def ffn():
        slab = r["slab_ffn"]
        y, dn, dw = call(
            ffn_kernel, "ffn", (tiles,),
            [entire(r["n3"]), entire(r["n3t"]), entire(r["g"]), entire(r["gt"]),
             (slab, (width, tile), lambda j: (0, j)), (slab, (width, tile), lambda j: (0, tiles + j))],
            [acc_out, acc_out, ((width, 2 * hidden), BF, (width, 2 * tile), lambda j: (0, j))], 12 * tokens * width * hidden)
        return {"y": y, "dn": dn, "dw": dw}

    def top():
        out = call(top_kernel, "top", steps,
                   [rows_in(r["y"]), rows_in(r["dn"]), rows_in(r["x3"]), rows_in(r["g"]), entire(r["gain"]), piece(r["slab_cross"], 3)],
                   [wide_low(), wide_f32(), turned(), wide_low(), gain_out()], unit)
        return dict(zip(("layer", "dx3", "three_t", "doc", "gain3"), out))

    def bwd_cross(i):
        out = attn_bwd(CROSS_SPANS[i], r["qc"], 0, r["kvc"], 0, r["kvc"], 6, r["doc"], r[f"oc{i}"], r[f"pc{i}"], r[f"sc{i}"], False)
        return dict(zip((f"dqc{i}", f"dkc{i}", f"dvc{i}"), out))

    def second():
        out = call(second_kernel, "second", steps,
                   [rows_in(r["x2"]), rows_in(r["dx3"]), entire(r["gain"]), piece(r["slab_cross"], 0), piece(r["slab_cross"], 4)] + [rows_in(d) for d in both("dqc")],
                   [wide_f32(), turned(), wide_low(), gain_out()], 2 * unit)
        return dict(zip(("dx2", "two_t", "do", "gain2"), out))

    def grads_cross():
        rights = both("dqc") + both("dkc") + both("dvc")
        n = len(CROSS_SPANS)
        return {"cut_cross": weight_grads("grads_cross", [r["n2t"], r["et"]], (0,) * n + (1,) * (2 * n), rights, (3 * n,), half, first_rows)}

    def grads_out():
        lefts = (0,) * len(CROSS_SPANS) + (1,) * len(SPANS)
        return {"cut_out": weight_grads("grads_out", [r["three_t"], r["two_t"]], lefts, both("oc") + both("o"), (len(lefts),), half, first_rows)}

    def bwd_self(i):
        out = attn_bwd(SPANS[i], r["qkv"], 0, r["qkv"], 6, r["qkv"], 12, r["do"], r[f"o{i}"], r[f"p{i}"], r[f"s{i}"], True)
        return dict(zip((f"dq{i}", f"dk{i}", f"dv{i}", f"diag{i}"), out))

    def grads_self(i):
        return {f"cut_self{i}": weight_grads("grads_self", [r["n1t"]], (0, 0, 0), [r[f"dq{i}"], r[f"dk{i}"], r[f"dv{i}"]], (3,), half, first_rows)}

    def last():
        out = call(last_kernel, "last", steps,
                   [rows_in(r["x"]), rows_in(r["dx2"]), entire(r["gain"])] + [piece(r["slab_self"], c) for c in range(3)]
                   + [rows_in(d) for name in ("dq", "dk", "dv") for d in both(name)],
                   [wide_f32(), gain_out()], 3 * unit)
        return dict(zip(("dx1", "gain1"), out))

    def encoder():
        out = call(encoder_kernel, "encoder_grad", steps,
                   [piece(r["slab_cross"], c) for c in (1, 2)] + [rows_in(d) for name in ("dkc", "dvc") for d in both(name)],
                   [wide_f32()], 2 * unit)
        return {"de": out[0]}

    def cut(pair, turn, direct=False):
        return Scatter(sizes, pair[0], pair[1], first, turn, direct)

    r.step(prepare, [g_self])
    r.run(None, [g_self, g_cross], [g_self])
    while len(g_self.plan) > 1:
        r.step(None, [g_self])
    r.run(None, [g_self], [g_self, g_cross])
    g_self.groups, shard_ffn = lax.optimization_barrier((g_self.groups, shard_ffn))
    slab_ffn = lax.all_gather(shard_ffn, (WIDE, NARROW), axis=0, tiled=True)
    r.run(take_self, [g_cross], [])
    r.run(proj, [], [g_cross])
    r.run(lambda: fwd_self(0), [g_cross], [])
    r.run(lambda: fwd_self(1), [], [g_cross])
    while g_cross.plan:
        r.step(None, [g_cross])
    r.step(lambda: {"slab_cross": g_cross.whole()}, [])
    r.step(mid, [])
    r.step(lambda: fwd_cross(0), [])
    r.step(third, [])
    r.moving = []
    r.live["slab_ffn"] = slab_ffn
    r.step(None, [])
    r.step(ffn, [])
    ffn_sum = lax.psum_scatter(r.live.pop("dw"), (WIDE, NARROW), scatter_dimension=0, tiled=True).astype(F32)
    ffn_sum = ffn_sum.reshape(-1, tiles, 2, tile)
    r.step(top, [])
    r.step(lambda: bwd_cross(0), [])
    r.step(grads_cross, [])
    sc = cut(r.live.pop("cut_cross"), 0)
    r.step(second, [sc])
    r.run(grads_out, [sc], [])
    so = cut(r.live.pop("cut_out"), 1)
    r.run(lambda: bwd_self(0), [so], [so])
    r.run(lambda: grads_self(0), [so], [sc])
    s0 = cut(r.live.pop("cut_self0"), 1, True)
    r.run(lambda: bwd_self(1), [sc, s0], [s0, sc, so])
    r.run(lambda: grads_self(1), [sc, so], [sc])
    s1 = cut(r.live.pop("cut_self1"), 0, True)
    r.run(last, [s0, s1], [s0, s1, so])

    def small():
        diag = jnp.concatenate(both("diag"), axis=0)
        bias_rows = bucket_sums(diag, buckets, rel_bias.shape[0])
        return {"small": jnp.concatenate([r["gain1"][0], r["gain2"][0], r["gain3"][0], bias_rows.reshape(-1)]).reshape(-1, 128)}

    r.live.update(small())
    total = Total(sizes, r.live.pop("small"))
    r.live["ffn_sum"] = ffn_sum
    r.step(encoder, [s1, total])
    ffn_sum = r.live.pop("ffn_sum")
    ends = [so, s0, s1]
    while any(s.plan != ["narrow"] for s in ends):
        r.step(None, [s for s in ends if s.plan != ["narrow"]])
    for other in (s0, s1):
        so.join(other)
        r.moving.remove(other)
    r.run(None, [so, total], [total])
    while len(total.plan) > 1:
        r.run(None, [total], [total])
    r.run(None, [total], [so, total])
    while any(s.plan for s in (sc, so, total)):
        r.step(None, [sc, so, total])

    summed = total.value.reshape(-1)
    shard = me * narrow + lax.axis_index(NARROW)
    own = width // (wide * narrow)
    gain_sum = lax.dynamic_slice_in_dim(summed[: 3 * width].reshape(3, width), shard * own, own, 1)
    bias_sum = summed[3 * width:].reshape(rel_bias.shape)

    own_rows = lambda value, at, n: value.keep[0, :, at: at + n]

    def self_part(index):
        found, at = [], 2 * width
        for _, pairs in SPANS:
            n = 128 * pairs
            found.append(own_rows(so, at + n * index, n))
            at += 3 * n
        return jnp.concatenate(found, axis=1)

    cross_part = lambda index: own_rows(sc, width * index, width)
    shaped = lambda v: v.reshape(micro, per, length, width)
    return (
        shaped(r["layer"]),
        shaped(r["dx1"]),
        shaped(r["de"]),
        gain_sum,
        bias_sum,
        self_part(0),
        jnp.stack([self_part(1), self_part(2)]),
        own_rows(so, width, width).T,
        cross_part(0),
        jnp.stack([cross_part(1), cross_part(2)]),
        own_rows(so, 0, width).T,
        ffn_sum[:, :, 0].reshape(-1, hidden),
        ffn_sum[:, :, 1].reshape(-1, hidden).T,
    )


def solution(mesh):
    axes = (WIDE, NARROW)
    batch4, batch3 = P(None, axes, None, None), P(None, axes, None)
    first, second, middle = P(axes, None), P(None, axes), P(None, axes, None)
    sizes = (mesh.shape[WIDE], mesh.shape[NARROW])
    weights = (first, middle, second, first, middle, second, first, second)
    return jax.shard_map(
        functools.partial(body, sizes),
        mesh=mesh,
        in_specs=(batch4, batch4, batch3, batch3, P(), second, P()) + weights + (batch4,),
        out_specs=(batch4, batch4, batch4, second, P()) + weights,
        check_vma=False,
    )
```
